32 devices in a mesh: groups: 1, expert: 32 (over z, y, x, core), dp: 1, tensor: 1.
Axes of the slice: x: 2, y: 2, z: 4, core: 2. Of those that a mesh axis runs over, the one named last changes fastest.
Arguments:
- tokens: bfloat16 [4096, 2048], P(('groups', 'expert', 'dp'), 'tensor'), may hold values from -6 to 6
- out_grad: bfloat16 [4096, 2048], P(('groups', 'expert', 'dp'), 'tensor'), may hold values from -6 to 6
- routes: int32 [4096, 8], P(('groups', 'expert', 'dp')), may hold values from 0 to 63, all different within a row; in each aligned block of 128 rows (0 to 127, 128 to 255, ...) at most 24 rows name the same one
- combine_fixed: int32 [4096, 8], P(('groups', 'expert', 'dp')), may hold values from 16 to 255
- down_proj: bfloat16 [512, 2048], P(('expert', 'dp'), 'tensor'), may hold values from -0.125 to 0.125
- up_proj: bfloat16 [512, 2048], P(('expert', 'dp'), 'tensor'), may hold values from -0.25 to 0.25
- expert_gate: bfloat16 [64, 512, 1024], P('expert', None, 'tensor'), may hold values from -0.25 to 0.25
- expert_up: bfloat16 [64, 512, 1024], P('expert', None, 'tensor'), may hold values from -0.25 to 0.25
- expert_down: bfloat16 [64, 1024, 512], P('expert', 'tensor'), may hold values from -0.1875 to 0.1875
Outputs:
- layer_out: bfloat16 [4096, 2048], P(('groups', 'expert', 'dp'), 'tensor')
- token_grad: bfloat16 [4096, 2048], P(('groups', 'expert', 'dp'), 'tensor')
- down_grad: float32 [512, 2048], P(('groups', 'expert', 'dp'), 'tensor')
- up_grad: float32 [512, 2048], P(('groups', 'expert', 'dp'), 'tensor')
The draws below stay inside these ranges and needn't reach their ends.
Inputs may be any that keep to these rules, and one draw needn't show every extreme that they name: `routes`: each row names 8 different experts; among the rows of one data shard (128 aligned rows) no expert is named by more than 24 rows, and in every draw some expert is named by exactly 24 rows of some shard.
All inputs are finite; a program needn't handle non-finite values.
Results may differ from the reference program's by a relative error of at most 0.011.
Values may be sent and summed in bfloat16 or wider, within the bound.
No kernel may reach another device: no remote copies, remote signals or barrier semaphores. Data moves between devices by JAX's collectives and lax.ppermute only.
A program may use at most 64 MiB of HBM per device.

```python
import math
import jax
import jax.numpy as jnp
import numpy as np
from jax import lax

D = 2048
L = 512
EFF = 1024
TOPK = 8
TOK_DEV = 128
EXPERTS = 64
CAP = 24
TOKENS = 4096
N_TENSOR = 1


def touch_ends(drawn, key, smallest, top_value):
    longest = drawn.shape.index(max(drawn.shape))
    spots = []
    for shift in (0, 1):
        where = [jax.random.randint(jax.random.fold_in(key, axis), (), 0, length) for axis, length in enumerate(drawn.shape)]
        where[longest] = (where[longest] + shift) % drawn.shape[longest]
        spots.append(tuple(where))
    return drawn.at[spots[0]].set(smallest).at[spots[1]].set(top_value)


def block_levels(rng, shape, cuts, low, high):
    factor_of = 1.0
    for axis_at, parts in cuts:
        draws = jax.random.uniform(jax.random.fold_in(jax.random.fold_in(rng, 6), axis_at), (parts,), jnp.float32, low / len(cuts), high / len(cuts))
        factor_of = factor_of * jnp.repeat(jnp.exp(draws), shape[axis_at] // parts).reshape((-1,) + (1,) * (len(shape) - 1 - axis_at))
    return factor_of


def shared_out(stream_key, own, number, rows, amount, top, bound, slope):
    order = jax.random.permutation(stream_key, amount)
    crowded, ordinary = portions_of(amount, rows * top, bound, slope, True), portions_of(amount, rows * top, bound, slope, False)
    places = jnp.arange(amount)

    def named(lengths, rotation):
        used = int((lengths > 0).sum())
        fixed = max(1, used // 4)
        shifted = fixed + (places - fixed + rotation * (used - fixed)) % max(1, amount - fixed)
        return jnp.zeros((amount,), jnp.int32).at[order[jnp.where(places < fixed, places, shifted)]].set(jnp.asarray(lengths, jnp.int32))

    lengths = jnp.where(number % 4 == 0, named(crowded, number // 4), named(ordinary, number - number // 4 - 1))
    mixed = jax.random.permutation(jax.random.fold_in(own, 3), amount)
    giver, receiver = mixed[0:amount // 2 * 2:2], mixed[1:amount // 2 * 2:2]
    room = jnp.minimum(lengths[giver] - 1, bound - lengths[receiver]) // 2
    room = jnp.where((giver == order[0]) | (receiver == order[0]) | (lengths[receiver] == 0), 0, jnp.maximum(room, 0))
    shifted = jax.random.randint(jax.random.fold_in(own, 4), (amount // 2,), 0, 1 << 20) % (room + 1)
    lengths = lengths.at[giver].add(-shifted).at[receiver].add(shifted)
    labels = jnp.searchsorted(jnp.cumsum(lengths), jnp.arange(rows * top), side="right").astype(jnp.int32)
    table = labels.reshape(top, rows).T
    table = table[jax.random.permutation(jax.random.fold_in(own, 1), rows)]
    rotation = jax.random.randint(jax.random.fold_in(own, 2), (rows, 1), 0, top)
    return jnp.take_along_axis(table, (jnp.arange(top)[None, :] + rotation) % top, axis=1)


def portions_of(count, total, reach, skew, full):
    portions = [(1 << 20) // math.isqrt(standing ** skew) + 1 for standing in range(1, count + 1)]
    largest = reach if full else min(reach, max(-(-total // count), total * portions[0] // sum(portions)))
    least = 1 if total - largest >= count - 1 else 0
    given, rest = [largest] + [least] * (count - 1), total - largest - least * (count - 1)
    while rest > 0:
        free = [i for i in range(1, count) if given[i] < largest] or [i for i in range(1, count) if given[i] < reach]
        whole, left = sum([portions[i] for i in free]), rest
        for i in free:
            more = min(reach - given[i], max(1, left * portions[i] // whole), rest)
            given[i] = given[i] + more
            rest = rest - more
    return np.array(given)


def gaussian(own_key, dims, deviation, most, pieces=(), held_as=jnp.bfloat16):
    factor_of = block_levels(own_key, dims, pieces, -0.22, 0.18) if pieces else 1.0
    array = jax.random.normal(own_key, dims, jnp.float32) * deviation * factor_of
    return jnp.minimum(jnp.maximum(array, -most), most).astype(held_as)


def setup_inputs(seed: int = 0, part: int = 0) -> dict:
    key_of = jax.random.split(jax.random.key(seed), 10)
    part_splits = jax.random.split(jax.random.fold_in(key_of[9], part), 10)
    tokens = gaussian(part_splits[0], (TOKENS, D), 1.0, 6.0, ((0, 32),))
    out_grad = gaussian(part_splits[1], (TOKENS, D), 1.0, 6.0, ((0, 32),))
    routes_keys = jax.random.split(jax.random.fold_in(part_splits[2], 1), TOKENS // TOK_DEV)
    routes_turns = jax.random.permutation(jax.random.fold_in(part_splits[2], 3), TOKENS // TOK_DEV)
    routes = jax.vmap(lambda own, number: shared_out(jax.random.fold_in(part_splits[2], 2), own, number, TOK_DEV, EXPERTS, TOPK, CAP, 2))(routes_keys, routes_turns).reshape((TOKENS, TOPK))
    combine_fixed = touch_ends(jax.random.randint(part_splits[3], (TOKENS, TOPK), 16, 256), jax.random.fold_in(part_splits[3], 1), 16, 255).astype(jnp.int32)
    down_proj = gaussian(key_of[4], (L, D), D ** -0.5, 0.125, ((0, 32),))
    up_proj = gaussian(key_of[5], (L, D), L ** -0.5, 0.25, ((0, 32),))
    expert_gate = gaussian(key_of[6], (EXPERTS, L, EFF), L ** -0.5, 0.25, ((0, 32),))
    expert_up = gaussian(key_of[7], (EXPERTS, L, EFF), L ** -0.5, 0.25, ((0, 32),))
    expert_down = gaussian(key_of[8], (EXPERTS, EFF, L), EFF ** -0.5, 0.1875, ((0, 32),))
    return {"tokens": tokens, "out_grad": out_grad, "routes": routes, "combine_fixed": combine_fixed, "down_proj": down_proj, "up_proj": up_proj, "expert_gate": expert_gate, "expert_up": expert_up, "expert_down": expert_down}


def rounded(values):
    lowered = values.astype(jnp.bfloat16)
    return lax.optimization_barrier(lowered).astype(jnp.float32)


def expert_slots(routes, weights, expert_id):
    chosen = routes == expert_id
    member = jnp.any(chosen, axis=1)
    row_index = jnp.nonzero(member, size=CAP * (TOKENS // TOK_DEV), fill_value=TOKENS)[0].astype(jnp.int32)
    scales = jnp.sum(jnp.where(chosen, weights, jnp.zeros_like(weights)), axis=1)
    padded = jnp.concatenate([scales, jnp.zeros((1,), scales.dtype)])
    return row_index, padded[row_index]


def reference(tokens, out_grad, routes, combine_fixed, down_proj, up_proj, expert_gate, expert_up, expert_down):
    weights = combine_fixed.astype(jnp.float32) / 256.0
    half_width = EFF // N_TENSOR
    latent = jnp.dot(tokens, down_proj.T, preferred_element_type=jnp.float32).astype(jnp.bfloat16)
    latent_pad = jnp.concatenate([latent, jnp.zeros((1, L), jnp.bfloat16)])
    stacked_all = (jnp.arange(EXPERTS, dtype=jnp.int32), expert_gate, expert_up, expert_down)

    def forward_step(running, stacked):
        expert_id, gate_w, up_w, down_w = stacked
        row_index, row_scale = expert_slots(routes, weights, expert_id)
        rows_in = latent_pad[row_index].astype(jnp.float32)
        for piece_id in range(N_TENSOR):
            lower = piece_id * half_width
            upper = lower + half_width
            gate_act = jnp.dot(rows_in, gate_w[:, lower:upper].astype(jnp.float32))
            up_act = jnp.dot(rows_in, up_w[:, lower:upper].astype(jnp.float32))
            hidden = rounded(gate_act * jax.nn.sigmoid(gate_act) * up_act)
            part_out = rounded(jnp.dot(hidden, down_w[lower:upper, :].astype(jnp.float32)))
            running = running.at[row_index].add(row_scale[:, None] * part_out)
        return running, None

    mixed_sum, _ = lax.scan(forward_step, jnp.zeros((TOKENS + 1, L), jnp.float32), stacked_all)
    mixed_rows = mixed_sum[:TOKENS].astype(jnp.bfloat16)
    layer_out = jnp.dot(mixed_rows, up_proj, preferred_element_type=jnp.float32).astype(jnp.bfloat16)
    mix_grad = jnp.dot(out_grad, up_proj.T, preferred_element_type=jnp.float32).astype(jnp.bfloat16)
    mix_pad = jnp.concatenate([mix_grad, jnp.zeros((1, L), jnp.bfloat16)])

    def backward_step(running, stacked):
        expert_id, gate_w, up_w, down_w = stacked
        row_index, row_scale = expert_slots(routes, weights, expert_id)
        rows_in = latent_pad[row_index].astype(jnp.float32)
        grad_in = rounded(row_scale[:, None] * mix_pad[row_index].astype(jnp.float32))
        for piece_id in range(N_TENSOR):
            lower = piece_id * half_width
            upper = lower + half_width
            gate_part = gate_w[:, lower:upper].astype(jnp.float32)
            up_part = up_w[:, lower:upper].astype(jnp.float32)
            gate_act = jnp.dot(rows_in, gate_part)
            up_act = jnp.dot(rows_in, up_part)
            sigmoid_gate = jax.nn.sigmoid(gate_act)
            hidden_grad = jnp.dot(grad_in, down_w[lower:upper, :].astype(jnp.float32).T)
            gate_grad = rounded(hidden_grad * up_act * sigmoid_gate * (1.0 + gate_act * (1.0 - sigmoid_gate)))
            value_grad = rounded(hidden_grad * gate_act * sigmoid_gate)
            back_rows = rounded(jnp.dot(gate_grad, gate_part.T) + jnp.dot(value_grad, up_part.T))
            running = running.at[row_index].add(back_rows)
        return running, None

    latent_sum, _ = lax.scan(backward_step, jnp.zeros((TOKENS + 1, L), jnp.float32), stacked_all)
    latent_grad = latent_sum[:TOKENS].astype(jnp.bfloat16)
    token_grad = jnp.dot(latent_grad, down_proj, preferred_element_type=jnp.float32).astype(jnp.bfloat16)
    down_grad = jnp.dot(latent_grad.T, tokens, preferred_element_type=jnp.float32)
    up_grad = jnp.dot(mixed_rows.T, out_grad, preferred_element_type=jnp.float32)
    return (layer_out, token_grad, down_grad, up_grad)
```

```python
import math

import jax
import jax.numpy as jnp
from jax import lax
from jax.sharding import PartitionSpec as P


def move_rows(blocks):
    return lax.all_to_all(blocks, "expert", split_axis=0, concat_axis=0, tiled=True)


def tensor_total(partial_sum):
    return lax.psum(partial_sum, "tensor")


def dispatch_rows(blocks):
    return move_rows(blocks)


OWNERS = ("expert", "dp")


def radices(count):
    return (count // 8, 2, 2, 2) if count % 8 == 0 else (count, 1, 1, 1)


def digit_of(count, place):
    sizes = radices(count)
    stride = math.prod(sizes[place + 1 :])
    return lax.rem(lax.axis_index(OWNERS) // stride, sizes[place])


def shifted(block, count, place, step):
    sizes = radices(count)
    stride = math.prod(sizes[place + 1 :])
    pairs = []
    for here in range(count):
        digit = here // stride % sizes[place]
        pairs.append((here, here + ((digit + step) % sizes[place] - digit) * stride))
    return lax.ppermute(block, OWNERS, pairs)


def gather_rows(shard, count, order):
    sizes = radices(count)
    block = shard.reshape((1, 1, 1, 1) + shard.shape)
    for place in order:
        size = sizes[place]
        if size == 1:
            continue
        digit = digit_of(count, place)
        if size == 2:
            other = shifted(block, count, place, 1)
            block = jnp.where(
                digit == 0,
                lax.concatenate([block, other], place),
                lax.concatenate([other, block], place),
            )
            continue
        pieces = [block] + [shifted(block, count, place, step) for step in range(1, size)]
        whole = jnp.zeros(block.shape[:place] + (size,) + block.shape[place + 1 :], block.dtype)
        for step, piece in enumerate(pieces):
            owner = lax.rem(digit + size - step, size)
            whole = lax.dynamic_update_slice_in_dim(whole, piece, owner, place)
        block = whole
    return block.reshape((count * shard.shape[0],) + shard.shape[1:])


def scatter_total(left, right, count, order):
    sizes = radices(count)
    width = left.shape[1]
    columns = left.reshape((left.shape[0],) + sizes + (width // count,))

    def product(part):
        out = jnp.einsum(
            "tl,td->ld", part.reshape(left.shape[0], -1), right, preferred_element_type=jnp.float32
        )
        return out.reshape(part.shape[1:] + right.shape[1:])

    def own(array, place, step, offset):
        size = sizes[place]
        where = lax.rem(digit_of(count, place) + step, size)
        return lax.dynamic_slice_in_dim(array, where, 1, place + offset)

    first, rest = order[0], order[1:]
    received = [
        shifted(product(own(columns, first, step, 1)).astype(jnp.bfloat16), count, first, step)
        for step in range(1, sizes[first])
    ]
    kept = product(own(columns, first, 0, 1))
    for place in rest:
        size = sizes[place]
        arriving = []
        for step in range(1, size):
            part = own(kept, place, step, 0)
            for block in received:
                part = part + own(block, place, step, 0).astype(jnp.float32)
            arriving.append(shifted(part.astype(jnp.bfloat16), count, place, step))
        kept = own(kept, place, 0, 0)
        for block in received:
            kept = kept + own(block, place, 0, 0).astype(jnp.float32)
        received = arriving
    for block in received:
        kept = kept + block.astype(jnp.float32)
    return kept.reshape(width // count, right.shape[1])


def local(
    tokens, out_grad, routes, combine_fixed, down_proj, up_proj, expert_gate, expert_up, expert_down
):
    count = lax.axis_size("expert") * lax.axis_size("dp")
    down_full = gather_rows(down_proj, count, (0, 1, 2, 3))
    up_full = gather_rows(up_proj, count, (0, 2, 1, 3))
    row_count = tokens.shape[0]
    top_count = routes.shape[1]
    latent_width = down_full.shape[0]
    local_experts = expert_gate.shape[0]
    groups = lax.axis_size("expert")
    experts = local_experts * groups
    capacity = 3 * row_count * top_count // (2 * experts)
    chosen = routes[:, :, None] == jnp.arange(experts, dtype=jnp.int32)[None, None, :]
    member = jnp.any(chosen, axis=1)
    ranking = jnp.cumsum(member.astype(jnp.int32), axis=0) - 1
    fixed_scale = combine_fixed[:, :, None].astype(jnp.float32) / 256.0
    scales = jnp.sum(jnp.where(chosen, fixed_scale, 0.0), axis=1)
    placed = (
        ranking.T[:, None, :] == jnp.arange(capacity, dtype=jnp.int32)[None, :, None]
    ) & member.T[:, None, :]
    dispatch = placed.astype(jnp.bfloat16)
    combining = jnp.where(placed, scales.T[:, None, :], 0.0).astype(jnp.bfloat16)
    latent_part = jnp.einsum("td,ld->tl", tokens, down_full, preferred_element_type=jnp.float32)
    latent = tensor_total(latent_part).astype(jnp.bfloat16)
    outgoing = jnp.einsum(
        "ect,tl->ecl", dispatch, latent, preferred_element_type=jnp.float32
    ).astype(jnp.bfloat16)
    arrived = dispatch_rows(outgoing).reshape(groups, local_experts, capacity, latent_width)
    gate_act = jnp.einsum(
        "sjcl,jlf->sjcf", arrived, expert_gate, preferred_element_type=jnp.float32
    )
    up_act = jnp.einsum("sjcl,jlf->sjcf", arrived, expert_up, preferred_element_type=jnp.float32)
    sigmoid_gate = jax.nn.sigmoid(gate_act)
    hidden = (gate_act * sigmoid_gate * up_act).astype(jnp.bfloat16)
    half_out = jnp.einsum(
        "sjcf,jfl->sjcl", hidden, expert_down, preferred_element_type=jnp.float32
    ).astype(jnp.bfloat16)
    returned = move_rows(half_out.reshape(experts, capacity, latent_width))
    mixed_part = jnp.einsum("ect,ecl->tl", combining, returned, preferred_element_type=jnp.float32)
    mixed_rows = tensor_total(mixed_part).astype(jnp.bfloat16)
    layer_out = jnp.dot(mixed_rows, up_full, preferred_element_type=jnp.float32).astype(
        jnp.bfloat16
    )
    mix_part = jnp.einsum("td,ld->tl", out_grad, up_full, preferred_element_type=jnp.float32)
    mix_grad = tensor_total(mix_part).astype(jnp.bfloat16)
    grad_rows = jnp.einsum(
        "ect,tl->ecl", combining, mix_grad, preferred_element_type=jnp.float32
    ).astype(jnp.bfloat16)
    grad_arrived = dispatch_rows(grad_rows).reshape(groups, local_experts, capacity, latent_width)
    hidden_grad = jnp.einsum(
        "sjcl,jfl->sjcf", grad_arrived, expert_down, preferred_element_type=jnp.float32
    )
    gate_grad = (
        hidden_grad * up_act * sigmoid_gate * (1.0 + gate_act * (1.0 - sigmoid_gate))
    ).astype(jnp.bfloat16)
    value_grad = (hidden_grad * gate_act * sigmoid_gate).astype(jnp.bfloat16)
    back_sum = jnp.einsum(
        "sjcf,jlf->sjcl", gate_grad, expert_gate, preferred_element_type=jnp.float32
    )
    back_sum = back_sum + jnp.einsum(
        "sjcf,jlf->sjcl", value_grad, expert_up, preferred_element_type=jnp.float32
    )
    back_rows = move_rows(back_sum.astype(jnp.bfloat16).reshape(experts, capacity, latent_width))
    latent_part_grad = jnp.einsum(
        "ect,ecl->tl", dispatch, back_rows, preferred_element_type=jnp.float32
    )
    latent_grad = tensor_total(latent_part_grad).astype(jnp.bfloat16)
    token_grad = jnp.dot(latent_grad, down_full, preferred_element_type=jnp.float32).astype(
        jnp.bfloat16
    )
    down_grad = scatter_total(latent_grad, tokens, count, (3, 2, 1, 0))
    up_grad = scatter_total(mixed_rows, out_grad, count, (3, 1, 2, 0))
    return (layer_out, token_grad, down_grad, up_grad)


def solution(mesh):
    in_specs = (
        P(("groups", "expert", "dp"), "tensor"),
        P(("groups", "expert", "dp"), "tensor"),
        P(("groups", "expert", "dp"), None),
        P(("groups", "expert", "dp"), None),
        P(("expert", "dp"), "tensor"),
        P(("expert", "dp"), "tensor"),
        P("expert", None, "tensor"),
        P("expert", None, "tensor"),
        P("expert", "tensor", None),
    )
    out_specs = (
        P(("groups", "expert", "dp"), "tensor"),
        P(("groups", "expert", "dp"), "tensor"),
        P(("groups", "expert", "dp"), "tensor"),
        P(("groups", "expert", "dp"), "tensor"),
    )
    return jax.shard_map(local, mesh=mesh, in_specs=in_specs, out_specs=out_specs, check_vma=False)
```

```python
import math

import jax
import jax.numpy as jnp
from jax import lax
from jax.experimental import pallas as pl
from jax.experimental.pallas import tpu as pltpu
from jax.sharding import PartitionSpec as P

OWNERS = ("expert", "dp")
EXPERT = ("expert",)
Z, Y, X, CORE = 0, 1, 2, 3
FAR_AWAY = -128.0


def tensor_total(partial_sum):
    return lax.psum(partial_sum, "tensor")


def radices(count):
    return (count // 8, 2, 2, 2)


def digit_of(axes, place):
    sizes = radices(math.prod(lax.axis_size(axis) for axis in axes))
    stride = math.prod(sizes[place + 1 :])
    return lax.rem(lax.axis_index(axes) // stride, sizes[place])


def shifted(block, axes, place, step=1):
    count = math.prod(lax.axis_size(axis) for axis in axes)
    sizes = radices(count)
    stride = math.prod(sizes[place + 1 :])
    pairs = []
    for here in range(count):
        digit = here // stride % sizes[place]
        pairs.append((here, here + ((digit + step) % sizes[place] - digit) * stride))
    return lax.ppermute(block, axes, pairs)


def gather_rows(shard, count, order):
    sizes = radices(count)
    block = shard.reshape((1, 1, 1, 1) + shard.shape)
    for place in order:
        size = sizes[place]
        digit = digit_of(OWNERS, place)
        if size == 2:
            other = shifted(block, OWNERS, place)
            block = jnp.where(
                digit == 0,
                lax.concatenate([block, other], place),
                lax.concatenate([other, block], place),
            )
            continue
        pieces = [block] + [shifted(block, OWNERS, place, step) for step in range(1, size)]
        whole = jnp.zeros(block.shape[:place] + (size,) + block.shape[place + 1 :], block.dtype)
        for step, piece in enumerate(pieces):
            owner = lax.rem(digit + size - step, size)
            whole = lax.dynamic_update_slice_in_dim(whole, piece, owner, place)
        block = whole
    return block.reshape((count * shard.shape[0],) + shard.shape[1:])


def scatter_total(left, right, count, order):
    sizes = radices(count)
    width = left.shape[1]
    columns = left.reshape((left.shape[0],) + sizes + (width // count,))

    def product(part):
        out = jnp.einsum(
            "tl,td->ld", part.reshape(left.shape[0], -1), right, preferred_element_type=jnp.float32
        )
        return out.reshape(part.shape[1:] + right.shape[1:])

    def own(array, place, step, offset):
        size = sizes[place]
        where = lax.rem(digit_of(OWNERS, place) + step, size)
        return lax.dynamic_slice_in_dim(array, where, 1, place + offset)

    first, rest = order[0], order[1:]
    received = [
        shifted(product(own(columns, first, step, 1)).astype(jnp.bfloat16), OWNERS, first, step)
        for step in range(1, sizes[first])
    ]
    kept = product(own(columns, first, 0, 1))
    for place in rest:
        size = sizes[place]
        arriving = []
        for step in range(1, size):
            part = own(kept, place, step, 0)
            for block in received:
                part = part + own(block, place, step, 0).astype(jnp.float32)
            arriving.append(shifted(part.astype(jnp.bfloat16), OWNERS, place, step))
        kept = own(kept, place, 0, 0)
        for block in received:
            kept = kept + own(block, place, 0, 0).astype(jnp.float32)
        received = arriving
    for block in received:
        kept = kept + block.astype(jnp.float32)
    return kept.reshape(width // count, right.shape[1])


def relative_owner(core_step, y_step, x_step, z_step):
    depth = radices(lax.axis_size("expert"))[Z]
    z = lax.rem(digit_of(EXPERT, Z) + depth - z_step, depth)
    y = lax.rem(digit_of(EXPERT, Y) + y_step, 2)
    x = lax.rem(digit_of(EXPERT, X) + x_step, 2)
    core = lax.rem(digit_of(EXPERT, CORE) + core_step, 2)
    return ((z * 2 + y) * 2 + x) * 2 + core


def relative_owners():
    depth = radices(lax.axis_size("expert"))[Z]
    return jnp.stack(
        [
            relative_owner(core_step, y_step, x_step, z_step)
            for core_step in (0, 1)
            for y_step, x_step in ((0, 0), (1, 0), (0, 1), (1, 1))
            for z_step in range(depth)
        ]
    )


def gather_tokens(rows):
    depth = radices(lax.axis_size("expert"))[Z]
    half = rows.shape[1] // 2
    own = lax.concatenate([rows] + [shifted(rows, EXPERT, Z, step) for step in range(1, depth)], 0)
    along_y = shifted(own, EXPERT, Y)
    along_x = shifted(own, EXPERT, X)
    across = lax.concatenate(
        [shifted(along_y[:, :half], EXPERT, X), shifted(along_x[:, half:], EXPERT, Y)], 1
    )
    near = lax.concatenate([own, along_y, along_x, across], 0)
    return near, shifted(near, EXPERT, CORE)


def total_tokens(near, far):
    depth = radices(lax.axis_size("expert"))[Z]
    half = near.shape[1] // 2
    terms = near.astype(jnp.float32) + shifted(far, EXPERT, CORE).astype(jnp.float32)
    own, along_y, along_x, across = jnp.split(terms, 4, axis=0)
    across = across.astype(jnp.bfloat16)
    left = shifted(across[:, :half], EXPERT, X).astype(jnp.float32)
    right = shifted(across[:, half:], EXPERT, Y).astype(jnp.float32)
    along_y = lax.concatenate([along_y[:, :half] + left, along_y[:, half:]], 1)
    along_x = lax.concatenate([along_x[:, :half], along_x[:, half:] + right], 1)
    own = own + shifted(along_y.astype(jnp.bfloat16), EXPERT, Y).astype(jnp.float32)
    own = own + shifted(along_x.astype(jnp.bfloat16), EXPERT, X).astype(jnp.float32)
    pieces = jnp.split(own, depth, axis=0)
    total = pieces[0]
    for step in range(1, depth):
        piece = shifted(pieces[step].astype(jnp.bfloat16), EXPERT, Z, depth - step)
        total = total + piece.astype(jnp.float32)
    return total


def matmul(left, right, contract=((1,), (0,))):
    return lax.dot_general(left, right, (contract, ((), ())), preferred_element_type=jnp.float32)


def selected(slot_ref, group, expert, slots, values=None):
    slot = slot_ref[group, expert]
    here = lax.broadcasted_iota(jnp.int32, (slots, slot.shape[1]), 0) == slot
    return jnp.where(here, 1.0 if values is None else values, 0.0).astype(jnp.bfloat16)


def forward_kernel(
    slot_ref,
    scale_ref,
    near_ref,
    far_ref,
    gate_ref,
    up_ref,
    down_ref,
    near_out,
    far_out,
    rows,
    hidden,
    results,
):
    experts, groups, slots, _ = results.shape
    span = near_ref.shape[0] // groups
    width = hidden.shape[1]
    chunk = 256
    for side, (source, target) in enumerate(((near_ref, near_out), (far_ref, far_out))):

        @pl.loop(0, experts)
        def _(expert):
            for group in range(groups):
                pick = selected(slot_ref, side * groups + group, expert, slots)
                picked = matmul(pick, source[group * span : (group + 1) * span, :])
                rows[group * slots : (group + 1) * slots, :] = picked.astype(jnp.bfloat16)
            for start in range(0, width, chunk):
                columns = slice(start, start + chunk)
                gate_act = matmul(rows[...], gate_ref[expert, :, columns])
                up_act = matmul(rows[...], up_ref[expert, :, columns])
                act = gate_act * jax.nn.sigmoid(gate_act) * up_act
                hidden[:, columns] = act.astype(jnp.bfloat16)
            result = matmul(hidden[...], down_ref[expert]).astype(jnp.bfloat16)
            for group in range(groups):
                results[expert, group] = result[group * slots : (group + 1) * slots, :]

        for group in range(groups):
            place = side * groups + group
            weights = jnp.concatenate(
                [
                    selected(slot_ref, place, expert, slots, scale_ref[place, expert])
                    for expert in range(experts)
                ],
                0,
            )
            values = jnp.concatenate([results[expert, group] for expert in range(experts)], 0)
            mixed = matmul(weights, values, ((0,), (0,)))
            target[group * span : (group + 1) * span, :] = mixed.astype(jnp.bfloat16)


def backward_kernel(
    slot_ref,
    scale_ref,
    near_ref,
    far_ref,
    near_grad,
    far_grad,
    gate_ref,
    up_ref,
    down_ref,
    near_out,
    far_out,
    rows,
    grads,
    gate_grads,
    value_grads,
    results,
):
    experts, groups, slots, _ = results.shape
    span = near_ref.shape[0] // groups
    width = gate_grads.shape[1]
    chunk = 256
    for side, (source, source_grad, target) in enumerate(
        ((near_ref, near_grad, near_out), (far_ref, far_grad, far_out))
    ):

        @pl.loop(0, experts)
        def _(expert):
            for group in range(groups):
                place = side * groups + group
                tokens = slice(group * span, (group + 1) * span)
                held = slice(group * slots, (group + 1) * slots)
                pick = selected(slot_ref, place, expert, slots)
                rows[held, :] = matmul(pick, source[tokens, :]).astype(jnp.bfloat16)
                weighed = selected(slot_ref, place, expert, slots, scale_ref[place, expert])
                grads[held, :] = matmul(weighed, source_grad[tokens, :]).astype(jnp.bfloat16)
            for start in range(0, width, chunk):
                columns = slice(start, start + chunk)
                gate_act = matmul(rows[...], gate_ref[expert, :, columns])
                up_act = matmul(rows[...], up_ref[expert, :, columns])
                hidden_grad = matmul(grads[...], down_ref[expert, columns, :], ((1,), (1,)))
                sigmoid = jax.nn.sigmoid(gate_act)
                scaled = hidden_grad * sigmoid
                gate_grad = scaled * up_act * (1.0 + gate_act * (1.0 - sigmoid))
                gate_grads[:, columns] = gate_grad.astype(jnp.bfloat16)
                value_grads[:, columns] = (scaled * gate_act).astype(jnp.bfloat16)
            result = matmul(gate_grads[...], gate_ref[expert], ((1,), (1,)))
            result = result + matmul(value_grads[...], up_ref[expert], ((1,), (1,)))
            result = result.astype(jnp.bfloat16)
            for group in range(groups):
                results[expert, group] = result[group * slots : (group + 1) * slots, :]

        for group in range(groups):
            place = side * groups + group
            picks = jnp.concatenate(
                [selected(slot_ref, place, expert, slots) for expert in range(experts)], 0
            )
            values = jnp.concatenate([results[expert, group] for expert in range(experts)], 0)
            total = matmul(picks, values, ((0,), (0,)))
            target[group * span : (group + 1) * span, :] = total.astype(jnp.bfloat16)


def expert_call(kernel, products, scratch, slots, scales, arrays, weights):
    near = arrays[0]
    experts, latent_width, width = weights[0].shape
    operands = (slots, scales) + tuple(arrays) + tuple(weights)
    whole = pl.BlockSpec(memory_space=pltpu.VMEM)
    row_count = scratch[0].shape[0] * 2
    return pl.pallas_call(
        kernel,
        out_shape=(jax.ShapeDtypeStruct(near.shape, jnp.bfloat16),) * 2,
        in_specs=[whole] * len(operands),
        out_specs=(whole,) * 2,
        scratch_shapes=scratch,
        compiler_params=pltpu.CompilerParams(vmem_limit_bytes=44 << 20),
        cost_estimate=pl.CostEstimate(
            flops=2 * products * experts * row_count * latent_width * width,
            bytes_accessed=sum(array.size * 2 for array in operands) + near.size * 4,
            transcendentals=experts * row_count * width,
        ),
    )(*operands)


def local(
    tokens, out_grad, routes, combine_fixed, down_proj, up_proj, expert_gate, expert_up, expert_down
):
    count = lax.axis_size("expert") * lax.axis_size("dp")
    down_full = gather_rows(down_proj, count, (Z, Y, X, CORE))
    up_full = gather_rows(up_proj, count, (Z, X, Y, CORE))
    row_count = tokens.shape[0]
    top_count = routes.shape[1]
    latent_width = down_full.shape[0]
    local_experts, _, width = expert_gate.shape
    shards = lax.axis_size("expert")
    depth = radices(shards)[Z]
    experts = local_experts * shards
    capacity = 3 * row_count * top_count // (2 * experts)

    chosen = routes[:, :, None] == jnp.arange(experts, dtype=jnp.int32)[None, None, :]
    member = jnp.any(chosen, axis=1)
    ranking = jnp.cumsum(member.astype(jnp.int32), axis=0) - 1
    slot = jnp.where(member, ranking.astype(jnp.float32), FAR_AWAY)
    fixed = jnp.sum(jnp.where(chosen, combine_fixed[:, :, None], 0), axis=1).astype(jnp.float32)
    plan = jnp.stack(
        [
            slot.T.reshape(shards, local_experts, row_count),
            fixed.T.reshape(shards, local_experts, row_count),
        ],
        1,
    )
    plan = plan.reshape(shards, 2 * local_experts * row_count).astype(jnp.bfloat16)
    plan = lax.all_to_all(plan, "expert", split_axis=0, concat_axis=0, tiled=True)
    order = relative_owners()[:, None] == jnp.arange(shards, dtype=jnp.int32)[None, :]
    plan = jnp.dot(order.astype(jnp.bfloat16), plan, preferred_element_type=jnp.float32)
    plan = plan.reshape(shards // depth, depth, 2, local_experts, row_count)
    plan = plan.transpose(2, 0, 3, 1, 4)
    offsets = (jnp.arange(depth, dtype=jnp.float32) * capacity)[:, None]
    slots = (plan[0] + offsets).astype(jnp.int32)
    slots = slots.reshape(shards // depth, local_experts, 1, depth * row_count)
    scales = (plan[1] / 256.0).reshape(slots.shape)

    latent_part = jnp.einsum("td,ld->tl", tokens, down_full, preferred_element_type=jnp.float32)
    latent = tensor_total(latent_part).astype(jnp.bfloat16)
    mix_part = jnp.einsum("td,ld->tl", out_grad, up_full, preferred_element_type=jnp.float32)
    mix_grad = tensor_total(mix_part).astype(jnp.bfloat16)
    latents = gather_tokens(latent)
    mix_grads = gather_tokens(mix_grad)

    half = shards // depth // 2 * depth * capacity
    narrow = pltpu.VMEM((half, latent_width), jnp.bfloat16)
    wide = pltpu.VMEM((half, width), jnp.bfloat16)
    held = pltpu.VMEM(
        (local_experts, shards // depth // 2, depth * capacity, latent_width), jnp.bfloat16
    )
    weights = (expert_gate, expert_up, expert_down)
    mixed_terms = expert_call(
        forward_kernel, 3, (narrow, wide, held), slots, scales, latents, weights
    )
    grad_terms = expert_call(
        backward_kernel,
        5,
        (narrow, narrow, wide, wide, held),
        slots,
        scales,
        latents + mix_grads,
        weights,
    )
    mixed_rows = tensor_total(total_tokens(*mixed_terms)).astype(jnp.bfloat16)
    latent_grad = tensor_total(total_tokens(*grad_terms)).astype(jnp.bfloat16)

    layer_out = jnp.dot(mixed_rows, up_full, preferred_element_type=jnp.float32).astype(
        jnp.bfloat16
    )
    token_grad = jnp.dot(latent_grad, down_full, preferred_element_type=jnp.float32).astype(
        jnp.bfloat16
    )
    up_grad = scatter_total(mixed_rows, out_grad, count, (CORE, Y, X, Z))
    down_grad = scatter_total(latent_grad, tokens, count, (CORE, X, Y, Z))
    return (layer_out, token_grad, down_grad, up_grad)


def solution(mesh):
    in_specs = (
        P(("groups", "expert", "dp"), "tensor"),
        P(("groups", "expert", "dp"), "tensor"),
        P(("groups", "expert", "dp"), None),
        P(("groups", "expert", "dp"), None),
        P(("expert", "dp"), "tensor"),
        P(("expert", "dp"), "tensor"),
        P("expert", None, "tensor"),
        P("expert", None, "tensor"),
        P("expert", "tensor", None),
    )
    out_specs = (
        P(("groups", "expert", "dp"), "tensor"),
        P(("groups", "expert", "dp"), "tensor"),
        P(("groups", "expert", "dp"), "tensor"),
        P(("groups", "expert", "dp"), "tensor"),
    )
    return jax.shard_map(local, mesh=mesh, in_specs=in_specs, out_specs=out_specs, check_vma=False)
```

```python
import math

import jax
import jax.numpy as jnp
from jax import lax
from jax.experimental import pallas as pl
from jax.experimental.pallas import tpu as pltpu
from jax.sharding import PartitionSpec as P

OWNERS = ("expert", "dp")
EXPERT = ("expert",)
Z, Y, X, CORE = 0, 1, 2, 3


def tensor_total(partial_sum):
    return lax.psum(partial_sum, "tensor")


def radices(count):
    return (count // 8, 2, 2, 2)


def digit_of(axes, place):
    sizes = radices(math.prod(lax.axis_size(axis) for axis in axes))
    stride = math.prod(sizes[place + 1 :])
    return lax.rem(lax.axis_index(axes) // stride, sizes[place])


def shifted(block, axes, place, step=1):
    count = math.prod(lax.axis_size(axis) for axis in axes)
    sizes = radices(count)
    stride = math.prod(sizes[place + 1 :])
    pairs = []
    for here in range(count):
        digit = here // stride % sizes[place]
        pairs.append((here, here + ((digit + step) % sizes[place] - digit) * stride))
    return lax.ppermute(block, axes, pairs)


SIDES = ((0, 0), (1, 0), (0, 1), (1, 1))


def device_count(axes):
    return math.prod(lax.axis_size(axis) for axis in axes)


def relative_owners(axes, first, second):
    depth = radices(device_count(axes))[Z]
    owners = []
    for core_step in (0, 1):
        for first_step, second_step in SIDES:
            for z_step in range(depth):
                steps = {Z: depth - z_step, first: first_step, second: second_step, CORE: core_step}
                owner = 0
                for place, size in enumerate(radices(device_count(axes))):
                    digit = lax.rem(digit_of(axes, place) + steps[place], size)
                    owner = owner * size + digit
                owners.append(owner)
    return jnp.stack(owners)


def gather_quarters(rows, axes, first, second):
    depth = radices(device_count(axes))[Z]
    half = rows.shape[1] // 2
    own = lax.concatenate([rows] + [shifted(rows, axes, Z, step) for step in range(1, depth)], 0)
    along_first = shifted(own, axes, first)
    along_second = shifted(own, axes, second)
    across = (
        shifted(along_first[:, :half], axes, second),
        shifted(along_second[:, half:], axes, first),
    )
    return (own, along_first, along_second) + across


def joined(quarters):
    return lax.concatenate(list(quarters[:3]) + [lax.concatenate(list(quarters[3:]), 1)], 0)


def total_tokens(near, far):
    depth = radices(device_count(EXPERT))[Z]

    def both_cores(index):
        other = shifted(far[index], EXPERT, CORE)
        return near[index].astype(jnp.float32) + other.astype(jnp.float32)

    across = both_cores(3).astype(jnp.bfloat16)
    half = across.shape[1] // 2
    left = shifted(across[:, :half], EXPERT, X).astype(jnp.float32)
    right = shifted(across[:, half:], EXPERT, Y).astype(jnp.float32)
    along_y, along_x = both_cores(1), both_cores(2)
    along_y = lax.concatenate([along_y[:, :half] + left, along_y[:, half:]], 1)
    along_x = lax.concatenate([along_x[:, :half], along_x[:, half:] + right], 1)
    own = both_cores(0)
    own = own + shifted(along_y.astype(jnp.bfloat16), EXPERT, Y).astype(jnp.float32)
    own = own + shifted(along_x.astype(jnp.bfloat16), EXPERT, X).astype(jnp.float32)
    pieces = jnp.split(own, depth, axis=0)
    total = pieces[0]
    for step in range(1, depth):
        piece = shifted(pieces[step].astype(jnp.bfloat16), EXPERT, Z, depth - step)
        total = total + piece.astype(jnp.float32)
    return total


def placement(rows, first, second):
    owners = relative_owners(OWNERS, first, second)
    targets = (owners[:, None] * rows + jnp.arange(rows, dtype=jnp.int32)[None, :]).reshape(-1)
    columns = jnp.arange(targets.shape[0], dtype=jnp.int32)
    return (targets[:, None] == columns[None, :]).astype(jnp.bfloat16)


def projected(pair_inputs, near_rows, place):
    part = tensor_total(matmul(pair_inputs, near_rows, ((1,), (1,)))).astype(jnp.bfloat16)
    count = part.shape[0] // 2
    other = shifted(part[count:], OWNERS, CORE)
    relative = lax.concatenate([part[:count], other], 1)
    return matmul(relative, place).astype(jnp.bfloat16)


def projection_grad(relative, quad_inputs, first, second):
    depth = radices(device_count(OWNERS))[Z]
    half = relative.shape[1] // 2
    pair = lax.concatenate([relative[:, :half], shifted(relative[:, half:], OWNERS, CORE)], 0)
    half = half // 2
    quad = lax.concatenate([pair[:, :half], shifted(pair[:, half:], OWNERS, second)], 0)
    half = half // 2
    sent = matmul(quad[:, half:], quad_inputs, ((0,), (0,))).astype(jnp.bfloat16)
    sent = shifted(sent, OWNERS, first)
    kept = matmul(quad[:, :half], quad_inputs, ((0,), (0,))) + sent.astype(jnp.float32)
    pieces = jnp.split(kept, depth, axis=0)
    total = pieces[0]
    for step in range(1, depth):
        piece = shifted(pieces[step].astype(jnp.bfloat16), OWNERS, Z, depth - step)
        total = total + piece.astype(jnp.float32)
    return total


def matmul(left, right, contract=((1,), (0,))):
    return lax.dot_general(left, right, (contract, ((), ())), preferred_element_type=jnp.float32)


def selected(slot_ref, group, expert, slots, values=None):
    slot = slot_ref[group, expert]
    here = lax.broadcasted_iota(jnp.int32, (slots, slot.shape[1]), 0) == slot
    return jnp.where(here, 1.0 if values is None else values, 0.0).astype(jnp.bfloat16)


def weight_copies(sources, targets, arrived, expert):
    return [
        pltpu.make_async_copy(source.at[expert], target.at[expert], arrived.at[place, expert])
        for place, (source, target) in enumerate(zip(sources, targets))
    ]


def pick_rows(pick, quarters, group, target, held):
    if group < 3:
        target[held, :] = matmul(pick, quarters[group][...]).astype(jnp.bfloat16)
        return
    half = target.shape[1] // 2
    for part in (0, 1):
        columns = slice(part * half, (part + 1) * half)
        target[held, columns] = matmul(pick, quarters[3 + part][...]).astype(jnp.bfloat16)


def spread_rows(slot_ref, scale_ref, results, targets):
    experts, groups, slots, _ = results.shape
    for group in range(groups):
        weights = jnp.concatenate(
            [
                selected(
                    slot_ref,
                    group,
                    expert,
                    slots,
                    None if scale_ref is None else scale_ref[group, expert],
                )
                for expert in range(experts)
            ],
            0,
        )
        values = jnp.concatenate([results[expert, group] for expert in range(experts)], 0)
        targets[group][...] = matmul(weights, values, ((0,), (0,))).astype(jnp.bfloat16)


def forward_kernel(*refs):
    slot_ref, scale_ref, *quarters = refs[:7]
    hbm_weights = refs[7:10]
    targets = refs[10:14]
    rows, hidden, results, gate_ref, up_ref, down_ref, arrived = refs[14:]
    experts, groups, slots, _ = results.shape
    width = hidden.shape[1]
    chunk = 256
    for expert in range(experts):
        for copy in weight_copies(hbm_weights, (gate_ref, up_ref, down_ref), arrived, expert):
            copy.start()

    @pl.loop(0, experts)
    def _(expert):
        copies = weight_copies(hbm_weights, (gate_ref, up_ref, down_ref), arrived, expert)
        for group in range(groups):
            held = slice(group * slots, (group + 1) * slots)
            pick_rows(selected(slot_ref, group, expert, slots), quarters, group, rows, held)
        copies[0].wait()
        copies[1].wait()
        for start in range(0, width, chunk):
            columns = slice(start, start + chunk)
            gate_act = matmul(rows[...], gate_ref[expert, :, columns])
            up_act = matmul(rows[...], up_ref[expert, :, columns])
            act = gate_act * jax.nn.sigmoid(gate_act) * up_act
            hidden[:, columns] = act.astype(jnp.bfloat16)
        copies[2].wait()
        result = matmul(hidden[...], down_ref[expert]).astype(jnp.bfloat16)
        for group in range(groups):
            results[expert, group] = result[group * slots : (group + 1) * slots, :]

    spread_rows(slot_ref, scale_ref, results, targets)


def backward_kernel(*refs):
    slot_ref, scale_ref, *quarters = refs[:7]
    quarter_grads = refs[7:12]
    hbm_weights = refs[12:15]
    targets = refs[15:19]
    rows, grads, gate_grads, value_grads, results, gate_ref, up_ref, down_ref, arrived = refs[19:]
    experts, groups, slots, _ = results.shape
    width = gate_grads.shape[1]
    chunk = 256
    for expert in range(experts):
        for copy in weight_copies(hbm_weights, (gate_ref, up_ref, down_ref), arrived, expert):
            copy.start()

    @pl.loop(0, experts)
    def _(expert):
        for group in range(groups):
            held = slice(group * slots, (group + 1) * slots)
            pick_rows(selected(slot_ref, group, expert, slots), quarters, group, rows, held)
            weighed = selected(slot_ref, group, expert, slots, scale_ref[group, expert])
            pick_rows(weighed, quarter_grads, group, grads, held)
        for copy in weight_copies(hbm_weights, (gate_ref, up_ref, down_ref), arrived, expert):
            copy.wait()
        for start in range(0, width, chunk):
            columns = slice(start, start + chunk)
            gate_act = matmul(rows[...], gate_ref[expert, :, columns])
            up_act = matmul(rows[...], up_ref[expert, :, columns])
            hidden_grad = matmul(grads[...], down_ref[expert, columns, :], ((1,), (1,)))
            sigmoid = jax.nn.sigmoid(gate_act)
            scaled = hidden_grad * sigmoid
            gate_grad = scaled * up_act * (1.0 + gate_act * (1.0 - sigmoid))
            gate_grads[:, columns] = gate_grad.astype(jnp.bfloat16)
            value_grads[:, columns] = (scaled * gate_act).astype(jnp.bfloat16)
        result = matmul(gate_grads[...], gate_ref[expert], ((1,), (1,)))
        result = result + matmul(value_grads[...], up_ref[expert], ((1,), (1,)))
        result = result.astype(jnp.bfloat16)
        for group in range(groups):
            results[expert, group] = result[group * slots : (group + 1) * slots, :]

    spread_rows(slot_ref, None, results, targets)


def expert_call(kernel, products, buffers, plan, quarters, weights):
    slots, scales = plan
    experts, latent_width, width = weights[0].shape
    groups, _, _, span = slots.shape
    operands = (slots, scales) + tuple(quarters) + tuple(weights)
    whole = pl.BlockSpec(memory_space=pltpu.VMEM)
    picked = buffers[0].shape[0]
    scratch = list(buffers) + [
        pltpu.VMEM((experts, groups, picked // groups, latent_width), jnp.bfloat16),
        *[pltpu.VMEM(weight.shape, jnp.bfloat16) for weight in weights],
        pltpu.SemaphoreType.DMA((3, experts)),
    ]
    return pl.pallas_call(
        kernel,
        out_shape=(jax.ShapeDtypeStruct((span, latent_width), jnp.bfloat16),) * groups,
        in_specs=[whole] * (len(operands) - 3) + [pl.BlockSpec(memory_space=pl.ANY)] * 3,
        out_specs=(whole,) * groups,
        scratch_shapes=scratch,
        compiler_params=pltpu.CompilerParams(vmem_limit_bytes=36 << 20),
        cost_estimate=pl.CostEstimate(
            flops=2 * products * experts * picked * latent_width * width,
            bytes_accessed=2 * sum(array.size for array in operands),
            transcendentals=experts * picked * width,
        ),
    )(*operands)


def expert_plans(routes, combine_fixed, local_experts):
    shards = lax.axis_size("expert")
    depth = radices(shards)[Z]
    row_count, top_count = routes.shape
    capacity = 3 * row_count * top_count // (2 * local_experts * shards)
    told = lax.concatenate([routes.T, combine_fixed.T], 0).astype(jnp.bfloat16)
    told = lax.all_gather(told.reshape(1, -1), "expert", axis=0, tiled=True)
    owners = relative_owners(EXPERT, Y, X)
    order = owners[:, None] == jnp.arange(shards, dtype=jnp.int32)[None, :]
    told = matmul(order.astype(jnp.bfloat16), told)
    told = told.astype(jnp.int32).reshape(shards, 2, top_count, row_count)
    mine = lax.axis_index("expert") * local_experts + jnp.arange(local_experts, dtype=jnp.int32)
    chosen = told[:, 0][:, None] == mine[None, :, None, None]
    fixed = jnp.sum(jnp.where(chosen, told[:, 1][:, None], 0), axis=2)
    member = jnp.any(chosen, axis=2)
    earlier = jnp.arange(row_count)[:, None] < jnp.arange(row_count)[None, :]
    ranking = jnp.einsum(
        "set,tu->seu",
        member.astype(jnp.bfloat16),
        earlier.astype(jnp.bfloat16),
        preferred_element_type=jnp.float32,
    ).astype(jnp.int32)
    offset = (jnp.arange(shards, dtype=jnp.int32) % depth * capacity)[:, None, None]
    slots = jnp.where(member, ranking + offset, -1)
    scales = fixed.astype(jnp.float32) / 256.0

    def by_quarter(values):
        values = values.reshape(2, 4, depth, local_experts, row_count).transpose(0, 1, 3, 2, 4)
        return values.reshape(2, 4, local_experts, 1, depth * row_count)

    slots, scales = by_quarter(slots), by_quarter(scales)
    return [(slots[core], scales[core]) for core in (0, 1)], depth * capacity


def local(
    tokens, out_grad, routes, combine_fixed, down_proj, up_proj, expert_gate, expert_up, expert_down
):
    local_experts, latent_width, width = expert_gate.shape
    rows = down_proj.shape[0]
    plans, slot_count = expert_plans(routes, combine_fixed, local_experts)

    pair_tokens = lax.concatenate([tokens, shifted(tokens, OWNERS, CORE)], 0)
    down_parts = gather_quarters(down_proj, OWNERS, Y, X)
    pair_grads = lax.concatenate([out_grad, shifted(out_grad, OWNERS, CORE)], 0)
    up_parts = gather_quarters(up_proj, OWNERS, X, Y)
    down_near, up_near = joined(down_parts), joined(up_parts)

    down_place = placement(rows, Y, X)
    up_place = placement(rows, X, Y)
    latent = projected(pair_tokens, down_near, down_place)
    near = gather_quarters(latent, EXPERT, Y, X)
    far = tuple(shifted(part, EXPERT, CORE) for part in near)
    mix_grad = projected(pair_grads, up_near, up_place)
    near_grad = gather_quarters(mix_grad, EXPERT, Y, X)
    far_grad = tuple(shifted(part, EXPERT, CORE) for part in near_grad)

    narrow = pltpu.VMEM((4 * slot_count, latent_width), jnp.bfloat16)
    wide = pltpu.VMEM((4 * slot_count, width), jnp.bfloat16)
    weights = (expert_gate, expert_up, expert_down)
    forward = [
        expert_call(forward_kernel, 3, (narrow, wide), plan, quarters, weights)
        for plan, quarters in zip(plans, (near, far))
    ]
    far_grad, forward = lax.optimization_barrier((far_grad, forward))
    backward = [
        expert_call(backward_kernel, 5, (narrow, narrow, wide, wide), plan, quarters, weights)
        for plan, quarters in zip(plans, (near + near_grad, far + far_grad))
    ]
    down_far = shifted(down_near, OWNERS, CORE)
    up_far = shifted(up_near, OWNERS, CORE)
    quad_tokens = lax.concatenate([pair_tokens, shifted(pair_tokens, OWNERS, X)], 0)
    quad_grads = lax.concatenate([pair_grads, shifted(pair_grads, OWNERS, Y)], 0)

    mixed_rows = tensor_total(total_tokens(*forward)).astype(jnp.bfloat16)
    mixed_relative = matmul(mixed_rows, up_place, ((1,), (1,))).astype(jnp.bfloat16)
    up_grad = projection_grad(mixed_relative, quad_grads, X, Y)
    layer_out = matmul(mixed_relative, lax.concatenate([up_near, up_far], 0)).astype(jnp.bfloat16)

    latent_grad = tensor_total(total_tokens(*backward)).astype(jnp.bfloat16)
    grad_relative = matmul(latent_grad, down_place, ((1,), (1,))).astype(jnp.bfloat16)
    down_grad = projection_grad(grad_relative, quad_tokens, Y, X)
    token_grad = matmul(grad_relative, lax.concatenate([down_near, down_far], 0)).astype(
        jnp.bfloat16
    )
    return (layer_out, token_grad, down_grad, up_grad)


def solution(mesh):
    in_specs = (
        P(("groups", "expert", "dp"), "tensor"),
        P(("groups", "expert", "dp"), "tensor"),
        P(("groups", "expert", "dp"), None),
        P(("groups", "expert", "dp"), None),
        P(("expert", "dp"), "tensor"),
        P(("expert", "dp"), "tensor"),
        P("expert", None, "tensor"),
        P("expert", None, "tensor"),
        P("expert", "tensor", None),
    )
    out_specs = (
        P(("groups", "expert", "dp"), "tensor"),
        P(("groups", "expert", "dp"), "tensor"),
        P(("groups", "expert", "dp"), "tensor"),
        P(("groups", "expert", "dp"), "tensor"),
    )
    return jax.shard_map(local, mesh=mesh, in_specs=in_specs, out_specs=out_specs, check_vma=False)
```

```python
import math

import jax
import jax.numpy as jnp
from jax import lax
from jax.experimental import pallas as pl
from jax.experimental.pallas import tpu as pltpu
from jax.sharding import PartitionSpec as P

OWNERS = ("expert", "dp")
EXPERT = ("expert",)
Z, Y, X, CORE = 0, 1, 2, 3


def tensor_total(partial_sum):
    return lax.psum(partial_sum, "tensor")


def radices(count):
    return (count // 8, 2, 2, 2)


def digit_of(axes, place):
    sizes = radices(math.prod(lax.axis_size(axis) for axis in axes))
    stride = math.prod(sizes[place + 1 :])
    return lax.rem(lax.axis_index(axes) // stride, sizes[place])


def shifted(block, axes, place, step=1):
    count = math.prod(lax.axis_size(axis) for axis in axes)
    sizes = radices(count)
    stride = math.prod(sizes[place + 1 :])
    pairs = []
    for here in range(count):
        digit = here // stride % sizes[place]
        pairs.append((here, here + ((digit + step) % sizes[place] - digit) * stride))
    return lax.ppermute(block, axes, pairs)


SIDES = ((0, 0), (1, 0), (0, 1), (1, 1))


def device_count(axes):
    return math.prod(lax.axis_size(axis) for axis in axes)


def relative_owners(axes, first, second):
    depth = radices(device_count(axes))[Z]
    owners = []
    for core_step in (0, 1):
        for first_step, second_step in SIDES:
            for z_step in range(depth):
                steps = {Z: depth - z_step, first: first_step, second: second_step, CORE: core_step}
                owner = 0
                for place, size in enumerate(radices(device_count(axes))):
                    digit = lax.rem(digit_of(axes, place) + steps[place], size)
                    owner = owner * size + digit
                owners.append(owner)
    return jnp.stack(owners)


def gather_quarters(rows, axes, first, second):
    return gather_chips(gather_depth(rows, axes), axes, first, second)


def gather_depth(rows, axes):
    depth = radices(device_count(axes))[Z]
    return lax.concatenate([rows] + [shifted(rows, axes, Z, step) for step in range(1, depth)], 0)


def gather_chips(own, axes, first, second):
    half = own.shape[1] // 256 * 128 or own.shape[1] // 2
    along_first = shifted(own, axes, first)
    along_second = shifted(own, axes, second)
    across = (
        shifted(along_first[:, :half], axes, second),
        shifted(along_second[:, half:], axes, first),
    )
    return (own, along_first, along_second) + across


def joined(quarters):
    return lax.concatenate(list(quarters[:3]) + [lax.concatenate(list(quarters[3:]), 1)], 0)


def core_totals(near, far):
    return [
        near[index].astype(jnp.float32) + shifted(far[index], EXPERT, CORE).astype(jnp.float32)
        for index in (3, 1, 2, 0)
    ]


def total_tokens(across, along_y, along_x, own):
    depth = radices(device_count(EXPERT))[Z]
    across = across.astype(jnp.bfloat16)
    half = across.shape[1] // 2
    left = shifted(across[:, :half], EXPERT, X).astype(jnp.float32)
    right = shifted(across[:, half:], EXPERT, Y).astype(jnp.float32)
    along_y = lax.concatenate([along_y[:, :half] + left, along_y[:, half:]], 1)
    along_x = lax.concatenate([along_x[:, :half], along_x[:, half:] + right], 1)
    own = own + shifted(along_y.astype(jnp.bfloat16), EXPERT, Y).astype(jnp.float32)
    own = own + shifted(along_x.astype(jnp.bfloat16), EXPERT, X).astype(jnp.float32)
    pieces = jnp.split(own, depth, axis=0)
    total = pieces[0]
    for step in range(1, depth):
        piece = shifted(pieces[step].astype(jnp.bfloat16), EXPERT, Z, depth - step)
        total = total + piece.astype(jnp.float32)
    return total


def placement(rows, first, second):
    owners = relative_owners(OWNERS, first, second)
    targets = (owners[:, None] * rows + jnp.arange(rows, dtype=jnp.int32)[None, :]).reshape(-1)
    columns = jnp.arange(targets.shape[0], dtype=jnp.int32)
    return (targets[:, None] == columns[None, :]).astype(jnp.bfloat16)


def vmem_call(kernel, out_shape, operands, products):
    whole = pl.BlockSpec(memory_space=pltpu.VMEM)
    return pl.pallas_call(
        kernel,
        out_shape=out_shape,
        in_specs=[whole] * len(operands),
        out_specs=(whole,) * len(out_shape),
        compiler_params=pltpu.CompilerParams(vmem_limit_bytes=20 << 20),
        cost_estimate=pl.CostEstimate(
            flops=2 * products,
            bytes_accessed=2 * sum(array.size for array in operands),
            transcendentals=0,
        ),
    )(*operands)


def projection_kernel(inputs, others, own, first, second, left, right, near, told, part, other):
    width = near.shape[1]
    count = own.shape[0]
    half = left.shape[1]
    for index, quarter in enumerate((own, first, second)):
        held = slice(index * count, (index + 1) * count)
        near[held, :] = quarter[:, :width]
        if quarter.shape[1] > width:
            told[held, :] = quarter[:, width:]
    near[3 * count :, :half] = left[...]
    near[3 * count :, half:] = right[:, : width - half]
    if half + right.shape[1] > width:
        told[3 * count :, :] = right[:, width - half :]
    else:
        told[...] = jnp.zeros_like(told)
    part[...] = matmul(inputs[...], near[...], ((1,), (1,))).astype(part.dtype)
    other[...] = matmul(others[...], near[...], ((1,), (1,))).astype(other.dtype)


def projected(inputs, others, quarters, place):
    width = inputs.shape[1]
    count = 4 * quarters[0].shape[0]
    extra = max(quarters[0].shape[1] - width, 128)
    dtype = jnp.bfloat16 if lax.axis_size("tensor") == 1 else jnp.float32
    result = jax.ShapeDtypeStruct((inputs.shape[0], count), dtype)
    near, told, part, other = vmem_call(
        projection_kernel,
        (
            jax.ShapeDtypeStruct((count, width), jnp.bfloat16),
            jax.ShapeDtypeStruct((count, extra), jnp.bfloat16),
            result,
            result,
        ),
        (inputs, others) + tuple(quarters),
        2 * inputs.shape[0] * width * count,
    )
    other = shifted(tensor_total(other).astype(jnp.bfloat16), OWNERS, CORE)
    relative = lax.concatenate([tensor_total(part).astype(jnp.bfloat16), other], 1)
    return matmul(relative, place).astype(jnp.bfloat16), near, told


def grad_kernel(quad, *refs):
    inputs, (sent, kept) = refs[:4], refs[4:]
    count = inputs[0].shape[0]
    half = quad.shape[1] // 2
    for target, columns in ((sent, slice(half, None)), (kept, slice(0, half))):
        total = None
        for index, block in enumerate(inputs):
            part = quad[index * count : (index + 1) * count, columns]
            term = matmul(part, block[...], ((0,), (0,)))
            total = term if total is None else total + term
        target[...] = total.astype(target.dtype)


def projection_grad(relative, quad_inputs, first, second):
    depth = radices(device_count(OWNERS))[Z]
    half = relative.shape[1] // 2
    pair = lax.concatenate([relative[:, :half], shifted(relative[:, half:], OWNERS, CORE)], 0)
    half = half // 2
    quad = lax.concatenate([pair[:, :half], shifted(pair[:, half:], OWNERS, second)], 0)
    half = half // 2
    shape = (half, quad_inputs[0].shape[1])
    sent, kept = vmem_call(
        grad_kernel,
        (jax.ShapeDtypeStruct(shape, jnp.bfloat16), jax.ShapeDtypeStruct(shape, jnp.float32)),
        (quad,) + tuple(quad_inputs),
        quad.size * shape[1],
    )
    kept = kept + shifted(sent, OWNERS, first).astype(jnp.float32)
    pieces = jnp.split(kept, depth, axis=0)
    total = pieces[0]
    for step in range(1, depth):
        piece = shifted(pieces[step].astype(jnp.bfloat16), OWNERS, Z, depth - step)
        total = total + piece.astype(jnp.float32)
    return total


def matmul(left, right, contract=((1,), (0,))):
    return lax.dot_general(left, right, (contract, ((), ())), preferred_element_type=jnp.float32)


def selected(slot_ref, group, expert, slots, values=None):
    slot = slot_ref[group, expert]
    here = lax.broadcasted_iota(jnp.int32, (slots, slot.shape[1]), 0) == slot
    return jnp.where(here, 1.0 if values is None else values, 0.0).astype(jnp.bfloat16)


def weight_copies(sources, targets, arrived, expert):
    return [
        pltpu.make_async_copy(source.at[expert], target.at[expert], arrived.at[place, expert])
        for place, (source, target) in enumerate(zip(sources, targets))
    ]


def pick_rows(pick, quarters, group, target, held):
    if group < 3:
        target[held, :] = matmul(pick, quarters[group][...]).astype(jnp.bfloat16)
        return
    half = target.shape[1] // 2
    for part in (0, 1):
        columns = slice(part * half, (part + 1) * half)
        target[held, columns] = matmul(pick, quarters[3 + part][...]).astype(jnp.bfloat16)


def spread_rows(slot_ref, scale_ref, results, targets):
    experts, groups, slots, _ = results.shape
    for group in range(groups):
        weights = jnp.concatenate(
            [
                selected(
                    slot_ref,
                    group,
                    expert,
                    slots,
                    None if scale_ref is None else scale_ref[group, expert],
                )
                for expert in range(experts)
            ],
            0,
        )
        values = jnp.concatenate([results[expert, group] for expert in range(experts)], 0)
        targets[group][...] = matmul(weights, values, ((0,), (0,))).astype(jnp.bfloat16)


def forward_kernel(*refs):
    slot_ref, scale_ref, *quarters = refs[:7]
    hbm_weights = refs[7:10]
    targets = refs[10:14]
    rows, hidden, results, gate_ref, up_ref, down_ref, arrived = refs[14:]
    experts, groups, slots, _ = results.shape
    width = hidden.shape[1]
    chunk = 256
    for expert in range(experts):
        for copy in weight_copies(hbm_weights, (gate_ref, up_ref, down_ref), arrived, expert):
            copy.start()

    @pl.loop(0, experts)
    def _(expert):
        copies = weight_copies(hbm_weights, (gate_ref, up_ref, down_ref), arrived, expert)
        for group in range(groups):
            held = slice(group * slots, (group + 1) * slots)
            pick_rows(selected(slot_ref, group, expert, slots), quarters, group, rows, held)
        copies[0].wait()
        copies[1].wait()
        for start in range(0, width, chunk):
            columns = slice(start, start + chunk)
            gate_act = matmul(rows[...], gate_ref[expert, :, columns])
            up_act = matmul(rows[...], up_ref[expert, :, columns])
            act = gate_act * jax.nn.sigmoid(gate_act) * up_act
            hidden[:, columns] = act.astype(jnp.bfloat16)
        copies[2].wait()
        result = matmul(hidden[...], down_ref[expert]).astype(jnp.bfloat16)
        for group in range(groups):
            results[expert, group] = result[group * slots : (group + 1) * slots, :]

    spread_rows(slot_ref, scale_ref, results, targets)


def backward_kernel(*refs):
    slot_ref, scale_ref, *quarters = refs[:7]
    quarter_grads = refs[7:12]
    hbm_weights = refs[12:15]
    targets = refs[15:19]
    rows, grads, gate_grads, value_grads, results, gate_ref, up_ref, down_ref, arrived = refs[19:]
    experts, groups, slots, _ = results.shape
    width = gate_grads.shape[1]
    chunk = 256
    for expert in range(experts):
        for copy in weight_copies(hbm_weights, (gate_ref, up_ref, down_ref), arrived, expert):
            copy.start()

    @pl.loop(0, experts)
    def _(expert):
        for group in range(groups):
            held = slice(group * slots, (group + 1) * slots)
            pick_rows(selected(slot_ref, group, expert, slots), quarters, group, rows, held)
            weighed = selected(slot_ref, group, expert, slots, scale_ref[group, expert])
            pick_rows(weighed, quarter_grads, group, grads, held)
        for copy in weight_copies(hbm_weights, (gate_ref, up_ref, down_ref), arrived, expert):
            copy.wait()
        for start in range(0, width, chunk):
            columns = slice(start, start + chunk)
            gate_act = matmul(rows[...], gate_ref[expert, :, columns])
            up_act = matmul(rows[...], up_ref[expert, :, columns])
            hidden_grad = matmul(grads[...], down_ref[expert, columns, :], ((1,), (1,)))
            sigmoid = jax.nn.sigmoid(gate_act)
            scaled = hidden_grad * sigmoid
            gate_grad = scaled * up_act * (1.0 + gate_act * (1.0 - sigmoid))
            gate_grads[:, columns] = gate_grad.astype(jnp.bfloat16)
            value_grads[:, columns] = (scaled * gate_act).astype(jnp.bfloat16)
        result = matmul(gate_grads[...], gate_ref[expert], ((1,), (1,)))
        result = result + matmul(value_grads[...], up_ref[expert], ((1,), (1,)))
        result = result.astype(jnp.bfloat16)
        for group in range(groups):
            results[expert, group] = result[group * slots : (group + 1) * slots, :]

    spread_rows(slot_ref, None, results, targets)


def expert_call(kernel, products, buffers, plan, quarters, weights):
    slots, scales = plan
    experts, latent_width, width = weights[0].shape
    groups, _, _, span = slots.shape
    operands = (slots, scales) + tuple(quarters) + tuple(weights)
    whole = pl.BlockSpec(memory_space=pltpu.VMEM)
    picked = buffers[0].shape[0]
    scratch = list(buffers) + [
        pltpu.VMEM((experts, groups, picked // groups, latent_width), jnp.bfloat16),
        *[pltpu.VMEM(weight.shape, jnp.bfloat16) for weight in weights],
        pltpu.SemaphoreType.DMA((3, experts)),
    ]
    return pl.pallas_call(
        kernel,
        out_shape=(jax.ShapeDtypeStruct((span, latent_width), jnp.bfloat16),) * groups,
        in_specs=[whole] * (len(operands) - 3) + [pl.BlockSpec(memory_space=pl.ANY)] * 3,
        out_specs=(whole,) * groups,
        scratch_shapes=scratch,
        compiler_params=pltpu.CompilerParams(vmem_limit_bytes=36 << 20),
        cost_estimate=pl.CostEstimate(
            flops=2 * products * experts * picked * latent_width * width,
            bytes_accessed=2 * sum(array.size for array in operands),
            transcendentals=experts * picked * width,
        ),
    )(*operands)


def expert_plans(told, local_experts, row_count):
    shards = lax.axis_size("expert")
    depth = radices(shards)[Z]
    told = told.astype(jnp.int32).reshape(shards, 2, -1, row_count)
    capacity = 3 * row_count * told.shape[2] // (2 * local_experts * shards)
    mine = lax.axis_index("expert") * local_experts + jnp.arange(local_experts, dtype=jnp.int32)
    chosen = told[:, 0][:, None] == mine[None, :, None, None]
    fixed = jnp.sum(jnp.where(chosen, told[:, 1][:, None], 0), axis=2)
    member = jnp.any(chosen, axis=2)
    earlier = jnp.arange(row_count)[:, None] < jnp.arange(row_count)[None, :]
    ranking = jnp.einsum(
        "set,tu->seu",
        member.astype(jnp.bfloat16),
        earlier.astype(jnp.bfloat16),
        preferred_element_type=jnp.float32,
    ).astype(jnp.int32)
    offset = (jnp.arange(shards, dtype=jnp.int32) % depth * capacity)[:, None, None]
    slots = jnp.where(member, ranking + offset, -1)
    scales = fixed.astype(jnp.float32) / 256.0

    def by_quarter(values):
        values = values.reshape(2, 4, depth, local_experts, row_count).transpose(0, 1, 3, 2, 4)
        return values.reshape(2, 4, local_experts, 1, depth * row_count)

    slots, scales = by_quarter(slots), by_quarter(scales)
    return [(slots[core], scales[core]) for core in (0, 1)], depth * capacity


def after(value, *earlier):
    return lax.optimization_barrier((value, earlier))[0]


def local(
    tokens, out_grad, routes, combine_fixed, down_proj, up_proj, expert_gate, expert_up, expert_down
):
    local_experts, latent_width, width = expert_gate.shape
    row_count = tokens.shape[0]
    rows = down_proj.shape[0]
    told = lax.concatenate([routes.T, combine_fixed.T], 0).astype(jnp.bfloat16)
    ride = lax.axis_size("dp") == 1
    down_sent = down_proj
    if ride:
        down_sent = lax.concatenate([down_proj, told.reshape(rows, -1)], 1)
    down_own = gather_depth(down_sent, OWNERS)
    other_tokens = shifted(tokens, OWNERS, CORE)
    down_parts = gather_chips(down_own, OWNERS, Y, X)
    up_own = gather_depth(after(up_proj, down_own), OWNERS)
    other_grads = shifted(after(out_grad, down_own), OWNERS, CORE)
    up_parts = gather_chips(up_own, OWNERS, X, Y)

    down_place = placement(rows, Y, X)
    up_place = placement(rows, X, Y)
    latent, down_near, told_near = projected(tokens, other_tokens, down_parts, down_place)
    if not ride:
        told_near = joined(gather_quarters(told, EXPERT, Y, X))
    told_far = shifted(told_near, EXPERT, CORE)
    plans, slot_count = expert_plans(
        lax.concatenate([told_near, told_far], 0), local_experts, row_count
    )
    latent_own = gather_depth(latent, EXPERT)
    near = gather_chips(latent_own, EXPERT, Y, X)
    far = tuple(shifted(part, EXPERT, CORE) for part in near)
    mix_grad, up_near, _ = projected(out_grad, other_grads, up_parts, up_place)
    near_grad = gather_quarters(after(mix_grad, latent_own), EXPERT, Y, X)
    far_grad = tuple(shifted(part, EXPERT, CORE) for part in near_grad)

    narrow = pltpu.VMEM((4 * slot_count, latent_width), jnp.bfloat16)
    wide = pltpu.VMEM((4 * slot_count, width), jnp.bfloat16)
    weights = (expert_gate, expert_up, expert_down)
    scratch = (narrow, narrow, wide, wide)
    forward_near = expert_call(forward_kernel, 3, (narrow, wide), plans[0], near, weights)
    forward_far = expert_call(
        forward_kernel, 3, (narrow, wide), plans[1], after(far, forward_near), weights
    )
    backward_far = expert_call(
        backward_kernel, 5, scratch, plans[1], far + after(far_grad, forward_far), weights
    )
    forward_sums = core_totals(forward_near, forward_far)
    near_grad = after(near_grad, backward_far, forward_sums)
    backward_near = expert_call(
        backward_kernel, 5, scratch, plans[0], near + near_grad, weights
    )

    tokens, out_grad, down_far, up_far = after(
        (tokens, out_grad, down_near, up_near), forward_far
    )
    down_far = shifted(down_far, OWNERS, CORE)
    up_far = shifted(up_far, OWNERS, CORE)
    next_tokens, next_grads = shifted(tokens, OWNERS, X), shifted(out_grad, OWNERS, Y)
    quad_tokens = (tokens, other_tokens, next_tokens, shifted(next_tokens, OWNERS, CORE))
    quad_grads = (out_grad, other_grads, next_grads, shifted(next_grads, OWNERS, CORE))

    mixed_rows = tensor_total(total_tokens(*forward_sums)).astype(jnp.bfloat16)
    mixed_relative = matmul(mixed_rows, up_place, ((1,), (1,))).astype(jnp.bfloat16)
    up_grad = projection_grad(mixed_relative, quad_grads, X, Y)
    half = latent_width // 2
    layer_out = matmul(mixed_relative[:, :half], up_near)
    layer_out = (layer_out + matmul(mixed_relative[:, half:], up_far)).astype(jnp.bfloat16)

    backward_sums = core_totals(backward_near, backward_far)
    latent_grad = tensor_total(total_tokens(*backward_sums)).astype(jnp.bfloat16)
    grad_relative = matmul(latent_grad, down_place, ((1,), (1,))).astype(jnp.bfloat16)
    down_grad = projection_grad(grad_relative, quad_tokens, Y, X)
    token_grad = matmul(grad_relative[:, :half], down_near)
    token_grad = (token_grad + matmul(grad_relative[:, half:], down_far)).astype(jnp.bfloat16)
    return (layer_out, token_grad, down_grad, up_grad)


def solution(mesh):
    in_specs = (
        P(("groups", "expert", "dp"), "tensor"),
        P(("groups", "expert", "dp"), "tensor"),
        P(("groups", "expert", "dp"), None),
        P(("groups", "expert", "dp"), None),
        P(("expert", "dp"), "tensor"),
        P(("expert", "dp"), "tensor"),
        P("expert", None, "tensor"),
        P("expert", None, "tensor"),
        P("expert", "tensor", None),
    )
    out_specs = (
        P(("groups", "expert", "dp"), "tensor"),
        P(("groups", "expert", "dp"), "tensor"),
        P(("groups", "expert", "dp"), "tensor"),
        P(("groups", "expert", "dp"), "tensor"),
    )
    return jax.shard_map(local, mesh=mesh, in_specs=in_specs, out_specs=out_specs, check_vma=False)
```

```python
import math

import jax
import jax.numpy as jnp
from jax import lax
from jax.experimental import pallas as pl
from jax.experimental.pallas import tpu as pltpu
from jax.sharding import PartitionSpec as P

OWNERS = ("expert", "dp")
EXPERT = ("expert",)
Z, Y, X, CORE = 0, 1, 2, 3


def tensor_total(partial_sum):
    return lax.psum(partial_sum, "tensor")


def radices(count):
    return (count // 8, 2, 2, 2)


def digit_of(axes, place):
    sizes = radices(math.prod(lax.axis_size(axis) for axis in axes))
    stride = math.prod(sizes[place + 1 :])
    return lax.rem(lax.axis_index(axes) // stride, sizes[place])


def shifted(block, axes, *places, step=1):
    count = math.prod(lax.axis_size(axis) for axis in axes)
    sizes = radices(count)
    pairs = []
    for here in range(count):
        there = here
        for place in places:
            stride = math.prod(sizes[place + 1 :])
            digit = here // stride % sizes[place]
            there += ((digit + step) % sizes[place] - digit) * stride
        pairs.append((here, there))
    return lax.ppermute(block, axes, pairs)


SIDES = ((0, 0), (1, 0), (0, 1), (1, 1))


def device_count(axes):
    return math.prod(lax.axis_size(axis) for axis in axes)


def relative_owners(axes, first, second):
    depth = radices(device_count(axes))[Z]
    owners = []
    for core_step in (0, 1):
        for first_step, second_step in SIDES:
            for z_step in range(depth):
                steps = {Z: depth - z_step, first: first_step, second: second_step, CORE: core_step}
                owner = 0
                for place, size in enumerate(radices(device_count(axes))):
                    digit = lax.rem(digit_of(axes, place) + steps[place], size)
                    owner = owner * size + digit
                owners.append(owner)
    return jnp.stack(owners)


def gather_depth(rows, axes):
    depth = radices(device_count(axes))[Z]
    return lax.concatenate(
        [rows] + [shifted(rows, axes, Z, step=step) for step in range(1, depth)], 0
    )


def gather_chips(own, axes, first, second):
    return (
        own,
        shifted(own, axes, first),
        shifted(own, axes, second),
        shifted(own, axes, first, second),
    )


def gather_chips_by_turns(alongs, axes, first, second):
    own, along_first, along_second = alongs
    half = own.shape[1] // 2
    left = shifted(along_first[:, :half], axes, second)
    right = shifted(along_second[:, half:], axes, first)
    return (own, along_first, along_second, lax.concatenate([left, right], 1))


def core_totals(near, far):
    return [
        near[index].astype(jnp.float32) + shifted(far[index], EXPERT, CORE).astype(jnp.float32)
        for index in (3, 1, 2, 0)
    ]


def depth_total(terms, axes):
    depth = radices(device_count(axes))[Z]
    pieces = jnp.split(terms, depth, axis=0)
    total = pieces[0]
    for step in range(1, depth):
        piece = shifted(pieces[step].astype(jnp.bfloat16), axes, Z, step=depth - step)
        total = total + piece.astype(jnp.float32)
    return total


def chip_totals(across, along_y, along_x, own):
    across = shifted(across.astype(jnp.bfloat16), EXPERT, X, Y)
    along_y = shifted(along_y.astype(jnp.bfloat16), EXPERT, Y)
    along_x = shifted(along_x.astype(jnp.bfloat16), EXPERT, X)
    total = own + across.astype(jnp.float32)
    return total + along_y.astype(jnp.float32) + along_x.astype(jnp.float32)


def chip_totals_by_turns(across, along_y, along_x, own):
    across = across.astype(jnp.bfloat16)
    half = across.shape[1] // 2
    left = shifted(across[:, :half], EXPERT, X).astype(jnp.float32)
    right = shifted(across[:, half:], EXPERT, Y).astype(jnp.float32)
    along_y = lax.concatenate([along_y[:, :half] + left, along_y[:, half:]], 1)
    along_x = lax.concatenate([along_x[:, :half], along_x[:, half:] + right], 1)
    own = own + shifted(along_y.astype(jnp.bfloat16), EXPERT, Y).astype(jnp.float32)
    return own + shifted(along_x.astype(jnp.bfloat16), EXPERT, X).astype(jnp.float32)


def placement(rows, first, second):
    owners = relative_owners(OWNERS, first, second)
    targets = (owners[:, None] * rows + jnp.arange(rows, dtype=jnp.int32)[None, :]).reshape(-1)
    columns = jnp.arange(targets.shape[0], dtype=jnp.int32)
    return (targets[:, None] == columns[None, :]).astype(jnp.bfloat16)


def vmem_call(kernel, out_shape, operands, products):
    whole = pl.BlockSpec(memory_space=pltpu.VMEM)
    return pl.pallas_call(
        kernel,
        out_shape=out_shape,
        in_specs=[whole] * len(operands),
        out_specs=(whole,) * len(out_shape),
        compiler_params=pltpu.CompilerParams(vmem_limit_bytes=20 << 20),
        cost_estimate=pl.CostEstimate(
            flops=2 * products,
            bytes_accessed=2 * sum(array.size for array in operands),
            transcendentals=0,
        ),
    )(*operands)


def projection_kernel(inputs, others, *refs):
    quarters, (near, told, part, other) = refs[:4], refs[4:]
    width = near.shape[1]
    count = quarters[0].shape[0]
    for index, quarter in enumerate(quarters):
        held = slice(index * count, (index + 1) * count)
        near[held, :] = quarter[:, :width]
        if quarter.shape[1] > width:
            told[held, :] = quarter[:, width:]
        else:
            told[held, :] = jnp.zeros((count, told.shape[1]), told.dtype)
    part[...] = matmul(inputs[...], near[...], ((1,), (1,))).astype(part.dtype)
    other[...] = matmul(others[...], near[...], ((1,), (1,))).astype(other.dtype)


def projected(inputs, others, quarters, place):
    width = inputs.shape[1]
    count = 4 * quarters[0].shape[0]
    extra = max(quarters[0].shape[1] - width, 128)
    dtype = jnp.bfloat16 if lax.axis_size("tensor") == 1 else jnp.float32
    result = jax.ShapeDtypeStruct((inputs.shape[0], count), dtype)
    near, told, part, other = vmem_call(
        projection_kernel,
        (
            jax.ShapeDtypeStruct((count, width), jnp.bfloat16),
            jax.ShapeDtypeStruct((count, extra), jnp.bfloat16),
            result,
            result,
        ),
        (inputs, others) + tuple(quarters),
        2 * inputs.shape[0] * width * count,
    )
    other = shifted(tensor_total(other).astype(jnp.bfloat16), OWNERS, CORE)
    relative = lax.concatenate([tensor_total(part).astype(jnp.bfloat16), other], 1)
    return matmul(relative, place).astype(jnp.bfloat16), near, told


def grad_kernel(*refs):
    quad, inputs, (sent, kept) = refs[:4], refs[4:8], refs[8:]
    half = quad[0].shape[1] // 2
    for target, columns in ((sent, slice(half, None)), (kept, slice(0, half))):
        total = None
        for part, block in zip(quad, inputs):
            term = matmul(part[:, columns], block[...], ((0,), (0,)))
            total = term if total is None else total + term
        target[...] = total.astype(target.dtype)


def projection_grad(relative, quad_inputs, first, second):
    mine, along_second, along_core, across = jnp.split(relative, 4, axis=1)
    quad = (
        mine,
        shifted(along_core, OWNERS, CORE),
        shifted(along_second, OWNERS, second),
        shifted(across, OWNERS, second, CORE),
    )
    half = mine.shape[1] // 2
    shape = (half, quad_inputs[0].shape[1])
    sent, kept = vmem_call(
        grad_kernel,
        (jax.ShapeDtypeStruct(shape, jnp.bfloat16), jax.ShapeDtypeStruct(shape, jnp.float32)),
        quad + tuple(quad_inputs),
        4 * mine.size * shape[1],
    )
    kept = kept + shifted(sent, OWNERS, first).astype(jnp.float32)
    return depth_total(kept, OWNERS)


def matmul(left, right, contract=((1,), (0,))):
    return lax.dot_general(left, right, (contract, ((), ())), preferred_element_type=jnp.float32)


def selected(slot_ref, group, expert, slots, values=None):
    slot = slot_ref[group, expert]
    here = lax.broadcasted_iota(jnp.int32, (slots, slot.shape[1]), 0) == slot
    return jnp.where(here, 1.0 if values is None else values, 0.0).astype(jnp.bfloat16)


def weight_copies(sources, targets, arrived, expert):
    return [
        pltpu.make_async_copy(source.at[expert], target.at[expert], arrived.at[place, expert])
        for place, (source, target) in enumerate(zip(sources, targets))
    ]


def pick_rows(pick, quarter, target, held):
    target[held, :] = matmul(pick, quarter[...]).astype(jnp.bfloat16)


def spread_rows(slot_ref, scale_ref, results, targets):
    experts, groups, slots, _ = results.shape
    for group in range(groups):
        weights = jnp.concatenate(
            [
                selected(
                    slot_ref,
                    group,
                    expert,
                    slots,
                    None if scale_ref is None else scale_ref[group, expert],
                )
                for expert in range(experts)
            ],
            0,
        )
        values = jnp.concatenate([results[expert, group] for expert in range(experts)], 0)
        targets[group][...] = matmul(weights, values, ((0,), (0,))).astype(jnp.bfloat16)


def forward_kernel(*refs):
    slot_ref, scale_ref, *quarters = refs[:6]
    hbm_weights = refs[6:9]
    targets = refs[9:13]
    rows, hidden, results, gate_ref, up_ref, down_ref, arrived = refs[13:]
    experts, groups, slots, _ = results.shape
    width = hidden.shape[1]
    chunk = 256
    for expert in range(experts):
        for copy in weight_copies(hbm_weights, (gate_ref, up_ref, down_ref), arrived, expert):
            copy.start()

    @pl.loop(0, experts)
    def _(expert):
        copies = weight_copies(hbm_weights, (gate_ref, up_ref, down_ref), arrived, expert)
        for group in range(groups):
            held = slice(group * slots, (group + 1) * slots)
            pick_rows(selected(slot_ref, group, expert, slots), quarters[group], rows, held)
        copies[0].wait()
        copies[1].wait()
        for start in range(0, width, chunk):
            columns = slice(start, start + chunk)
            gate_act = matmul(rows[...], gate_ref[expert, :, columns])
            up_act = matmul(rows[...], up_ref[expert, :, columns])
            act = gate_act * jax.nn.sigmoid(gate_act) * up_act
            hidden[:, columns] = act.astype(jnp.bfloat16)
        copies[2].wait()
        result = matmul(hidden[...], down_ref[expert]).astype(jnp.bfloat16)
        for group in range(groups):
            results[expert, group] = result[group * slots : (group + 1) * slots, :]

    spread_rows(slot_ref, scale_ref, results, targets)


def backward_kernel(*refs):
    slot_ref, scale_ref, *quarters = refs[:6]
    quarter_grads = refs[6:10]
    hbm_weights = refs[10:13]
    targets = refs[13:17]
    rows, grads, gate_grads, value_grads, results, gate_ref, up_ref, down_ref, arrived = refs[17:]
    experts, groups, slots, _ = results.shape
    width = gate_grads.shape[1]
    chunk = 256
    for expert in range(experts):
        for copy in weight_copies(hbm_weights, (gate_ref, up_ref, down_ref), arrived, expert):
            copy.start()

    @pl.loop(0, experts)
    def _(expert):
        for group in range(groups):
            held = slice(group * slots, (group + 1) * slots)
            pick_rows(selected(slot_ref, group, expert, slots), quarters[group], rows, held)
            weighed = selected(slot_ref, group, expert, slots, scale_ref[group, expert])
            pick_rows(weighed, quarter_grads[group], grads, held)
        for copy in weight_copies(hbm_weights, (gate_ref, up_ref, down_ref), arrived, expert):
            copy.wait()
        for start in range(0, width, chunk):
            columns = slice(start, start + chunk)
            gate_act = matmul(rows[...], gate_ref[expert, :, columns])
            up_act = matmul(rows[...], up_ref[expert, :, columns])
            hidden_grad = matmul(grads[...], down_ref[expert, columns, :], ((1,), (1,)))
            sigmoid = jax.nn.sigmoid(gate_act)
            scaled = hidden_grad * sigmoid
            gate_grad = scaled * up_act * (1.0 + gate_act * (1.0 - sigmoid))
            gate_grads[:, columns] = gate_grad.astype(jnp.bfloat16)
            value_grads[:, columns] = (scaled * gate_act).astype(jnp.bfloat16)
        result = matmul(gate_grads[...], gate_ref[expert], ((1,), (1,)))
        result = result + matmul(value_grads[...], up_ref[expert], ((1,), (1,)))
        result = result.astype(jnp.bfloat16)
        for group in range(groups):
            results[expert, group] = result[group * slots : (group + 1) * slots, :]

    spread_rows(slot_ref, None, results, targets)


def expert_call(kernel, products, buffers, plan, quarters, weights):
    slots, scales = plan
    experts, latent_width, width = weights[0].shape
    groups, _, _, span = slots.shape
    operands = (slots, scales) + tuple(quarters) + tuple(weights)
    whole = pl.BlockSpec(memory_space=pltpu.VMEM)
    picked = buffers[0].shape[0]
    scratch = list(buffers) + [
        pltpu.VMEM((experts, groups, picked // groups, latent_width), jnp.bfloat16),
        *[pltpu.VMEM(weight.shape, jnp.bfloat16) for weight in weights],
        pltpu.SemaphoreType.DMA((3, experts)),
    ]
    return pl.pallas_call(
        kernel,
        out_shape=(jax.ShapeDtypeStruct((span, latent_width), jnp.bfloat16),) * groups,
        in_specs=[whole] * (len(operands) - 3) + [pl.BlockSpec(memory_space=pl.ANY)] * 3,
        out_specs=(whole,) * groups,
        scratch_shapes=scratch,
        compiler_params=pltpu.CompilerParams(vmem_limit_bytes=36 << 20),
        cost_estimate=pl.CostEstimate(
            flops=2 * products * experts * picked * latent_width * width,
            bytes_accessed=2 * sum(array.size for array in operands),
            transcendentals=experts * picked * width,
        ),
    )(*operands)


def expert_plans(told, local_experts, row_count):
    shards = lax.axis_size("expert")
    depth = radices(shards)[Z]
    told = told.astype(jnp.int32).reshape(shards, 2, -1, row_count)
    capacity = 3 * row_count * told.shape[2] // (2 * local_experts * shards)
    mine = lax.axis_index("expert") * local_experts + jnp.arange(local_experts, dtype=jnp.int32)
    chosen = told[:, 0][:, None] == mine[None, :, None, None]
    fixed = jnp.sum(jnp.where(chosen, told[:, 1][:, None], 0), axis=2)
    member = jnp.any(chosen, axis=2)
    earlier = jnp.arange(row_count)[:, None] < jnp.arange(row_count)[None, :]
    ranking = jnp.einsum(
        "set,tu->seu",
        member.astype(jnp.bfloat16),
        earlier.astype(jnp.bfloat16),
        preferred_element_type=jnp.float32,
    ).astype(jnp.int32)
    offset = (jnp.arange(shards, dtype=jnp.int32) % depth * capacity)[:, None, None]
    slots = jnp.where(member, ranking + offset, -1)
    scales = fixed.astype(jnp.float32) / 256.0

    def by_quarter(values):
        values = values.reshape(2, 4, depth, local_experts, row_count).transpose(0, 1, 3, 2, 4)
        return values.reshape(2, 4, local_experts, 1, depth * row_count)

    slots, scales = by_quarter(slots), by_quarter(scales)
    return [(slots[core], scales[core]) for core in (0, 1)], depth * capacity


def after(value, *earlier):
    return lax.optimization_barrier((value, earlier))[0]


def local(
    tokens, out_grad, routes, combine_fixed, down_proj, up_proj, expert_gate, expert_up, expert_down
):
    local_experts, latent_width, width = expert_gate.shape
    row_count = tokens.shape[0]
    rows = down_proj.shape[0]
    told = lax.concatenate([routes.T, combine_fixed.T], 0).astype(jnp.bfloat16)
    ride = lax.axis_size("dp") == 1
    down_sent = down_proj
    if ride:
        down_sent = lax.concatenate([down_proj, told.reshape(rows, -1)], 1)
    down_own = gather_depth(down_sent, OWNERS)
    other_tokens = shifted(tokens, OWNERS, CORE)
    next_tokens = shifted(tokens, OWNERS, X)
    down_parts = gather_chips(down_own, OWNERS, Y, X)
    next_grads = shifted(out_grad, OWNERS, Y)
    up_own = gather_depth(after(up_proj, down_own), OWNERS)
    other_grads = shifted(after(out_grad, down_own), OWNERS, CORE)
    up_parts = gather_chips(up_own, OWNERS, X, Y)

    down_place = placement(rows, Y, X)
    up_place = placement(rows, X, Y)
    latent, down_near, told_near = projected(
        after(tokens, next_tokens), other_tokens, down_parts, down_place
    )
    if not ride:
        told_near = lax.concatenate(
            list(gather_chips(gather_depth(told, EXPERT), EXPERT, Y, X)), 0
        )
    latent_own = gather_depth(latent, EXPERT)
    told_far = shifted(after(told_near, latent), EXPERT, CORE)
    plans, slot_count = expert_plans(
        lax.concatenate([told_near, told_far], 0), local_experts, row_count
    )
    near = (latent_own, shifted(latent_own, EXPERT, Y), shifted(latent_own, EXPERT, X))
    mix_grad, up_near, _ = projected(
        after(out_grad, next_grads), other_grads, after(up_parts, latent), up_place
    )
    mix_own = gather_depth(after(mix_grad, latent_own), EXPERT)
    mix_own, near = lax.optimization_barrier((mix_own, near))
    near = gather_chips_by_turns(near, EXPERT, Y, X)
    far = tuple(shifted(part, EXPERT, CORE) for part in near)
    near_grad = (mix_own, shifted(mix_own, EXPERT, Y), shifted(mix_own, EXPERT, X))

    narrow = pltpu.VMEM((4 * slot_count, latent_width), jnp.bfloat16)
    wide = pltpu.VMEM((4 * slot_count, width), jnp.bfloat16)
    weights = (expert_gate, expert_up, expert_down)
    scratch = (narrow, narrow, wide, wide)
    forward_near = expert_call(forward_kernel, 3, (narrow, wide), plans[0], near, weights)
    near_grad = gather_chips_by_turns(after(near_grad, forward_near), EXPERT, Y, X)
    forward_far = expert_call(
        forward_kernel, 3, (narrow, wide), plans[1], after(far, forward_near), weights
    )
    far_grad = tuple(shifted(part, EXPERT, CORE) for part in near_grad)
    forward_sums = core_totals(forward_near, forward_far)
    far_grad = after(far_grad, forward_sums)
    backward_far = expert_call(
        backward_kernel, 5, scratch, plans[1], far + far_grad, weights
    )
    near_grad = after(near_grad, backward_far)
    backward_near = expert_call(
        backward_kernel, 5, scratch, plans[0], near + near_grad, weights
    )

    down_far, up_far, last_tokens, last_grads = after(
        (down_near, up_near, next_tokens, next_grads), forward_far
    )
    down_far = shifted(down_far, OWNERS, CORE)
    up_far = shifted(up_far, OWNERS, CORE)
    last_tokens = shifted(last_tokens, OWNERS, CORE)
    last_grads = shifted(last_grads, OWNERS, CORE)
    quad_tokens = (tokens, other_tokens, next_tokens, last_tokens)
    quad_grads = (out_grad, other_grads, next_grads, last_grads)

    mixed_rows = depth_total(chip_totals(*forward_sums), EXPERT)
    mixed_rows = tensor_total(mixed_rows).astype(jnp.bfloat16)
    mixed_relative = matmul(mixed_rows, up_place, ((1,), (1,))).astype(jnp.bfloat16)
    up_grad = projection_grad(mixed_relative, quad_grads, X, Y)
    half = latent_width // 2
    layer_out = matmul(mixed_relative[:, :half], up_near)
    layer_out = (layer_out + matmul(mixed_relative[:, half:], up_far)).astype(jnp.bfloat16)

    backward_sums = core_totals(backward_near, backward_far)
    latent_grad = depth_total(chip_totals_by_turns(*backward_sums), EXPERT)
    latent_grad = tensor_total(latent_grad).astype(jnp.bfloat16)
    grad_relative = matmul(latent_grad, down_place, ((1,), (1,))).astype(jnp.bfloat16)
    down_grad = projection_grad(grad_relative, quad_tokens, Y, X)
    token_grad = matmul(grad_relative[:, :half], down_near)
    token_grad = (token_grad + matmul(grad_relative[:, half:], down_far)).astype(jnp.bfloat16)
    return (layer_out, token_grad, down_grad, up_grad)


def solution(mesh):
    in_specs = (
        P(("groups", "expert", "dp"), "tensor"),
        P(("groups", "expert", "dp"), "tensor"),
        P(("groups", "expert", "dp"), None),
        P(("groups", "expert", "dp"), None),
        P(("expert", "dp"), "tensor"),
        P(("expert", "dp"), "tensor"),
        P("expert", None, "tensor"),
        P("expert", None, "tensor"),
        P("expert", "tensor", None),
    )
    out_specs = (
        P(("groups", "expert", "dp"), "tensor"),
        P(("groups", "expert", "dp"), "tensor"),
        P(("groups", "expert", "dp"), "tensor"),
        P(("groups", "expert", "dp"), "tensor"),
    )
    return jax.shard_map(local, mesh=mesh, in_specs=in_specs, out_specs=out_specs, check_vma=False)
```

```python
import math

import jax
import jax.numpy as jnp
from jax import lax
from jax.experimental import pallas as pl
from jax.experimental.pallas import tpu as pltpu
from jax.sharding import PartitionSpec as P

OWNERS = ("expert", "dp")
EXPERT = ("expert",)
Z, Y, X, CORE = 0, 1, 2, 3


def tensor_total(partial_sum):
    return lax.psum(partial_sum, "tensor")


def radices(count):
    return (count // 8, 2, 2, 2)


def digit_of(axes, place):
    sizes = radices(math.prod(lax.axis_size(axis) for axis in axes))
    stride = math.prod(sizes[place + 1 :])
    return lax.rem(lax.axis_index(axes) // stride, sizes[place])


def shifted(block, axes, *places, step=1):
    count = math.prod(lax.axis_size(axis) for axis in axes)
    sizes = radices(count)
    pairs = []
    for here in range(count):
        there = here
        for place in places:
            stride = math.prod(sizes[place + 1 :])
            digit = here // stride % sizes[place]
            there += ((digit + step) % sizes[place] - digit) * stride
        pairs.append((here, there))
    return lax.ppermute(block, axes, pairs)


SIDES = ((0, 0), (1, 0), (0, 1), (1, 1))


def device_count(axes):
    return math.prod(lax.axis_size(axis) for axis in axes)


def relative_owners(axes, first, second):
    depth = radices(device_count(axes))[Z]
    owners = []
    for core_step in (0, 1):
        for first_step, second_step in SIDES:
            for z_step in range(depth):
                steps = {Z: depth - z_step, first: first_step, second: second_step, CORE: core_step}
                owner = 0
                for place, size in enumerate(radices(device_count(axes))):
                    digit = lax.rem(digit_of(axes, place) + steps[place], size)
                    owner = owner * size + digit
                owners.append(owner)
    return jnp.stack(owners)


def gather_depth(rows, axes):
    depth = radices(device_count(axes))[Z]
    return lax.concatenate(
        [rows] + [shifted(rows, axes, Z, step=step) for step in range(1, depth)], 0
    )


def gather_chips(own, axes, first, second):
    return (
        own,
        shifted(own, axes, first),
        shifted(own, axes, second),
        shifted(own, axes, first, second),
    )


def gather_chips_by_turns(alongs, axes, first, second):
    own, along_first, along_second = alongs
    half = own.shape[1] // 2
    left = shifted(along_first[:, :half], axes, second)
    right = shifted(along_second[:, half:], axes, first)
    return (own, along_first, along_second, lax.concatenate([left, right], 1))


def core_totals(near, far):
    return [
        near[index].astype(jnp.float32) + shifted(far[index], EXPERT, CORE).astype(jnp.float32)
        for index in (3, 1, 2, 0)
    ]


def depth_total(terms, axes):
    depth = radices(device_count(axes))[Z]
    pieces = jnp.split(terms, depth, axis=0)
    total = pieces[0]
    for step in range(1, depth):
        piece = shifted(pieces[step].astype(jnp.bfloat16), axes, Z, step=depth - step)
        total = total + piece.astype(jnp.float32)
    return total


def chip_totals(across, along_y, along_x, own):
    across = shifted(across.astype(jnp.bfloat16), EXPERT, X, Y)
    along_y = shifted(along_y.astype(jnp.bfloat16), EXPERT, Y)
    along_x = shifted(along_x.astype(jnp.bfloat16), EXPERT, X)
    total = own + across.astype(jnp.float32)
    return total + along_y.astype(jnp.float32) + along_x.astype(jnp.float32)


def across_by_turns(across):
    across = across.astype(jnp.bfloat16)
    half = across.shape[1] // 2
    return shifted(across[:, :half], EXPERT, X), shifted(across[:, half:], EXPERT, Y)


def chip_totals_by_turns(left, right, along_y, along_x, own):
    half = left.shape[1]
    left, right = left.astype(jnp.float32), right.astype(jnp.float32)
    along_y = lax.concatenate([along_y[:, :half] + left, along_y[:, half:]], 1)
    along_x = lax.concatenate([along_x[:, :half], along_x[:, half:] + right], 1)
    own = own + shifted(along_y.astype(jnp.bfloat16), EXPERT, Y).astype(jnp.float32)
    return own + shifted(along_x.astype(jnp.bfloat16), EXPERT, X).astype(jnp.float32)


def placement(rows, first, second):
    owners = relative_owners(OWNERS, first, second)
    targets = (owners[:, None] * rows + jnp.arange(rows, dtype=jnp.int32)[None, :]).reshape(-1)
    columns = jnp.arange(targets.shape[0], dtype=jnp.int32)
    return (targets[:, None] == columns[None, :]).astype(jnp.bfloat16)


def vmem_call(kernel, out_shape, operands, products):
    whole = pl.BlockSpec(memory_space=pltpu.VMEM)
    return pl.pallas_call(
        kernel,
        out_shape=out_shape,
        in_specs=[whole] * len(operands),
        out_specs=(whole,) * len(out_shape),
        compiler_params=pltpu.CompilerParams(vmem_limit_bytes=20 << 20),
        cost_estimate=pl.CostEstimate(
            flops=2 * products,
            bytes_accessed=2 * sum(array.size for array in operands),
            transcendentals=0,
        ),
    )(*operands)


def projection_kernel(inputs, others, *refs):
    quarters, (near, told, part, other) = refs[:4], refs[4:]
    width = near.shape[1]
    count = quarters[0].shape[0]
    for index, quarter in enumerate(quarters):
        held = slice(index * count, (index + 1) * count)
        near[held, :] = quarter[:, :width]
        if quarter.shape[1] > width:
            told[held, :] = quarter[:, width:]
        else:
            told[held, :] = jnp.zeros((count, told.shape[1]), told.dtype)
    part[...] = matmul(inputs[...], near[...], ((1,), (1,))).astype(part.dtype)
    other[...] = matmul(others[...], near[...], ((1,), (1,))).astype(other.dtype)


def projected(inputs, others, quarters, place):
    width = inputs.shape[1]
    count = 4 * quarters[0].shape[0]
    extra = max(quarters[0].shape[1] - width, 128)
    dtype = jnp.bfloat16 if lax.axis_size("tensor") == 1 else jnp.float32
    result = jax.ShapeDtypeStruct((inputs.shape[0], count), dtype)
    near, told, part, other = vmem_call(
        projection_kernel,
        (
            jax.ShapeDtypeStruct((count, width), jnp.bfloat16),
            jax.ShapeDtypeStruct((count, extra), jnp.bfloat16),
            result,
            result,
        ),
        (inputs, others) + tuple(quarters),
        2 * inputs.shape[0] * width * count,
    )
    other = shifted(tensor_total(other).astype(jnp.bfloat16), OWNERS, CORE)
    relative = lax.concatenate([tensor_total(part).astype(jnp.bfloat16), other], 1)
    return matmul(relative, place).astype(jnp.bfloat16), near, told


def grad_kernel(*refs):
    quad, inputs, (sent, kept) = refs[:4], refs[4:8], refs[8:]
    half = quad[0].shape[1] // 2
    for target, columns in ((sent, slice(half, None)), (kept, slice(0, half))):
        total = None
        for part, block in zip(quad, inputs):
            term = matmul(part[:, columns], block[...], ((0,), (0,)))
            total = term if total is None else total + term
        target[...] = total.astype(target.dtype)


def quad_columns(relative, second):
    mine, along_second, along_core, across = jnp.split(relative, 4, axis=1)
    return (
        mine,
        shifted(along_core, OWNERS, CORE),
        shifted(along_second, OWNERS, second),
        shifted(across, OWNERS, second, CORE),
    )


def quad_grads_of(quad, quad_inputs):
    shape = (quad[0].shape[1] // 2, quad_inputs[0].shape[1])
    return vmem_call(
        grad_kernel,
        (jax.ShapeDtypeStruct(shape, jnp.bfloat16), jax.ShapeDtypeStruct(shape, jnp.float32)),
        quad + tuple(quad_inputs),
        4 * quad[0].size * shape[1],
    )


def matmul(left, right, contract=((1,), (0,))):
    return lax.dot_general(left, right, (contract, ((), ())), preferred_element_type=jnp.float32)


def selected(slot_ref, group, expert, slots, values=None):
    slot = slot_ref[group, expert]
    here = lax.broadcasted_iota(jnp.int32, (slots, slot.shape[1]), 0) == slot
    return jnp.where(here, 1.0 if values is None else values, 0.0).astype(jnp.bfloat16)


def weight_copies(sources, targets, arrived, expert):
    return [
        pltpu.make_async_copy(source.at[expert], target.at[expert], arrived.at[place, expert])
        for place, (source, target) in enumerate(zip(sources, targets))
    ]


def pick_rows(pick, quarter, target, held):
    target[held, :] = matmul(pick, quarter[...]).astype(jnp.bfloat16)


def spread_rows(slot_ref, scale_ref, results, targets):
    experts, groups, slots, _ = results.shape
    for group in range(groups):
        weights = jnp.concatenate(
            [
                selected(
                    slot_ref,
                    group,
                    expert,
                    slots,
                    None if scale_ref is None else scale_ref[group, expert],
                )
                for expert in range(experts)
            ],
            0,
        )
        values = jnp.concatenate([results[expert, group] for expert in range(experts)], 0)
        targets[group][...] = matmul(weights, values, ((0,), (0,))).astype(jnp.bfloat16)


def forward_kernel(*refs):
    slot_ref, scale_ref, *quarters = refs[:6]
    hbm_weights = refs[6:9]
    targets = refs[9:13]
    rows, hidden, results, gate_ref, up_ref, down_ref, arrived = refs[13:]
    experts, groups, slots, _ = results.shape
    width = hidden.shape[1]
    chunk = 256
    for expert in range(experts):
        for copy in weight_copies(hbm_weights, (gate_ref, up_ref, down_ref), arrived, expert):
            copy.start()

    @pl.loop(0, experts)
    def _(expert):
        copies = weight_copies(hbm_weights, (gate_ref, up_ref, down_ref), arrived, expert)
        for group in range(groups):
            held = slice(group * slots, (group + 1) * slots)
            pick_rows(selected(slot_ref, group, expert, slots), quarters[group], rows, held)
        copies[0].wait()
        copies[1].wait()
        for start in range(0, width, chunk):
            columns = slice(start, start + chunk)
            gate_act = matmul(rows[...], gate_ref[expert, :, columns])
            up_act = matmul(rows[...], up_ref[expert, :, columns])
            act = gate_act * jax.nn.sigmoid(gate_act) * up_act
            hidden[:, columns] = act.astype(jnp.bfloat16)
        copies[2].wait()
        result = matmul(hidden[...], down_ref[expert]).astype(jnp.bfloat16)
        for group in range(groups):
            results[expert, group] = result[group * slots : (group + 1) * slots, :]

    spread_rows(slot_ref, scale_ref, results, targets)


def backward_kernel(*refs):
    slot_ref, scale_ref, *quarters = refs[:6]
    quarter_grads = refs[6:10]
    hbm_weights = refs[10:13]
    targets = refs[13:17]
    rows, grads, gate_grads, value_grads, results, gate_ref, up_ref, down_ref, arrived = refs[17:]
    experts, groups, slots, _ = results.shape
    width = gate_grads.shape[1]
    chunk = 256
    for expert in range(experts):
        for copy in weight_copies(hbm_weights, (gate_ref, up_ref, down_ref), arrived, expert):
            copy.start()

    @pl.loop(0, experts)
    def _(expert):
        for group in range(groups):
            held = slice(group * slots, (group + 1) * slots)
            pick_rows(selected(slot_ref, group, expert, slots), quarters[group], rows, held)
            weighed = selected(slot_ref, group, expert, slots, scale_ref[group, expert])
            pick_rows(weighed, quarter_grads[group], grads, held)
        for copy in weight_copies(hbm_weights, (gate_ref, up_ref, down_ref), arrived, expert):
            copy.wait()
        for start in range(0, width, chunk):
            columns = slice(start, start + chunk)
            gate_act = matmul(rows[...], gate_ref[expert, :, columns])
            up_act = matmul(rows[...], up_ref[expert, :, columns])
            hidden_grad = matmul(grads[...], down_ref[expert, columns, :], ((1,), (1,)))
            sigmoid = jax.nn.sigmoid(gate_act)
            scaled = hidden_grad * sigmoid
            gate_grad = scaled * up_act * (1.0 + gate_act * (1.0 - sigmoid))
            gate_grads[:, columns] = gate_grad.astype(jnp.bfloat16)
            value_grads[:, columns] = (scaled * gate_act).astype(jnp.bfloat16)
        result = matmul(gate_grads[...], gate_ref[expert], ((1,), (1,)))
        result = result + matmul(value_grads[...], up_ref[expert], ((1,), (1,)))
        result = result.astype(jnp.bfloat16)
        for group in range(groups):
            results[expert, group] = result[group * slots : (group + 1) * slots, :]

    spread_rows(slot_ref, None, results, targets)


def expert_call(kernel, products, buffers, plan, quarters, weights):
    slots, scales = plan
    experts, latent_width, width = weights[0].shape
    groups, _, _, span = slots.shape
    operands = (slots, scales) + tuple(quarters) + tuple(weights)
    whole = pl.BlockSpec(memory_space=pltpu.VMEM)
    picked = buffers[0].shape[0]
    scratch = list(buffers) + [
        pltpu.VMEM((experts, groups, picked // groups, latent_width), jnp.bfloat16),
        *[pltpu.VMEM(weight.shape, jnp.bfloat16) for weight in weights],
        pltpu.SemaphoreType.DMA((3, experts)),
    ]
    return pl.pallas_call(
        kernel,
        out_shape=(jax.ShapeDtypeStruct((span, latent_width), jnp.bfloat16),) * groups,
        in_specs=[whole] * (len(operands) - 3) + [pl.BlockSpec(memory_space=pl.ANY)] * 3,
        out_specs=(whole,) * groups,
        scratch_shapes=scratch,
        compiler_params=pltpu.CompilerParams(vmem_limit_bytes=36 << 20),
        cost_estimate=pl.CostEstimate(
            flops=2 * products * experts * picked * latent_width * width,
            bytes_accessed=2 * sum(array.size for array in operands),
            transcendentals=experts * picked * width,
        ),
    )(*operands)


def expert_plans(told, local_experts, row_count):
    shards = lax.axis_size("expert")
    depth = radices(shards)[Z]
    told = told.astype(jnp.int32).reshape(shards, 2, -1, row_count)
    capacity = 3 * row_count * told.shape[2] // (2 * local_experts * shards)
    mine = lax.axis_index("expert") * local_experts + jnp.arange(local_experts, dtype=jnp.int32)
    chosen = told[:, 0][:, None] == mine[None, :, None, None]
    fixed = jnp.sum(jnp.where(chosen, told[:, 1][:, None], 0), axis=2)
    member = jnp.any(chosen, axis=2)
    earlier = jnp.arange(row_count)[:, None] < jnp.arange(row_count)[None, :]
    ranking = jnp.einsum(
        "set,tu->seu",
        member.astype(jnp.bfloat16),
        earlier.astype(jnp.bfloat16),
        preferred_element_type=jnp.float32,
    ).astype(jnp.int32)
    offset = (jnp.arange(shards, dtype=jnp.int32) % depth * capacity)[:, None, None]
    slots = jnp.where(member, ranking + offset, -1)
    scales = fixed.astype(jnp.float32) / 256.0

    def by_quarter(values):
        values = values.reshape(2, 4, depth, local_experts, row_count).transpose(0, 1, 3, 2, 4)
        return values.reshape(2, 4, local_experts, 1, depth * row_count)

    slots, scales = by_quarter(slots), by_quarter(scales)
    return [(slots[core], scales[core]) for core in (0, 1)], depth * capacity


def tied(*values):
    return lax.optimization_barrier(values)


def local(
    tokens, out_grad, routes, combine_fixed, down_proj, up_proj, expert_gate, expert_up, expert_down
):
    local_experts, latent_width, width = expert_gate.shape
    row_count = tokens.shape[0]
    rows = down_proj.shape[0]
    told = lax.concatenate([routes.T, combine_fixed.T], 0).astype(jnp.bfloat16)
    ride = lax.axis_size("dp") == 1
    down_sent = down_proj
    if ride:
        down_sent = lax.concatenate([down_proj, told.reshape(rows, -1)], 1)
    next_tokens, next_grads = shifted(tokens, OWNERS, X), shifted(out_grad, OWNERS, Y)
    down_own, later_tokens, later_up = tied(
        gather_depth(down_sent, OWNERS), tokens, up_proj
    )
    down_parts = gather_chips(down_own, OWNERS, Y, X)
    other_tokens = shifted(later_tokens, OWNERS, CORE)
    up_own = gather_depth(later_up, OWNERS)
    down_parts, next_tokens, next_grads = tied(down_parts, next_tokens, next_grads)

    down_place = placement(rows, Y, X)
    up_place = placement(rows, X, Y)
    latent, down_near, told_near = projected(tokens, other_tokens, down_parts, down_place)
    if not ride:
        told_near = lax.concatenate(
            list(gather_chips(gather_depth(told, EXPERT), EXPERT, Y, X)), 0
        )
    latent, up_own, later_grads, next_tokens, next_grads = tied(
        latent, up_own, out_grad, next_tokens, next_grads
    )
    latent_own = gather_depth(latent, EXPERT)
    up_parts = gather_chips(up_own, OWNERS, X, Y)
    other_grads = shifted(later_grads, OWNERS, CORE)
    last_tokens = shifted(next_tokens, OWNERS, CORE)
    last_grads = shifted(next_grads, OWNERS, CORE)
    latent_own, told_near = tied(latent_own, told_near)
    near = (latent_own, shifted(latent_own, EXPERT, Y), shifted(latent_own, EXPERT, X))
    up_parts, latent_own, last_tokens, last_grads = tied(
        up_parts, latent_own, last_tokens, last_grads
    )
    near = (latent_own,) + near[1:]
    mix_grad, up_near, _ = projected(out_grad, other_grads, up_parts, up_place)
    mix_own = gather_depth(mix_grad, EXPERT)
    told_far = shifted(told_near, EXPERT, CORE)
    plans, slot_count = expert_plans(
        lax.concatenate([told_near, told_far], 0), local_experts, row_count
    )
    mix_own, near = tied(mix_own, gather_chips_by_turns(near, EXPERT, Y, X))
    far = tuple(shifted(part, EXPERT, CORE) for part in near)
    near_grad = (mix_own, shifted(mix_own, EXPERT, Y), shifted(mix_own, EXPERT, X))

    narrow = pltpu.VMEM((4 * slot_count, latent_width), jnp.bfloat16)
    wide = pltpu.VMEM((4 * slot_count, width), jnp.bfloat16)
    weights = (expert_gate, expert_up, expert_down)
    scratch = (narrow, narrow, wide, wide)
    forward_near = expert_call(forward_kernel, 3, (narrow, wide), plans[0], near, weights)
    forward_near, far, down_near, up_near = tied(forward_near, far, down_near, up_near)
    near_grad = gather_chips_by_turns(near_grad, EXPERT, Y, X)
    forward_far = expert_call(forward_kernel, 3, (narrow, wide), plans[1], far, weights)
    far_grad = tuple(shifted(part, EXPERT, CORE) for part in near_grad)
    down_far = shifted(down_near, OWNERS, CORE)
    up_far = shifted(up_near, OWNERS, CORE)
    across, along_y, along_x, own = core_totals(forward_near, forward_far)
    forward_sums = [part.astype(jnp.bfloat16) for part in (across, along_y, along_x)] + [own]
    far_grad, forward_sums = tied(far_grad, forward_sums)
    backward_far = expert_call(
        backward_kernel, 5, scratch, plans[1], far + tuple(far_grad), weights
    )
    near_grad, backward_far, down_far, up_far = tied(near_grad, backward_far, down_far, up_far)
    backward_near = expert_call(
        backward_kernel, 5, scratch, plans[0], near + tuple(near_grad), weights
    )
    quad_tokens = (tokens, other_tokens, next_tokens, last_tokens)
    quad_grads = (out_grad, other_grads, next_grads, last_grads)

    mixed_sums = chip_totals(*forward_sums)
    backward_across, *backward_sums = core_totals(backward_near, backward_far)
    backward_across = across_by_turns(backward_across)
    mixed_sums, backward_sums = tied(mixed_sums, backward_sums)
    mixed_rows = tensor_total(depth_total(mixed_sums, EXPERT)).astype(jnp.bfloat16)
    mixed_relative = matmul(mixed_rows, up_place, ((1,), (1,))).astype(jnp.bfloat16)
    mixed_relative, backward_across = tied(mixed_relative, backward_across)
    latent_sums = chip_totals_by_turns(*backward_across, *backward_sums)
    quad = quad_columns(mixed_relative, Y)
    quad, latent_sums = tied(quad, latent_sums)
    latent_grad = tensor_total(depth_total(latent_sums, EXPERT)).astype(jnp.bfloat16)
    up_sent, up_kept = quad_grads_of(quad, quad_grads)
    up_sums = up_kept + shifted(up_sent, OWNERS, X).astype(jnp.float32)
    grad_relative = matmul(latent_grad, down_place, ((1,), (1,))).astype(jnp.bfloat16)
    up_sums, mixed_relative, grad_relative = tied(up_sums, mixed_relative, grad_relative)
    quad = quad_columns(grad_relative, X)
    up_grad = depth_total(up_sums, OWNERS)
    down_sent, down_kept = quad_grads_of(quad, quad_tokens)
    down_sums = down_kept + shifted(down_sent, OWNERS, Y).astype(jnp.float32)
    half = latent_width // 2
    layer_out = matmul(mixed_relative[:, :half], up_near)
    layer_out = (layer_out + matmul(mixed_relative[:, half:], up_far)).astype(jnp.bfloat16)
    token_grad = matmul(grad_relative[:, :half], down_near)
    token_grad = (token_grad + matmul(grad_relative[:, half:], down_far)).astype(jnp.bfloat16)
    down_grad = depth_total(down_sums, OWNERS)
    return (layer_out, token_grad, down_grad, up_grad)


def solution(mesh):
    in_specs = (
        P(("groups", "expert", "dp"), "tensor"),
        P(("groups", "expert", "dp"), "tensor"),
        P(("groups", "expert", "dp"), None),
        P(("groups", "expert", "dp"), None),
        P(("expert", "dp"), "tensor"),
        P(("expert", "dp"), "tensor"),
        P("expert", None, "tensor"),
        P("expert", None, "tensor"),
        P("expert", "tensor", None),
    )
    out_specs = (
        P(("groups", "expert", "dp"), "tensor"),
        P(("groups", "expert", "dp"), "tensor"),
        P(("groups", "expert", "dp"), "tensor"),
        P(("groups", "expert", "dp"), "tensor"),
    )
    return jax.shard_map(local, mesh=mesh, in_specs=in_specs, out_specs=out_specs, check_vma=False)
```

```python
import math

import jax
import jax.numpy as jnp
from jax import lax
from jax.experimental import pallas as pl
from jax.experimental.pallas import tpu as pltpu
from jax.sharding import PartitionSpec as P

OWNERS = ("expert", "dp")
EXPERT = ("expert",)
Z, Y, X, CORE = 0, 1, 2, 3


def tensor_total(partial_sum):
    return lax.psum(partial_sum, "tensor")


def radices(count):
    return (count // 8, 2, 2, 2)


def digit_of(axes, place):
    sizes = radices(math.prod(lax.axis_size(axis) for axis in axes))
    stride = math.prod(sizes[place + 1 :])
    return lax.rem(lax.axis_index(axes) // stride, sizes[place])


def shifted(block, axes, *places, step=1):
    count = math.prod(lax.axis_size(axis) for axis in axes)
    sizes = radices(count)
    pairs = []
    for here in range(count):
        there = here
        for place in places:
            stride = math.prod(sizes[place + 1 :])
            digit = here // stride % sizes[place]
            there += ((digit + step) % sizes[place] - digit) * stride
        pairs.append((here, there))
    return lax.ppermute(block, axes, pairs)


SIDES = ((0, 0), (1, 0), (0, 1), (1, 1))


def device_count(axes):
    return math.prod(lax.axis_size(axis) for axis in axes)


def relative_owners(axes, first, second):
    depth = radices(device_count(axes))[Z]
    owners = []
    for core_step in (0, 1):
        for first_step, second_step in SIDES:
            for z_step in range(depth):
                steps = {Z: depth - z_step, first: first_step, second: second_step, CORE: core_step}
                owner = 0
                for place, size in enumerate(radices(device_count(axes))):
                    digit = lax.rem(digit_of(axes, place) + steps[place], size)
                    owner = owner * size + digit
                owners.append(owner)
    return jnp.stack(owners)


def gather_depth(rows, axes):
    depth = radices(device_count(axes))[Z]
    return lax.concatenate(
        [rows] + [shifted(rows, axes, Z, step=step) for step in range(1, depth)], 0
    )


def gather_chips(own, axes, first, second):
    return (
        own,
        shifted(own, axes, first),
        shifted(own, axes, second),
        shifted(own, axes, first, second),
    )


def gather_chips_by_turns(alongs, axes, first, second):
    own, along_first, along_second = alongs
    half = own.shape[1] // 2
    left = shifted(along_first[:, :half], axes, second)
    right = shifted(along_second[:, half:], axes, first)
    return (own, along_first, along_second, lax.concatenate([left, right], 1))


def core_totals(near, far):
    return [
        near[index].astype(jnp.float32) + shifted(far[index], EXPERT, CORE).astype(jnp.float32)
        for index in (3, 1, 2, 0)
    ]


def depth_total(terms, axes):
    depth = radices(device_count(axes))[Z]
    pieces = jnp.split(terms, depth, axis=0)
    total = pieces[0]
    for step in range(1, depth):
        piece = shifted(pieces[step].astype(jnp.bfloat16), axes, Z, step=depth - step)
        total = total + piece.astype(jnp.float32)
    return total


def chip_totals(across, along_y, along_x, own):
    across = shifted(across.astype(jnp.bfloat16), EXPERT, X, Y)
    along_y = shifted(along_y.astype(jnp.bfloat16), EXPERT, Y)
    along_x = shifted(along_x.astype(jnp.bfloat16), EXPERT, X)
    total = own + across.astype(jnp.float32)
    return total + along_y.astype(jnp.float32) + along_x.astype(jnp.float32)


def across_by_turns(across):
    across = across.astype(jnp.bfloat16)
    half = across.shape[1] // 2
    return shifted(across[:, :half], EXPERT, X), shifted(across[:, half:], EXPERT, Y)


def chip_totals_by_turns(left, right, along_y, along_x, own):
    half = left.shape[1]
    left, right = left.astype(jnp.float32), right.astype(jnp.float32)
    along_y = lax.concatenate([along_y[:, :half] + left, along_y[:, half:]], 1)
    along_x = lax.concatenate([along_x[:, :half], along_x[:, half:] + right], 1)
    own = own + shifted(along_y.astype(jnp.bfloat16), EXPERT, Y).astype(jnp.float32)
    return own + shifted(along_x.astype(jnp.bfloat16), EXPERT, X).astype(jnp.float32)


def placement(rows, first, second):
    owners = relative_owners(OWNERS, first, second)
    targets = (owners[:, None] * rows + jnp.arange(rows, dtype=jnp.int32)[None, :]).reshape(-1)
    columns = jnp.arange(targets.shape[0], dtype=jnp.int32)
    return (targets[:, None] == columns[None, :]).astype(jnp.bfloat16)


def vmem_call(kernel, out_shape, operands, products):
    whole = pl.BlockSpec(memory_space=pltpu.VMEM)
    return pl.pallas_call(
        kernel,
        out_shape=out_shape,
        in_specs=[whole] * len(operands),
        out_specs=(whole,) * len(out_shape),
        compiler_params=pltpu.CompilerParams(vmem_limit_bytes=20 << 20),
        cost_estimate=pl.CostEstimate(
            flops=2 * products,
            bytes_accessed=2 * sum(array.size for array in operands),
            transcendentals=0,
        ),
    )(*operands)


def projection_kernel(*refs):
    tokens, other_tokens, grads, other_grads, *quarters = refs[:8]
    nears, (told, part, other) = refs[8:10], refs[10:]
    width = nears[0].shape[1]
    count = quarters[0].shape[0]
    for near, start, order in zip(nears, (0, width), ((0, 1, 2, 3), (0, 2, 1, 3))):
        for index, quarter in enumerate(order):
            held = slice(index * count, (index + 1) * count)
            near[held, :] = quarters[quarter][:, start : start + width]
    for index, quarter in enumerate(quarters):
        held = slice(index * count, (index + 1) * count)
        if quarter.shape[1] > 2 * width:
            told[held, :] = quarter[:, 2 * width :]
        else:
            told[held, :] = jnp.zeros((count, told.shape[1]), told.dtype)
    half = nears[0].shape[0]
    for target, down, up in ((part, tokens, grads), (other, other_tokens, other_grads)):
        for source, near, start in ((down, nears[0], 0), (up, nears[1], half)):
            product = matmul(source[...], near[...], ((1,), (1,)))
            target[:, start : start + half] = product.astype(target.dtype)


def projected(inputs, quarters):
    row_count, width = inputs[0].shape
    count = 4 * quarters[0].shape[0]
    extra = max(quarters[0].shape[1] - 2 * width, 128)
    dtype = jnp.bfloat16 if lax.axis_size("tensor") == 1 else jnp.float32
    near = jax.ShapeDtypeStruct((count, width), jnp.bfloat16)
    result = jax.ShapeDtypeStruct((row_count, 2 * count), dtype)
    down_near, up_near, told, part, other = vmem_call(
        projection_kernel,
        (near, near, jax.ShapeDtypeStruct((count, extra), jnp.bfloat16), result, result),
        tuple(inputs) + tuple(quarters),
        4 * row_count * width * count,
    )
    other = shifted(tensor_total(other).astype(jnp.bfloat16), OWNERS, CORE)
    part = tensor_total(part).astype(jnp.bfloat16)
    results = []
    for start, (first, second) in ((0, (Y, X)), (count, (X, Y))):
        place = placement(count // 4 // radices(device_count(OWNERS))[Z], first, second)
        columns = slice(start, start + count)
        relative = lax.concatenate([part[:, columns], other[:, columns]], 1)
        results.append(matmul(relative, place).astype(jnp.bfloat16))
    return results, (down_near, up_near), told


def grad_kernel(*refs):
    quad, inputs, (sent, kept) = refs[:4], refs[4:8], refs[8:]
    half = quad[0].shape[1] // 2
    for target, columns in ((sent, slice(half, None)), (kept, slice(0, half))):
        total = None
        for part, block in zip(quad, inputs):
            term = matmul(part[:, columns], block[...], ((0,), (0,)))
            total = term if total is None else total + term
        target[...] = total.astype(target.dtype)


def quad_columns(relative, second):
    mine, along_second, along_core, across = jnp.split(relative, 4, axis=1)
    return (
        mine,
        shifted(along_core, OWNERS, CORE),
        shifted(along_second, OWNERS, second),
        shifted(across, OWNERS, second, CORE),
    )


def quad_grads_of(quad, quad_inputs):
    shape = (quad[0].shape[1] // 2, quad_inputs[0].shape[1])
    return vmem_call(
        grad_kernel,
        (jax.ShapeDtypeStruct(shape, jnp.bfloat16), jax.ShapeDtypeStruct(shape, jnp.float32)),
        quad + tuple(quad_inputs),
        4 * quad[0].size * shape[1],
    )


def matmul(left, right, contract=((1,), (0,))):
    return lax.dot_general(left, right, (contract, ((), ())), preferred_element_type=jnp.float32)


def selected(slot_ref, group, expert, slots, values=None):
    slot = slot_ref[group, expert]
    here = lax.broadcasted_iota(jnp.int32, (slots, slot.shape[1]), 0) == slot
    return jnp.where(here, 1.0 if values is None else values, 0.0).astype(jnp.bfloat16)


def weight_copies(sources, targets, arrived, expert):
    return [
        pltpu.make_async_copy(source.at[expert], target.at[expert], arrived.at[place, expert])
        for place, (source, target) in enumerate(zip(sources, targets))
    ]


def pick_rows(pick, quarter, target, held):
    target[held, :] = matmul(pick, quarter[...]).astype(jnp.bfloat16)


def spread_rows(slot_ref, scale_ref, results, targets):
    experts, groups, slots, _ = results.shape
    for group in range(groups):
        weights = jnp.concatenate(
            [
                selected(
                    slot_ref,
                    group,
                    expert,
                    slots,
                    None if scale_ref is None else scale_ref[group, expert],
                )
                for expert in range(experts)
            ],
            0,
        )
        values = jnp.concatenate([results[expert, group] for expert in range(experts)], 0)
        targets[group][...] = matmul(weights, values, ((0,), (0,))).astype(jnp.bfloat16)


def forward_kernel(*refs):
    slot_ref, scale_ref, *quarters = refs[:6]
    hbm_weights = refs[6:9]
    targets = refs[9:13]
    rows, hidden, results, gate_ref, up_ref, down_ref, arrived = refs[13:]
    experts, groups, slots, _ = results.shape
    width = hidden.shape[1]
    chunk = 256
    for expert in range(experts):
        for copy in weight_copies(hbm_weights, (gate_ref, up_ref, down_ref), arrived, expert):
            copy.start()

    @pl.loop(0, experts)
    def _(expert):
        copies = weight_copies(hbm_weights, (gate_ref, up_ref, down_ref), arrived, expert)
        for group in range(groups):
            held = slice(group * slots, (group + 1) * slots)
            pick_rows(selected(slot_ref, group, expert, slots), quarters[group], rows, held)
        copies[0].wait()
        copies[1].wait()
        for start in range(0, width, chunk):
            columns = slice(start, start + chunk)
            gate_act = matmul(rows[...], gate_ref[expert, :, columns])
            up_act = matmul(rows[...], up_ref[expert, :, columns])
            act = gate_act * jax.nn.sigmoid(gate_act) * up_act
            hidden[:, columns] = act.astype(jnp.bfloat16)
        copies[2].wait()
        result = matmul(hidden[...], down_ref[expert]).astype(jnp.bfloat16)
        for group in range(groups):
            results[expert, group] = result[group * slots : (group + 1) * slots, :]

    spread_rows(slot_ref, scale_ref, results, targets)


def backward_kernel(*refs):
    slot_ref, scale_ref, *quarters = refs[:6]
    quarter_grads = refs[6:10]
    hbm_weights = refs[10:13]
    targets = refs[13:17]
    rows, grads, gate_grads, value_grads, results, gate_ref, up_ref, down_ref, arrived = refs[17:]
    experts, groups, slots, _ = results.shape
    width = gate_grads.shape[1]
    chunk = 256
    for expert in range(experts):
        for copy in weight_copies(hbm_weights, (gate_ref, up_ref, down_ref), arrived, expert):
            copy.start()

    @pl.loop(0, experts)
    def _(expert):
        for group in range(groups):
            held = slice(group * slots, (group + 1) * slots)
            pick_rows(selected(slot_ref, group, expert, slots), quarters[group], rows, held)
            weighed = selected(slot_ref, group, expert, slots, scale_ref[group, expert])
            pick_rows(weighed, quarter_grads[group], grads, held)
        for copy in weight_copies(hbm_weights, (gate_ref, up_ref, down_ref), arrived, expert):
            copy.wait()
        for start in range(0, width, chunk):
            columns = slice(start, start + chunk)
            gate_act = matmul(rows[...], gate_ref[expert, :, columns])
            up_act = matmul(rows[...], up_ref[expert, :, columns])
            hidden_grad = matmul(grads[...], down_ref[expert, columns, :], ((1,), (1,)))
            sigmoid = jax.nn.sigmoid(gate_act)
            scaled = hidden_grad * sigmoid
            gate_grad = scaled * up_act * (1.0 + gate_act * (1.0 - sigmoid))
            gate_grads[:, columns] = gate_grad.astype(jnp.bfloat16)
            value_grads[:, columns] = (scaled * gate_act).astype(jnp.bfloat16)
        result = matmul(gate_grads[...], gate_ref[expert], ((1,), (1,)))
        result = result + matmul(value_grads[...], up_ref[expert], ((1,), (1,)))
        result = result.astype(jnp.bfloat16)
        for group in range(groups):
            results[expert, group] = result[group * slots : (group + 1) * slots, :]

    spread_rows(slot_ref, None, results, targets)


def expert_call(kernel, products, buffers, plan, quarters, weights):
    slots, scales = plan
    experts, latent_width, width = weights[0].shape
    groups, _, _, span = slots.shape
    operands = (slots, scales) + tuple(quarters) + tuple(weights)
    whole = pl.BlockSpec(memory_space=pltpu.VMEM)
    picked = buffers[0].shape[0]
    scratch = list(buffers) + [
        pltpu.VMEM((experts, groups, picked // groups, latent_width), jnp.bfloat16),
        *[pltpu.VMEM(weight.shape, jnp.bfloat16) for weight in weights],
        pltpu.SemaphoreType.DMA((3, experts)),
    ]
    return pl.pallas_call(
        kernel,
        out_shape=(jax.ShapeDtypeStruct((span, latent_width), jnp.bfloat16),) * groups,
        in_specs=[whole] * (len(operands) - 3) + [pl.BlockSpec(memory_space=pl.ANY)] * 3,
        out_specs=(whole,) * groups,
        scratch_shapes=scratch,
        compiler_params=pltpu.CompilerParams(vmem_limit_bytes=36 << 20),
        cost_estimate=pl.CostEstimate(
            flops=2 * products * experts * picked * latent_width * width,
            bytes_accessed=2 * sum(array.size for array in operands),
            transcendentals=experts * picked * width,
        ),
    )(*operands)


def expert_plans(told, local_experts, row_count):
    shards = lax.axis_size("expert")
    depth = radices(shards)[Z]
    told = told.astype(jnp.int32).reshape(shards, 2, -1, row_count)
    capacity = 3 * row_count * told.shape[2] // (2 * local_experts * shards)
    mine = lax.axis_index("expert") * local_experts + jnp.arange(local_experts, dtype=jnp.int32)
    chosen = told[:, 0][:, None] == mine[None, :, None, None]
    fixed = jnp.sum(jnp.where(chosen, told[:, 1][:, None], 0), axis=2)
    member = jnp.any(chosen, axis=2)
    earlier = jnp.arange(row_count)[:, None] < jnp.arange(row_count)[None, :]
    ranking = jnp.einsum(
        "set,tu->seu",
        member.astype(jnp.bfloat16),
        earlier.astype(jnp.bfloat16),
        preferred_element_type=jnp.float32,
    ).astype(jnp.int32)
    offset = (jnp.arange(shards, dtype=jnp.int32) % depth * capacity)[:, None, None]
    slots = jnp.where(member, ranking + offset, -1)
    scales = fixed.astype(jnp.float32) / 256.0

    def by_quarter(values):
        values = values.reshape(2, 4, depth, local_experts, row_count).transpose(0, 1, 3, 2, 4)
        return values.reshape(2, 4, local_experts, 1, depth * row_count)

    slots, scales = by_quarter(slots), by_quarter(scales)
    return [(slots[core], scales[core]) for core in (0, 1)], depth * capacity


def tied(*values):
    return lax.optimization_barrier(values)


def local(
    tokens, out_grad, routes, combine_fixed, down_proj, up_proj, expert_gate, expert_up, expert_down
):
    local_experts, latent_width, width = expert_gate.shape
    row_count = tokens.shape[0]
    rows = down_proj.shape[0]
    told = lax.concatenate([routes.T, combine_fixed.T], 0).astype(jnp.bfloat16)
    ride = lax.axis_size("dp") == 1
    sent = [down_proj, up_proj]
    if ride:
        sent.append(told.reshape(rows, -1))
    next_tokens, next_grads = shifted(tokens, OWNERS, X), shifted(out_grad, OWNERS, Y)
    own = gather_depth(lax.concatenate(sent, 1), OWNERS)
    own, next_tokens, next_grads, later_tokens, later_grads = tied(
        own, next_tokens, next_grads, tokens, out_grad
    )
    quarters = gather_chips(own, OWNERS, Y, X)
    other_tokens = shifted(later_tokens, OWNERS, CORE)
    other_grads = shifted(later_grads, OWNERS, CORE)
    down_place = placement(rows, Y, X)
    up_place = placement(rows, X, Y)
    (latent, mix_grad), (down_near, up_near), told_near = projected(
        (tokens, other_tokens, out_grad, other_grads), quarters
    )
    if not ride:
        told_near = lax.concatenate(
            list(gather_chips(gather_depth(told, EXPERT), EXPERT, Y, X)), 0
        )
    latent, next_tokens, next_grads, told_near = tied(latent, next_tokens, next_grads, told_near)
    latent_own = gather_depth(latent, EXPERT)
    last_tokens = shifted(next_tokens, OWNERS, CORE)
    last_grads = shifted(next_grads, OWNERS, CORE)
    latent_own, last_tokens, last_grads, mix_grad = tied(
        latent_own, last_tokens, last_grads, mix_grad
    )
    near = (latent_own, shifted(latent_own, EXPERT, Y), shifted(latent_own, EXPERT, X))
    mix_own = gather_depth(mix_grad, EXPERT)
    told_far = shifted(told_near, EXPERT, CORE)
    plans, slot_count = expert_plans(
        lax.concatenate([told_near, told_far], 0), local_experts, row_count
    )
    mix_own, near = tied(mix_own, gather_chips_by_turns(near, EXPERT, Y, X))
    far = tuple(shifted(part, EXPERT, CORE) for part in near)
    near_grad = (mix_own, shifted(mix_own, EXPERT, Y), shifted(mix_own, EXPERT, X))

    narrow = pltpu.VMEM((4 * slot_count, latent_width), jnp.bfloat16)
    wide = pltpu.VMEM((4 * slot_count, width), jnp.bfloat16)
    weights = (expert_gate, expert_up, expert_down)
    scratch = (narrow, narrow, wide, wide)
    forward_near = expert_call(forward_kernel, 3, (narrow, wide), plans[0], near, weights)
    forward_near, far, down_near, up_near = tied(forward_near, far, down_near, up_near)
    near_grad = gather_chips_by_turns(near_grad, EXPERT, Y, X)
    forward_far = expert_call(forward_kernel, 3, (narrow, wide), plans[1], far, weights)
    far_grad = tuple(shifted(part, EXPERT, CORE) for part in near_grad)
    down_far = shifted(down_near, OWNERS, CORE)
    up_far = shifted(up_near, OWNERS, CORE)
    across, along_y, along_x, own = core_totals(forward_near, forward_far)
    forward_sums = [part.astype(jnp.bfloat16) for part in (across, along_y, along_x)] + [own]
    far_grad, forward_sums = tied(far_grad, forward_sums)
    backward_far = expert_call(
        backward_kernel, 5, scratch, plans[1], far + tuple(far_grad), weights
    )
    near_grad, backward_far, down_far, up_far = tied(near_grad, backward_far, down_far, up_far)
    backward_near = expert_call(
        backward_kernel, 5, scratch, plans[0], near + tuple(near_grad), weights
    )
    quad_tokens = (tokens, other_tokens, next_tokens, last_tokens)
    quad_grads = (out_grad, other_grads, next_grads, last_grads)

    mixed_sums = chip_totals(*forward_sums)
    backward_across, *backward_sums = core_totals(backward_near, backward_far)
    backward_across = across_by_turns(backward_across)
    mixed_sums, backward_sums = tied(mixed_sums, backward_sums)
    mixed_rows = tensor_total(depth_total(mixed_sums, EXPERT)).astype(jnp.bfloat16)
    mixed_relative = matmul(mixed_rows, up_place, ((1,), (1,))).astype(jnp.bfloat16)
    mixed_relative, backward_across = tied(mixed_relative, backward_across)
    latent_sums = chip_totals_by_turns(*backward_across, *backward_sums)
    quad = quad_columns(mixed_relative, Y)
    quad, latent_sums = tied(quad, latent_sums)
    latent_grad = tensor_total(depth_total(latent_sums, EXPERT)).astype(jnp.bfloat16)
    up_sent, up_kept = quad_grads_of(quad, quad_grads)
    up_sums = up_kept + shifted(up_sent, OWNERS, X).astype(jnp.float32)
    grad_relative = matmul(latent_grad, down_place, ((1,), (1,))).astype(jnp.bfloat16)
    up_sums, mixed_relative, grad_relative = tied(up_sums, mixed_relative, grad_relative)
    quad = quad_columns(grad_relative, X)
    up_grad = depth_total(up_sums, OWNERS)
    down_sent, down_kept = quad_grads_of(quad, quad_tokens)
    down_sums = down_kept + shifted(down_sent, OWNERS, Y).astype(jnp.float32)
    half = latent_width // 2
    layer_out = matmul(mixed_relative[:, :half], up_near)
    layer_out = (layer_out + matmul(mixed_relative[:, half:], up_far)).astype(jnp.bfloat16)
    token_grad = matmul(grad_relative[:, :half], down_near)
    token_grad = (token_grad + matmul(grad_relative[:, half:], down_far)).astype(jnp.bfloat16)
    down_grad = depth_total(down_sums, OWNERS)
    return (layer_out, token_grad, down_grad, up_grad)


def solution(mesh):
    in_specs = (
        P(("groups", "expert", "dp"), "tensor"),
        P(("groups", "expert", "dp"), "tensor"),
        P(("groups", "expert", "dp"), None),
        P(("groups", "expert", "dp"), None),
        P(("expert", "dp"), "tensor"),
        P(("expert", "dp"), "tensor"),
        P("expert", None, "tensor"),
        P("expert", None, "tensor"),
        P("expert", "tensor", None),
    )
    out_specs = (
        P(("groups", "expert", "dp"), "tensor"),
        P(("groups", "expert", "dp"), "tensor"),
        P(("groups", "expert", "dp"), "tensor"),
        P(("groups", "expert", "dp"), "tensor"),
    )
    return jax.shard_map(local, mesh=mesh, in_specs=in_specs, out_specs=out_specs, check_vma=False)
```

```python
import math

import jax
import jax.numpy as jnp
from jax import lax
from jax.experimental import pallas as pl
from jax.experimental.pallas import tpu as pltpu
from jax.sharding import PartitionSpec as P

OWNERS = ("expert", "dp")
EXPERT = ("expert",)
Z, Y, X, CORE = 0, 1, 2, 3


def tensor_total(partial_sum):
    return lax.psum(partial_sum, "tensor")


def radices(count):
    return (count // 8, 2, 2, 2)


def digit_of(axes, place):
    sizes = radices(math.prod(lax.axis_size(axis) for axis in axes))
    stride = math.prod(sizes[place + 1 :])
    return lax.rem(lax.axis_index(axes) // stride, sizes[place])


def shifted(block, axes, *places, step=1):
    count = math.prod(lax.axis_size(axis) for axis in axes)
    sizes = radices(count)
    pairs = []
    for here in range(count):
        there = here
        for place in places:
            stride = math.prod(sizes[place + 1 :])
            digit = here // stride % sizes[place]
            there += ((digit + step) % sizes[place] - digit) * stride
        pairs.append((here, there))
    return lax.ppermute(block, axes, pairs)


SIDES = ((0, 0), (1, 0), (0, 1), (1, 1))


def device_count(axes):
    return math.prod(lax.axis_size(axis) for axis in axes)


def relative_owners(axes, first, second):
    depth = radices(device_count(axes))[Z]
    owners = []
    for core_step in (0, 1):
        for first_step, second_step in SIDES:
            for z_step in range(depth):
                steps = {Z: depth - z_step, first: first_step, second: second_step, CORE: core_step}
                owner = 0
                for place, size in enumerate(radices(device_count(axes))):
                    digit = lax.rem(digit_of(axes, place) + steps[place], size)
                    owner = owner * size + digit
                owners.append(owner)
    return jnp.stack(owners)


def gather_depth(rows, axes):
    depth = radices(device_count(axes))[Z]
    return lax.concatenate(
        [rows] + [shifted(rows, axes, Z, step=step) for step in range(1, depth)], 0
    )


def gather_chips(own, axes, first, second):
    return (
        own,
        shifted(own, axes, first),
        shifted(own, axes, second),
        shifted(own, axes, first, second),
    )


def gather_chips_by_turns(alongs, axes, first, second):
    own, along_first, along_second = alongs
    half = own.shape[1] // 2
    left = shifted(along_first[:, :half], axes, second)
    right = shifted(along_second[:, half:], axes, first)
    return (own, along_first, along_second, lax.concatenate([left, right], 1))


def core_totals(near, far):
    return [
        near[index].astype(jnp.float32) + shifted(far[index], EXPERT, CORE).astype(jnp.float32)
        for index in (3, 1, 2, 0)
    ]


def depth_total(terms, axes):
    depth = radices(device_count(axes))[Z]
    pieces = jnp.split(terms, depth, axis=0)
    total = pieces[0]
    for step in range(1, depth):
        piece = shifted(pieces[step].astype(jnp.bfloat16), axes, Z, step=depth - step)
        total = total + piece.astype(jnp.float32)
    return total


def chip_totals(across, along_y, along_x, own):
    across = shifted(across.astype(jnp.bfloat16), EXPERT, X, Y)
    along_y = shifted(along_y.astype(jnp.bfloat16), EXPERT, Y)
    along_x = shifted(along_x.astype(jnp.bfloat16), EXPERT, X)
    total = own + across.astype(jnp.float32)
    return total + along_y.astype(jnp.float32) + along_x.astype(jnp.float32)


def across_by_turns(across):
    across = across.astype(jnp.bfloat16)
    half = across.shape[1] // 2
    return shifted(across[:, :half], EXPERT, X), shifted(across[:, half:], EXPERT, Y)


def chip_totals_by_turns(left, right, along_y, along_x, own):
    half = left.shape[1]
    left, right = left.astype(jnp.float32), right.astype(jnp.float32)
    along_y = lax.concatenate([along_y[:, :half] + left, along_y[:, half:]], 1)
    along_x = lax.concatenate([along_x[:, :half], along_x[:, half:] + right], 1)
    own = own + shifted(along_y.astype(jnp.bfloat16), EXPERT, Y).astype(jnp.float32)
    return own + shifted(along_x.astype(jnp.bfloat16), EXPERT, X).astype(jnp.float32)


def placement(rows, first, second):
    owners = relative_owners(OWNERS, first, second)
    targets = (owners[:, None] * rows + jnp.arange(rows, dtype=jnp.int32)[None, :]).reshape(-1)
    columns = jnp.arange(targets.shape[0], dtype=jnp.int32)
    return (targets[:, None] == columns[None, :]).astype(jnp.bfloat16)


def vmem_call(kernel, out_shape, operands, products):
    whole = pl.BlockSpec(memory_space=pltpu.VMEM)
    return pl.pallas_call(
        kernel,
        out_shape=out_shape,
        in_specs=[whole] * len(operands),
        out_specs=(whole,) * len(out_shape),
        compiler_params=pltpu.CompilerParams(vmem_limit_bytes=20 << 20),
        cost_estimate=pl.CostEstimate(
            flops=2 * products,
            bytes_accessed=2 * sum(array.size for array in operands),
            transcendentals=0,
        ),
    )(*operands)


def projection_kernel(*refs):
    tokens, other_tokens, grads, other_grads, *quarters = refs[:8]
    nears, (told, part, other) = refs[8:10], refs[10:]
    width = nears[0].shape[1]
    count = quarters[0].shape[0]
    for near, start, order in zip(nears, (0, width), ((0, 1, 2, 3), (0, 2, 1, 3))):
        for index, quarter in enumerate(order):
            held = slice(index * count, (index + 1) * count)
            near[held, :] = quarters[quarter][:, start : start + width]
    for index, quarter in enumerate(quarters):
        held = slice(index * count, (index + 1) * count)
        if quarter.shape[1] > 2 * width:
            told[held, :] = quarter[:, 2 * width :]
        else:
            told[held, :] = jnp.zeros((count, told.shape[1]), told.dtype)
    half = nears[0].shape[0]
    for target, down, up in ((part, tokens, grads), (other, other_tokens, other_grads)):
        for source, near, start in ((down, nears[0], 0), (up, nears[1], half)):
            product = matmul(source[...], near[...], ((1,), (1,)))
            target[:, start : start + half] = product.astype(target.dtype)


def projected(inputs, quarters):
    row_count, width = inputs[0].shape
    count = 4 * quarters[0].shape[0]
    extra = max(quarters[0].shape[1] - 2 * width, 128)
    dtype = jnp.bfloat16 if lax.axis_size("tensor") == 1 else jnp.float32
    near = jax.ShapeDtypeStruct((count, width), jnp.bfloat16)
    result = jax.ShapeDtypeStruct((row_count, 2 * count), dtype)
    down_near, up_near, told, part, other = vmem_call(
        projection_kernel,
        (near, near, jax.ShapeDtypeStruct((count, extra), jnp.bfloat16), result, result),
        tuple(inputs) + tuple(quarters),
        4 * row_count * width * count,
    )
    other = shifted(tensor_total(other).astype(jnp.bfloat16), OWNERS, CORE)
    part = tensor_total(part).astype(jnp.bfloat16)
    results = []
    for start, (first, second) in ((0, (Y, X)), (count, (X, Y))):
        place = placement(count // 4 // radices(device_count(OWNERS))[Z], first, second)
        columns = slice(start, start + count)
        relative = lax.concatenate([part[:, columns], other[:, columns]], 1)
        results.append(matmul(relative, place).astype(jnp.bfloat16))
    return results, (down_near, up_near), told


def grad_kernel(*refs):
    quad, inputs, (sent, kept) = refs[:4], refs[4:8], refs[8:]
    half = quad[0].shape[1] // 2
    for target, columns in ((sent, slice(half, None)), (kept, slice(0, half))):
        total = None
        for part, block in zip(quad, inputs):
            term = matmul(part[:, columns], block[...], ((0,), (0,)))
            total = term if total is None else total + term
        target[...] = total.astype(target.dtype)


def quad_columns(relative, second):
    mine, along_second, along_core, across = jnp.split(relative, 4, axis=1)
    return (
        mine,
        shifted(along_core, OWNERS, CORE),
        shifted(along_second, OWNERS, second),
        shifted(across, OWNERS, second, CORE),
    )


def quad_grads_of(quad, quad_inputs):
    shape = (quad[0].shape[1] // 2, quad_inputs[0].shape[1])
    return vmem_call(
        grad_kernel,
        (jax.ShapeDtypeStruct(shape, jnp.bfloat16), jax.ShapeDtypeStruct(shape, jnp.float32)),
        quad + tuple(quad_inputs),
        4 * quad[0].size * shape[1],
    )


def matmul(left, right, contract=((1,), (0,))):
    return lax.dot_general(left, right, (contract, ((), ())), preferred_element_type=jnp.float32)


def selected(slot_ref, group, expert, slots, values=None):
    slot = slot_ref[group, expert]
    here = lax.broadcasted_iota(jnp.int32, (slots, slot.shape[1]), 0) == slot
    return jnp.where(here, 1.0 if values is None else values, 0.0).astype(jnp.bfloat16)


def weight_copies(sources, targets, arrived, expert):
    return [
        pltpu.make_async_copy(source.at[expert], target.at[expert], arrived.at[place, expert])
        for place, (source, target) in enumerate(zip(sources, targets))
    ]


def pick_rows(pick, quarter, target, held):
    target[held, :] = matmul(pick, quarter[...]).astype(jnp.bfloat16)


def spread_rows(slot_ref, scale_ref, results, targets):
    experts, groups, slots, _ = results.shape
    for group in range(groups):
        weights = jnp.concatenate(
            [
                selected(
                    slot_ref,
                    group,
                    expert,
                    slots,
                    None if scale_ref is None else scale_ref[group, expert],
                )
                for expert in range(experts)
            ],
            0,
        )
        values = jnp.concatenate([results[expert, group] for expert in range(experts)], 0)
        targets[group][...] = matmul(weights, values, ((0,), (0,))).astype(jnp.bfloat16)


def forward_kernel(*refs):
    slot_ref, scale_ref, *refs = refs
    rows, hidden, results, gate_ref, up_ref, down_ref, arrived = refs[-7:]
    experts, groups, slots, _ = results.shape
    quarters, hbm_weights, targets = refs[:groups], refs[groups : groups + 3], refs[groups + 3 : -7]
    width = hidden.shape[1]
    chunk = 256
    for expert in range(experts):
        for copy in weight_copies(hbm_weights, (gate_ref, up_ref, down_ref), arrived, expert):
            copy.start()

    @pl.loop(0, experts)
    def _(expert):
        copies = weight_copies(hbm_weights, (gate_ref, up_ref, down_ref), arrived, expert)
        for group in range(groups):
            held = slice(group * slots, (group + 1) * slots)
            pick_rows(selected(slot_ref, group, expert, slots), quarters[group], rows, held)
        copies[0].wait()
        copies[1].wait()
        for start in range(0, width, chunk):
            columns = slice(start, start + chunk)
            gate_act = matmul(rows[...], gate_ref[expert, :, columns])
            up_act = matmul(rows[...], up_ref[expert, :, columns])
            act = gate_act * jax.nn.sigmoid(gate_act) * up_act
            hidden[:, columns] = act.astype(jnp.bfloat16)
        copies[2].wait()
        result = matmul(hidden[...], down_ref[expert]).astype(jnp.bfloat16)
        for group in range(groups):
            results[expert, group] = result[group * slots : (group + 1) * slots, :]

    spread_rows(slot_ref, scale_ref, results, targets)


def backward_kernel(*refs):
    slot_ref, scale_ref, *refs = refs
    rows, grads, gate_grads, value_grads, results, gate_ref, up_ref, down_ref, arrived = refs[-9:]
    experts, groups, slots, _ = results.shape
    quarters, quarter_grads = refs[:groups], refs[groups : 2 * groups]
    hbm_weights, targets = refs[2 * groups : 2 * groups + 3], refs[2 * groups + 3 : -9]
    width = gate_grads.shape[1]
    chunk = 256
    for expert in range(experts):
        for copy in weight_copies(hbm_weights, (gate_ref, up_ref, down_ref), arrived, expert):
            copy.start()

    @pl.loop(0, experts)
    def _(expert):
        for group in range(groups):
            held = slice(group * slots, (group + 1) * slots)
            pick_rows(selected(slot_ref, group, expert, slots), quarters[group], rows, held)
            weighed = selected(slot_ref, group, expert, slots, scale_ref[group, expert])
            pick_rows(weighed, quarter_grads[group], grads, held)
        for copy in weight_copies(hbm_weights, (gate_ref, up_ref, down_ref), arrived, expert):
            copy.wait()
        for start in range(0, width, chunk):
            columns = slice(start, start + chunk)
            gate_act = matmul(rows[...], gate_ref[expert, :, columns])
            up_act = matmul(rows[...], up_ref[expert, :, columns])
            hidden_grad = matmul(grads[...], down_ref[expert, columns, :], ((1,), (1,)))
            sigmoid = jax.nn.sigmoid(gate_act)
            scaled = hidden_grad * sigmoid
            gate_grad = scaled * up_act * (1.0 + gate_act * (1.0 - sigmoid))
            gate_grads[:, columns] = gate_grad.astype(jnp.bfloat16)
            value_grads[:, columns] = (scaled * gate_act).astype(jnp.bfloat16)
        result = matmul(gate_grads[...], gate_ref[expert], ((1,), (1,)))
        result = result + matmul(value_grads[...], up_ref[expert], ((1,), (1,)))
        result = result.astype(jnp.bfloat16)
        for group in range(groups):
            results[expert, group] = result[group * slots : (group + 1) * slots, :]

    spread_rows(slot_ref, None, results, targets)


def expert_call(kernel, plan, quarters, weights, slot_count, grads=None):
    slots, scales = plan
    experts, latent_width, width = weights[0].shape
    groups, _, _, span = slots.shape
    picked = groups * slot_count
    narrow = pltpu.VMEM((picked, latent_width), jnp.bfloat16)
    wide = pltpu.VMEM((picked, width), jnp.bfloat16)
    products = 3
    scratch = [narrow, wide]
    operands = (slots, scales) + tuple(quarters)
    if grads is not None:
        products = 5
        scratch = [narrow, narrow, wide, wide]
        operands = operands + tuple(grads)
    operands = operands + tuple(weights)
    scratch = scratch + [
        pltpu.VMEM((experts, groups, slot_count, latent_width), jnp.bfloat16),
        *[pltpu.VMEM(weight.shape, jnp.bfloat16) for weight in weights],
        pltpu.SemaphoreType.DMA((3, experts)),
    ]
    whole = pl.BlockSpec(memory_space=pltpu.VMEM)
    return pl.pallas_call(
        kernel,
        out_shape=(jax.ShapeDtypeStruct((span, latent_width), jnp.bfloat16),) * groups,
        in_specs=[whole] * (len(operands) - 3) + [pl.BlockSpec(memory_space=pl.ANY)] * 3,
        out_specs=(whole,) * groups,
        scratch_shapes=scratch,
        compiler_params=pltpu.CompilerParams(vmem_limit_bytes=32 << 20),
        cost_estimate=pl.CostEstimate(
            flops=2 * products * experts * picked * latent_width * width,
            bytes_accessed=2 * sum(array.size for array in operands),
            transcendentals=experts * picked * width,
        ),
    )(*operands)


STAGES = ((0,), (1, 2), (3,))


def stage_sums(kernel, plans, near, far, weights, slot_count, stage, grads=None):
    plan = [
        lax.concatenate(
            [plans[side][part][index : index + 1] for side in (0, 1) for index in stage], 0
        )
        for part in (0, 1)
    ]
    return expert_call(
        kernel,
        plan,
        [side[index] for side in (near, far) for index in stage],
        weights,
        slot_count,
        None if grads is None else [side[index] for side in grads for index in stage],
    )


def by_quarter(stages):
    near, far = [], []
    for sums in stages:
        near.extend(sums[: len(sums) // 2])
        far.extend(sums[len(sums) // 2 :])
    return near, far


def expert_plans(told, local_experts, row_count):
    shards = lax.axis_size("expert")
    depth = radices(shards)[Z]
    told = told.astype(jnp.int32).reshape(shards, 2, -1, row_count)
    capacity = 3 * row_count * told.shape[2] // (2 * local_experts * shards)
    mine = lax.axis_index("expert") * local_experts + jnp.arange(local_experts, dtype=jnp.int32)
    chosen = told[:, 0][:, None] == mine[None, :, None, None]
    fixed = jnp.sum(jnp.where(chosen, told[:, 1][:, None], 0), axis=2)
    member = jnp.any(chosen, axis=2)
    earlier = jnp.arange(row_count)[:, None] < jnp.arange(row_count)[None, :]
    ranking = jnp.einsum(
        "set,tu->seu",
        member.astype(jnp.bfloat16),
        earlier.astype(jnp.bfloat16),
        preferred_element_type=jnp.float32,
    ).astype(jnp.int32)
    offset = (jnp.arange(shards, dtype=jnp.int32) % depth * capacity)[:, None, None]
    slots = jnp.where(member, ranking + offset, -1)
    scales = fixed.astype(jnp.float32) / 256.0

    def in_quarters(values):
        values = values.reshape(2, 4, depth, local_experts, row_count).transpose(0, 1, 3, 2, 4)
        return values.reshape(2, 4, local_experts, 1, depth * row_count)

    slots, scales = in_quarters(slots), in_quarters(scales)
    return [(slots[core], scales[core]) for core in (0, 1)], depth * capacity


def tied(*values):
    return lax.optimization_barrier(values)


def local(
    tokens, out_grad, routes, combine_fixed, down_proj, up_proj, expert_gate, expert_up, expert_down
):
    local_experts, latent_width, width = expert_gate.shape
    row_count = tokens.shape[0]
    rows = down_proj.shape[0]
    told = lax.concatenate([routes.T, combine_fixed.T], 0).astype(jnp.bfloat16)
    ride = lax.axis_size("dp") == 1
    sent = [down_proj, up_proj]
    if ride:
        sent.append(told.reshape(rows, -1))
    own, later_tokens, later_grads = tied(
        gather_depth(lax.concatenate(sent, 1), OWNERS), tokens, out_grad
    )
    quarters = gather_chips(own, OWNERS, Y, X)
    other_tokens = shifted(later_tokens, OWNERS, CORE)
    other_grads = shifted(later_grads, OWNERS, CORE)
    down_place = placement(rows, Y, X)
    up_place = placement(rows, X, Y)
    (latent, mix_grad), (down_near, up_near), told_near = projected(
        (tokens, other_tokens, out_grad, other_grads), quarters
    )
    if not ride:
        told_near = lax.concatenate(
            list(gather_chips(gather_depth(told, EXPERT), EXPERT, Y, X)), 0
        )
    latent, later_tokens, later_grads, told_near = tied(latent, tokens, out_grad, told_near)
    latent_own = gather_depth(latent, EXPERT)
    next_tokens, next_grads = shifted(later_tokens, OWNERS, X), shifted(later_grads, OWNERS, Y)
    latent_own, next_tokens, next_grads, mix_grad = tied(
        latent_own, next_tokens, next_grads, mix_grad
    )
    near = (latent_own, shifted(latent_own, EXPERT, Y), shifted(latent_own, EXPERT, X))
    mix_own = gather_depth(mix_grad, EXPERT)
    told_far = shifted(told_near, EXPERT, CORE)
    plans, slot_count = expert_plans(
        lax.concatenate([told_near, told_far], 0), local_experts, row_count
    )
    mix_own, near = tied(mix_own, near)
    near = gather_chips_by_turns(near, EXPERT, Y, X)
    far = tuple(shifted(part, EXPERT, CORE) for part in near[:3])
    near_grad = (mix_own, shifted(mix_own, EXPERT, Y), shifted(mix_own, EXPERT, X))
    near_grad = gather_chips_by_turns(near_grad, EXPERT, Y, X)

    weights = (expert_gate, expert_up, expert_down)
    shared = (weights, slot_count)
    first_sums = stage_sums(forward_kernel, plans, near, far, *shared, STAGES[0])
    last_near, first_sums = tied(near[3], first_sums)
    far = far + (shifted(last_near, EXPERT, CORE),)
    forward = [first_sums] + [
        stage_sums(forward_kernel, plans, near, far, *shared, stage) for stage in STAGES[1:]
    ]
    forward_near, forward_far = by_quarter(forward)
    forward_far, near_grad, later_near, next_tokens, next_grads = tied(
        forward_far, near_grad, (down_near, up_near), next_tokens, next_grads
    )
    far_grad = tuple(shifted(part, EXPERT, CORE) for part in near_grad)
    down_far = shifted(later_near[0], OWNERS, CORE)
    up_far = shifted(later_near[1], OWNERS, CORE)
    last_tokens = shifted(next_tokens, OWNERS, CORE)
    last_grads = shifted(next_grads, OWNERS, CORE)
    across, along_y, along_x, own = core_totals(forward_near, forward_far)
    forward_sums = [part.astype(jnp.bfloat16) for part in (across, along_y, along_x)] + [own]
    backward_near, backward_far = by_quarter(
        [
            stage_sums(
                backward_kernel, plans, near, far, *shared, stage, (near_grad, far_grad)
            )
            for stage in STAGES
        ]
    )
    quad_tokens = (tokens, other_tokens, next_tokens, last_tokens)
    quad_grads = (out_grad, other_grads, next_grads, last_grads)

    mixed_sums = chip_totals(*forward_sums)
    backward_across, *backward_sums = core_totals(backward_near, backward_far)
    backward_across = across_by_turns(backward_across)
    mixed_sums, backward_across, backward_sums = tied(
        mixed_sums, backward_across, backward_sums
    )
    mixed_rows = tensor_total(depth_total(mixed_sums, EXPERT)).astype(jnp.bfloat16)
    mixed_relative = matmul(mixed_rows, up_place, ((1,), (1,))).astype(jnp.bfloat16)
    latent_sums = chip_totals_by_turns(*backward_across, *backward_sums)
    mixed_relative, latent_sums = tied(mixed_relative, latent_sums)
    quad = quad_columns(mixed_relative, Y)
    latent_grad = tensor_total(depth_total(latent_sums, EXPERT)).astype(jnp.bfloat16)
    up_sent, up_kept = quad_grads_of(quad, quad_grads)
    up_sums = up_kept + shifted(up_sent, OWNERS, X).astype(jnp.float32)
    grad_relative = matmul(latent_grad, down_place, ((1,), (1,))).astype(jnp.bfloat16)
    up_sums, mixed_relative, grad_relative = tied(up_sums, mixed_relative, grad_relative)
    quad = quad_columns(grad_relative, X)
    up_grad = depth_total(up_sums, OWNERS)
    down_sent, down_kept = quad_grads_of(quad, quad_tokens)
    down_sums = down_kept + shifted(down_sent, OWNERS, Y).astype(jnp.float32)
    half = latent_width // 2
    layer_out = matmul(mixed_relative[:, :half], up_near)
    layer_out = (layer_out + matmul(mixed_relative[:, half:], up_far)).astype(jnp.bfloat16)
    token_grad = matmul(grad_relative[:, :half], down_near)
    token_grad = (token_grad + matmul(grad_relative[:, half:], down_far)).astype(jnp.bfloat16)
    down_grad = depth_total(down_sums, OWNERS)
    return (layer_out, token_grad, down_grad, up_grad)


def solution(mesh):
    in_specs = (
        P(("groups", "expert", "dp"), "tensor"),
        P(("groups", "expert", "dp"), "tensor"),
        P(("groups", "expert", "dp"), None),
        P(("groups", "expert", "dp"), None),
        P(("expert", "dp"), "tensor"),
        P(("expert", "dp"), "tensor"),
        P("expert", None, "tensor"),
        P("expert", None, "tensor"),
        P("expert", "tensor", None),
    )
    out_specs = (
        P(("groups", "expert", "dp"), "tensor"),
        P(("groups", "expert", "dp"), "tensor"),
        P(("groups", "expert", "dp"), "tensor"),
        P(("groups", "expert", "dp"), "tensor"),
    )
    return jax.shard_map(local, mesh=mesh, in_specs=in_specs, out_specs=out_specs, check_vma=False)
```

```python
import math

import jax
import jax.numpy as jnp
from jax import lax
from jax.experimental import pallas as pl
from jax.experimental.pallas import tpu as pltpu
from jax.sharding import PartitionSpec as P

OWNERS = ("expert", "dp")
EXPERT = ("expert",)
Z, Y, X, CORE = 0, 1, 2, 3


def tensor_total(partial_sum):
    return lax.psum(partial_sum, "tensor")


def radices(count):
    return (count // 8, 2, 2, 2)


def digit_of(axes, place):
    sizes = radices(math.prod(lax.axis_size(axis) for axis in axes))
    stride = math.prod(sizes[place + 1 :])
    return lax.rem(lax.axis_index(axes) // stride, sizes[place])


def shifted(block, axes, *places, step=1):
    count = math.prod(lax.axis_size(axis) for axis in axes)
    sizes = radices(count)
    pairs = []
    for here in range(count):
        there = here
        for place in places:
            stride = math.prod(sizes[place + 1 :])
            digit = here // stride % sizes[place]
            there += ((digit + step) % sizes[place] - digit) * stride
        pairs.append((here, there))
    return lax.ppermute(block, axes, pairs)


SIDES = ((0, 0), (1, 0), (0, 1), (1, 1))


def device_count(axes):
    return math.prod(lax.axis_size(axis) for axis in axes)


def relative_owners(axes, first, second):
    depth = radices(device_count(axes))[Z]
    owners = []
    for core_step in (0, 1):
        for first_step, second_step in SIDES:
            for z_step in range(depth):
                steps = {Z: depth - z_step, first: first_step, second: second_step, CORE: core_step}
                owner = 0
                for place, size in enumerate(radices(device_count(axes))):
                    digit = lax.rem(digit_of(axes, place) + steps[place], size)
                    owner = owner * size + digit
                owners.append(owner)
    return jnp.stack(owners)


def gather_depth(rows, axes):
    depth = radices(device_count(axes))[Z]
    return lax.concatenate(
        [rows] + [shifted(rows, axes, Z, step=step) for step in range(1, depth)], 0
    )


def gather_chips(own, axes, first, second):
    return (
        own,
        shifted(own, axes, first),
        shifted(own, axes, second),
        shifted(own, axes, first, second),
    )


def gather_chips_by_turns(alongs, axes, first, second):
    own, along_first, along_second = alongs
    half = own.shape[1] // 2
    left = shifted(along_first[:, :half], axes, second)
    right = shifted(along_second[:, half:], axes, first)
    return (own, along_first, along_second, lax.concatenate([left, right], 1))


def core_totals(near, far):
    return [
        near[index].astype(jnp.float32) + shifted(far[index], EXPERT, CORE).astype(jnp.float32)
        for index in (3, 1, 2, 0)
    ]


def depth_total(terms, axes):
    depth = radices(device_count(axes))[Z]
    pieces = jnp.split(terms, depth, axis=0)
    total = pieces[0]
    for step in range(1, depth):
        piece = shifted(pieces[step].astype(jnp.bfloat16), axes, Z, step=depth - step)
        total = total + piece.astype(jnp.float32)
    return total


def chip_totals(across, along_y, along_x, own):
    across = shifted(across.astype(jnp.bfloat16), EXPERT, X, Y)
    along_y = shifted(along_y.astype(jnp.bfloat16), EXPERT, Y)
    along_x = shifted(along_x.astype(jnp.bfloat16), EXPERT, X)
    total = own + across.astype(jnp.float32)
    return total + along_y.astype(jnp.float32) + along_x.astype(jnp.float32)


def across_by_turns(across):
    across = across.astype(jnp.bfloat16)
    half = across.shape[1] // 2
    return shifted(across[:, :half], EXPERT, X), shifted(across[:, half:], EXPERT, Y)


def chip_totals_by_turns(left, right, along_y, along_x, own):
    half = left.shape[1]
    left, right = left.astype(jnp.float32), right.astype(jnp.float32)
    along_y = lax.concatenate([along_y[:, :half] + left, along_y[:, half:]], 1)
    along_x = lax.concatenate([along_x[:, :half], along_x[:, half:] + right], 1)
    own = own + shifted(along_y.astype(jnp.bfloat16), EXPERT, Y).astype(jnp.float32)
    return own + shifted(along_x.astype(jnp.bfloat16), EXPERT, X).astype(jnp.float32)


def placement(rows, first, second):
    owners = relative_owners(OWNERS, first, second)
    targets = (owners[:, None] * rows + jnp.arange(rows, dtype=jnp.int32)[None, :]).reshape(-1)
    columns = jnp.arange(targets.shape[0], dtype=jnp.int32)
    return (targets[:, None] == columns[None, :]).astype(jnp.bfloat16)


def vmem_call(kernel, out_shape, operands, products):
    whole = pl.BlockSpec(memory_space=pltpu.VMEM)
    return pl.pallas_call(
        kernel,
        out_shape=out_shape,
        in_specs=[whole] * len(operands),
        out_specs=(whole,) * len(out_shape),
        compiler_params=pltpu.CompilerParams(vmem_limit_bytes=20 << 20),
        cost_estimate=pl.CostEstimate(
            flops=2 * products,
            bytes_accessed=2 * sum(array.size for array in operands),
            transcendentals=0,
        ),
    )(*operands)


def projection_kernel(*refs):
    tokens, other_tokens, grads, other_grads, *quarters, left, right = refs[:9]
    nears, (told, part, other) = refs[9:11], refs[11:]
    width = nears[0].shape[1]
    count = left.shape[0]
    for near, start, order in zip(nears, (0, width), ((0, 1, 2), (0, 2, 1))):
        for index, quarter in enumerate(order):
            held = slice(index * count, (index + 1) * count)
            near[held, :] = quarters[quarter][:, start : start + width]
    nears[0][3 * count :, :] = left[...]
    nears[1][3 * count :, :] = right[:, :width]
    if right.shape[1] > width:
        for index, quarter in enumerate(quarters):
            told[index * count : (index + 1) * count, :] = quarter[:, 2 * width :]
        told[3 * count :, :] = right[:, width:]
    else:
        told[...] = jnp.zeros_like(told)
    half = nears[0].shape[0]
    for target, down, up in ((part, tokens, grads), (other, other_tokens, other_grads)):
        for source, near, start in ((down, nears[0], 0), (up, nears[1], half)):
            product = matmul(source[...], near[...], ((1,), (1,)))
            target[:, start : start + half] = product.astype(target.dtype)


def projected(inputs, quarters):
    row_count, width = inputs[0].shape
    count = 4 * quarters[0].shape[0]
    extra = max(quarters[0].shape[1] - 2 * width, 128)
    dtype = jnp.bfloat16 if lax.axis_size("tensor") == 1 else jnp.float32
    near = jax.ShapeDtypeStruct((count, width), jnp.bfloat16)
    result = jax.ShapeDtypeStruct((row_count, 2 * count), dtype)
    down_near, up_near, told, part, other = vmem_call(
        projection_kernel,
        (near, near, jax.ShapeDtypeStruct((count, extra), jnp.bfloat16), result, result),
        tuple(inputs) + tuple(quarters),
        4 * row_count * width * count,
    )
    other = shifted(tensor_total(other).astype(jnp.bfloat16), OWNERS, CORE)
    part = tensor_total(part).astype(jnp.bfloat16)
    results = []
    for start, (first, second) in ((0, (Y, X)), (count, (X, Y))):
        place = placement(count // 4 // radices(device_count(OWNERS))[Z], first, second)
        columns = slice(start, start + count)
        relative = lax.concatenate([part[:, columns], other[:, columns]], 1)
        results.append(matmul(relative, place).astype(jnp.bfloat16))
    return results, (down_near, up_near), told


def grad_kernel(*refs):
    quad, inputs, (sent, kept) = refs[:4], refs[4:8], refs[8:]
    half = quad[0].shape[1] // 2
    for target, columns in ((sent, slice(half, None)), (kept, slice(0, half))):
        total = None
        for part, block in zip(quad, inputs):
            term = matmul(part[:, columns], block[...], ((0,), (0,)))
            total = term if total is None else total + term
        target[...] = total.astype(target.dtype)


def quad_columns(relative, second):
    mine, along_second, along_core, across = jnp.split(relative, 4, axis=1)
    return (
        mine,
        shifted(along_core, OWNERS, CORE),
        shifted(along_second, OWNERS, second),
        shifted(across, OWNERS, second, CORE),
    )


def quad_grads_of(quad, quad_inputs):
    shape = (quad[0].shape[1] // 2, quad_inputs[0].shape[1])
    return vmem_call(
        grad_kernel,
        (jax.ShapeDtypeStruct(shape, jnp.bfloat16), jax.ShapeDtypeStruct(shape, jnp.float32)),
        quad + tuple(quad_inputs),
        4 * quad[0].size * shape[1],
    )


def matmul(left, right, contract=((1,), (0,))):
    return lax.dot_general(left, right, (contract, ((), ())), preferred_element_type=jnp.float32)


def selected(slot_ref, group, expert, slots, values=None):
    slot = slot_ref[group, expert]
    here = lax.broadcasted_iota(jnp.int32, (slots, slot.shape[1]), 0) == slot
    return jnp.where(here, 1.0 if values is None else values, 0.0).astype(jnp.bfloat16)


def weight_copies(sources, targets, arrived, expert):
    return [
        pltpu.make_async_copy(source.at[expert], target.at[expert], arrived.at[place, expert])
        for place, (source, target) in enumerate(zip(sources, targets))
    ]


def pick_rows(pick, quarter, target, held):
    target[held, :] = matmul(pick, quarter[...]).astype(jnp.bfloat16)


def spread_rows(slot_ref, scale_ref, results, targets):
    experts, groups, slots, _ = results.shape
    for group in range(groups):
        weights = jnp.concatenate(
            [
                selected(
                    slot_ref,
                    group,
                    expert,
                    slots,
                    None if scale_ref is None else scale_ref[group, expert],
                )
                for expert in range(experts)
            ],
            0,
        )
        values = jnp.concatenate([results[expert, group] for expert in range(experts)], 0)
        targets[group][...] = matmul(weights, values, ((0,), (0,))).astype(jnp.bfloat16)


def forward_kernel(*refs):
    slot_ref, scale_ref, *refs = refs
    rows, hidden, results, gate_ref, up_ref, down_ref, arrived = refs[-7:]
    experts, groups, slots, _ = results.shape
    quarters, hbm_weights, targets = refs[:groups], refs[groups : groups + 3], refs[groups + 3 : -7]
    width = hidden.shape[1]
    chunk = 256
    for expert in range(experts):
        for copy in weight_copies(hbm_weights, (gate_ref, up_ref, down_ref), arrived, expert):
            copy.start()

    @pl.loop(0, experts)
    def _(expert):
        copies = weight_copies(hbm_weights, (gate_ref, up_ref, down_ref), arrived, expert)
        for group in range(groups):
            held = slice(group * slots, (group + 1) * slots)
            pick_rows(selected(slot_ref, group, expert, slots), quarters[group], rows, held)
        copies[0].wait()
        copies[1].wait()
        for start in range(0, width, chunk):
            columns = slice(start, start + chunk)
            gate_act = matmul(rows[...], gate_ref[expert, :, columns])
            up_act = matmul(rows[...], up_ref[expert, :, columns])
            act = gate_act * jax.nn.sigmoid(gate_act) * up_act
            hidden[:, columns] = act.astype(jnp.bfloat16)
        copies[2].wait()
        result = matmul(hidden[...], down_ref[expert]).astype(jnp.bfloat16)
        for group in range(groups):
            results[expert, group] = result[group * slots : (group + 1) * slots, :]

    spread_rows(slot_ref, scale_ref, results, targets)


def backward_kernel(*refs):
    slot_ref, scale_ref, *refs = refs
    rows, grads, gate_grads, value_grads, results, gate_ref, up_ref, down_ref, arrived = refs[-9:]
    experts, groups, slots, _ = results.shape
    quarters, quarter_grads = refs[:groups], refs[groups : 2 * groups]
    hbm_weights, targets = refs[2 * groups : 2 * groups + 3], refs[2 * groups + 3 : -9]
    width = gate_grads.shape[1]
    chunk = 256
    for expert in range(experts):
        for copy in weight_copies(hbm_weights, (gate_ref, up_ref, down_ref), arrived, expert):
            copy.start()

    @pl.loop(0, experts)
    def _(expert):
        for group in range(groups):
            held = slice(group * slots, (group + 1) * slots)
            pick_rows(selected(slot_ref, group, expert, slots), quarters[group], rows, held)
            weighed = selected(slot_ref, group, expert, slots, scale_ref[group, expert])
            pick_rows(weighed, quarter_grads[group], grads, held)
        for copy in weight_copies(hbm_weights, (gate_ref, up_ref, down_ref), arrived, expert):
            copy.wait()
        for start in range(0, width, chunk):
            columns = slice(start, start + chunk)
            gate_act = matmul(rows[...], gate_ref[expert, :, columns])
            up_act = matmul(rows[...], up_ref[expert, :, columns])
            hidden_grad = matmul(grads[...], down_ref[expert, columns, :], ((1,), (1,)))
            sigmoid = jax.nn.sigmoid(gate_act)
            scaled = hidden_grad * sigmoid
            gate_grad = scaled * up_act * (1.0 + gate_act * (1.0 - sigmoid))
            gate_grads[:, columns] = gate_grad.astype(jnp.bfloat16)
            value_grads[:, columns] = (scaled * gate_act).astype(jnp.bfloat16)
        result = matmul(gate_grads[...], gate_ref[expert], ((1,), (1,)))
        result = result + matmul(value_grads[...], up_ref[expert], ((1,), (1,)))
        result = result.astype(jnp.bfloat16)
        for group in range(groups):
            results[expert, group] = result[group * slots : (group + 1) * slots, :]

    spread_rows(slot_ref, None, results, targets)


def expert_call(kernel, plan, quarters, weights, slot_count, grads=None):
    slots, scales = plan
    experts, latent_width, width = weights[0].shape
    groups, _, _, span = slots.shape
    picked = groups * slot_count
    narrow = pltpu.VMEM((picked, latent_width), jnp.bfloat16)
    wide = pltpu.VMEM((picked, width), jnp.bfloat16)
    products = 3
    scratch = [narrow, wide]
    operands = (slots, scales) + tuple(quarters)
    if grads is not None:
        products = 5
        scratch = [narrow, narrow, wide, wide]
        operands = operands + tuple(grads)
    operands = operands + tuple(weights)
    scratch = scratch + [
        pltpu.VMEM((experts, groups, slot_count, latent_width), jnp.bfloat16),
        *[pltpu.VMEM(weight.shape, jnp.bfloat16) for weight in weights],
        pltpu.SemaphoreType.DMA((3, experts)),
    ]
    whole = pl.BlockSpec(memory_space=pltpu.VMEM)
    return pl.pallas_call(
        kernel,
        out_shape=(jax.ShapeDtypeStruct((span, latent_width), jnp.bfloat16),) * groups,
        in_specs=[whole] * (len(operands) - 3) + [pl.BlockSpec(memory_space=pl.ANY)] * 3,
        out_specs=(whole,) * groups,
        scratch_shapes=scratch,
        compiler_params=pltpu.CompilerParams(vmem_limit_bytes=32 << 20),
        cost_estimate=pl.CostEstimate(
            flops=2 * products * experts * picked * latent_width * width,
            bytes_accessed=2 * sum(array.size for array in operands),
            transcendentals=experts * picked * width,
        ),
    )(*operands)


STAGES = ((0,), (1, 2), (3,))


def stage_sums(kernel, plans, near, far, weights, slot_count, stage, grads=None):
    plan = [
        lax.concatenate(
            [plans[side][part][index : index + 1] for side in (0, 1) for index in stage], 0
        )
        for part in (0, 1)
    ]
    return expert_call(
        kernel,
        plan,
        [side[index] for side in (near, far) for index in stage],
        weights,
        slot_count,
        None if grads is None else [side[index] for side in grads for index in stage],
    )


def by_quarter(stages):
    near, far = [], []
    for sums in stages:
        near.extend(sums[: len(sums) // 2])
        far.extend(sums[len(sums) // 2 :])
    return near, far


def expert_plans(told, local_experts, row_count):
    shards = lax.axis_size("expert")
    depth = radices(shards)[Z]
    told = told.astype(jnp.int32).reshape(shards, 2, -1, row_count)
    capacity = 3 * row_count * told.shape[2] // (2 * local_experts * shards)
    mine = lax.axis_index("expert") * local_experts + jnp.arange(local_experts, dtype=jnp.int32)
    chosen = told[:, 0][:, None] == mine[None, :, None, None]
    fixed = jnp.sum(jnp.where(chosen, told[:, 1][:, None], 0), axis=2)
    member = jnp.any(chosen, axis=2)
    earlier = jnp.arange(row_count)[:, None] < jnp.arange(row_count)[None, :]
    ranking = jnp.einsum(
        "set,tu->seu",
        member.astype(jnp.bfloat16),
        earlier.astype(jnp.bfloat16),
        preferred_element_type=jnp.float32,
    ).astype(jnp.int32)
    offset = (jnp.arange(shards, dtype=jnp.int32) % depth * capacity)[:, None, None]
    slots = jnp.where(member, ranking + offset, -1)
    scales = fixed.astype(jnp.float32) / 256.0

    def in_quarters(values):
        values = values.reshape(2, 4, depth, local_experts, row_count).transpose(0, 1, 3, 2, 4)
        return values.reshape(2, 4, local_experts, 1, depth * row_count)

    slots, scales = in_quarters(slots), in_quarters(scales)
    return [(slots[core], scales[core]) for core in (0, 1)], depth * capacity


def tied(*values):
    return lax.optimization_barrier(values)


def local(
    tokens, out_grad, routes, combine_fixed, down_proj, up_proj, expert_gate, expert_up, expert_down
):
    local_experts, latent_width, width = expert_gate.shape
    row_count = tokens.shape[0]
    rows = down_proj.shape[0]
    told = lax.concatenate([routes.T, combine_fixed.T], 0).astype(jnp.bfloat16)
    ride = lax.axis_size("dp") == 1
    sent = [down_proj, up_proj]
    if ride:
        sent.append(told.reshape(rows, -1))
    own, later_tokens, later_grads = tied(
        gather_depth(lax.concatenate(sent, 1), OWNERS), tokens, out_grad
    )
    along_y, along_x = shifted(own, OWNERS, Y), shifted(own, OWNERS, X)
    quarters = (
        own,
        along_y,
        along_x,
        shifted(along_y[:, : tokens.shape[1]], OWNERS, X),
        shifted(along_x[:, tokens.shape[1] :], OWNERS, Y),
    )
    other_tokens = shifted(later_tokens, OWNERS, CORE)
    other_grads = shifted(later_grads, OWNERS, CORE)
    down_place = placement(rows, Y, X)
    up_place = placement(rows, X, Y)
    (latent, mix_grad), (down_near, up_near), told_near = projected(
        (tokens, other_tokens, out_grad, other_grads), quarters
    )
    if not ride:
        told_near = lax.concatenate(
            list(gather_chips(gather_depth(told, EXPERT), EXPERT, Y, X)), 0
        )
    latent, later_tokens, later_grads, told_near = tied(latent, tokens, out_grad, told_near)
    latent_own = gather_depth(latent, EXPERT)
    next_tokens, next_grads = shifted(later_tokens, OWNERS, X), shifted(later_grads, OWNERS, Y)
    latent_own, mix_grad = tied(latent_own, mix_grad)
    near = (latent_own, shifted(latent_own, EXPERT, Y), shifted(latent_own, EXPERT, X))
    mix_own = gather_depth(mix_grad, EXPERT)
    told_far = shifted(told_near, EXPERT, CORE)
    plans, slot_count = expert_plans(
        lax.concatenate([told_near, told_far], 0), local_experts, row_count
    )
    mix_own, near, next_tokens, next_grads = tied(mix_own, near, next_tokens, next_grads)
    near = gather_chips_by_turns(near, EXPERT, Y, X)
    far = tuple(shifted(part, EXPERT, CORE) for part in near[:3])
    near_grad = (mix_own, shifted(mix_own, EXPERT, Y), shifted(mix_own, EXPERT, X))
    near_grad = gather_chips_by_turns(near_grad, EXPERT, Y, X)

    weights = (expert_gate, expert_up, expert_down)
    shared = (weights, slot_count)
    first_sums = stage_sums(forward_kernel, plans, near, far, *shared, STAGES[0])
    last_near, first_sums = tied(near[3], first_sums)
    far = far + (shifted(last_near, EXPERT, CORE),)
    forward = [first_sums] + [
        stage_sums(forward_kernel, plans, near, far, *shared, stage) for stage in STAGES[1:]
    ]
    forward_near, forward_far = by_quarter(forward)
    far_grad = tuple(shifted(part, EXPERT, CORE) for part in near_grad)
    across, along_y, along_x, own = core_totals(forward_near, forward_far)
    forward_sums = [part.astype(jnp.bfloat16) for part in (across, along_y, along_x)] + [own]
    mix_own, *forward_alongs = tied(near_grad[0], *forward_sums[1:])
    near_grad = (mix_own,) + tuple(near_grad[1:])
    backward = [
        stage_sums(
            backward_kernel, plans, near, far, *shared, STAGES[0], (near_grad, far_grad)
        )
    ]
    along_grads, forward_across = tied(near_grad[1:], forward_sums[0])
    forward_sums = [forward_across] + forward_alongs
    near_grad = near_grad[:1] + tuple(along_grads)
    backward += [
        stage_sums(backward_kernel, plans, near, far, *shared, stage, (near_grad, far_grad))
        for stage in STAGES[1:]
    ]
    backward[0], next_tokens, next_grads, down_near, up_near = tied(
        backward[0], next_tokens, next_grads, down_near, up_near
    )
    backward_near, backward_far = by_quarter(backward)
    last_tokens, last_grads, down_far, up_far = [
        shifted(array, OWNERS, CORE) for array in (next_tokens, next_grads, down_near, up_near)
    ]
    quad_tokens = (tokens, other_tokens, next_tokens, last_tokens)
    quad_grads = (out_grad, other_grads, next_grads, last_grads)

    mixed_sums = chip_totals(*forward_sums)
    backward_across, *backward_sums = core_totals(backward_near, backward_far)
    backward_across = across_by_turns(backward_across)
    mixed_sums, backward_across, backward_sums = tied(
        mixed_sums, backward_across, backward_sums
    )
    mixed_rows = tensor_total(depth_total(mixed_sums, EXPERT)).astype(jnp.bfloat16)
    mixed_relative = matmul(mixed_rows, up_place, ((1,), (1,))).astype(jnp.bfloat16)
    latent_sums = chip_totals_by_turns(*backward_across, *backward_sums)
    mixed_relative, latent_sums = tied(mixed_relative, latent_sums)
    quad = quad_columns(mixed_relative, Y)
    latent_grad = tensor_total(depth_total(latent_sums, EXPERT)).astype(jnp.bfloat16)
    up_sent, up_kept = quad_grads_of(quad, quad_grads)
    up_sums = up_kept + shifted(up_sent, OWNERS, X).astype(jnp.float32)
    grad_relative = matmul(latent_grad, down_place, ((1,), (1,))).astype(jnp.bfloat16)
    quad = quad_columns(grad_relative, X)
    down_sent, down_kept = quad_grads_of(quad, quad_tokens)
    up_sums, mixed_relative, grad_relative, down_sent = tied(
        up_sums, mixed_relative, grad_relative, down_sent
    )
    up_grad = depth_total(up_sums, OWNERS)
    down_sums = down_kept + shifted(down_sent, OWNERS, Y).astype(jnp.float32)
    half = latent_width // 2
    layer_out = matmul(mixed_relative[:, :half], up_near)
    layer_out = (layer_out + matmul(mixed_relative[:, half:], up_far)).astype(jnp.bfloat16)
    token_grad = matmul(grad_relative[:, :half], down_near)
    token_grad = (token_grad + matmul(grad_relative[:, half:], down_far)).astype(jnp.bfloat16)
    down_grad = depth_total(down_sums, OWNERS)
    return (layer_out, token_grad, down_grad, up_grad)


def solution(mesh):
    in_specs = (
        P(("groups", "expert", "dp"), "tensor"),
        P(("groups", "expert", "dp"), "tensor"),
        P(("groups", "expert", "dp"), None),
        P(("groups", "expert", "dp"), None),
        P(("expert", "dp"), "tensor"),
        P(("expert", "dp"), "tensor"),
        P("expert", None, "tensor"),
        P("expert", None, "tensor"),
        P("expert", "tensor", None),
    )
    out_specs = (
        P(("groups", "expert", "dp"), "tensor"),
        P(("groups", "expert", "dp"), "tensor"),
        P(("groups", "expert", "dp"), "tensor"),
        P(("groups", "expert", "dp"), "tensor"),
    )
    return jax.shard_map(local, mesh=mesh, in_specs=in_specs, out_specs=out_specs, check_vma=False)
```

```python
import math

import jax
import jax.numpy as jnp
from jax import lax
from jax.experimental import pallas as pl
from jax.experimental.pallas import tpu as pltpu
from jax.sharding import PartitionSpec as P

OWNERS = ("expert", "dp")
EXPERT = ("expert",)
Z, Y, X, CORE = 0, 1, 2, 3


def tensor_total(partial_sum):
    return lax.psum(partial_sum, "tensor")


def radices(count):
    return (count // 8, 2, 2, 2)


def digit_of(axes, place):
    sizes = radices(math.prod(lax.axis_size(axis) for axis in axes))
    stride = math.prod(sizes[place + 1 :])
    return lax.rem(lax.axis_index(axes) // stride, sizes[place])


def shifted(block, axes, *places, step=1):
    count = math.prod(lax.axis_size(axis) for axis in axes)
    sizes = radices(count)
    pairs = []
    for here in range(count):
        there = here
        for place in places:
            stride = math.prod(sizes[place + 1 :])
            digit = here // stride % sizes[place]
            there += ((digit + step) % sizes[place] - digit) * stride
        pairs.append((here, there))
    return lax.ppermute(block, axes, pairs)


SIDES = ((0, 0), (1, 0), (0, 1), (1, 1))


def device_count(axes):
    return math.prod(lax.axis_size(axis) for axis in axes)


def relative_owners(axes, first, second):
    depth = radices(device_count(axes))[Z]
    owners = []
    for core_step in (0, 1):
        for first_step, second_step in SIDES:
            for z_step in range(depth):
                steps = {Z: depth - z_step, first: first_step, second: second_step, CORE: core_step}
                owner = 0
                for place, size in enumerate(radices(device_count(axes))):
                    digit = lax.rem(digit_of(axes, place) + steps[place], size)
                    owner = owner * size + digit
                owners.append(owner)
    return jnp.stack(owners)


def gather_depth(rows, axes):
    depth = radices(device_count(axes))[Z]
    return lax.concatenate(
        [rows] + [shifted(rows, axes, Z, step=step) for step in range(1, depth)], 0
    )


def gather_chips(own, axes, first, second):
    return (
        own,
        shifted(own, axes, first),
        shifted(own, axes, second),
        shifted(own, axes, first, second),
    )


def gather_chips_by_turns(alongs, axes, first, second):
    own, along_first, along_second = alongs
    half = own.shape[1] // 2
    left = shifted(along_first[:, :half], axes, second)
    right = shifted(along_second[:, half:], axes, first)
    return (own, along_first, along_second, lax.concatenate([left, right], 1))


def core_totals(near, far):
    return [
        near[index].astype(jnp.float32) + shifted(far[index], EXPERT, CORE).astype(jnp.float32)
        for index in (3, 1, 2, 0)
    ]


def depth_total(terms, axes):
    depth = radices(device_count(axes))[Z]
    pieces = jnp.split(terms, depth, axis=0)
    total = pieces[0]
    for step in range(1, depth):
        piece = shifted(pieces[step].astype(jnp.bfloat16), axes, Z, step=depth - step)
        total = total + piece.astype(jnp.float32)
    return total


def chip_totals(across, along_y, along_x, own):
    across = shifted(across.astype(jnp.bfloat16), EXPERT, X, Y)
    along_y = shifted(along_y.astype(jnp.bfloat16), EXPERT, Y)
    along_x = shifted(along_x.astype(jnp.bfloat16), EXPERT, X)
    total = own + across.astype(jnp.float32)
    return total + along_y.astype(jnp.float32) + along_x.astype(jnp.float32)


def across_by_turns(across):
    across = across.astype(jnp.bfloat16)
    half = across.shape[1] // 2
    return shifted(across[:, :half], EXPERT, X), shifted(across[:, half:], EXPERT, Y)


def chip_totals_by_turns(left, right, along_y, along_x, own):
    half = left.shape[1]
    left, right = left.astype(jnp.float32), right.astype(jnp.float32)
    along_y = lax.concatenate([along_y[:, :half] + left, along_y[:, half:]], 1)
    along_x = lax.concatenate([along_x[:, :half], along_x[:, half:] + right], 1)
    own = own + shifted(along_y.astype(jnp.bfloat16), EXPERT, Y).astype(jnp.float32)
    return own + shifted(along_x.astype(jnp.bfloat16), EXPERT, X).astype(jnp.float32)


def placement(rows, first, second):
    owners = relative_owners(OWNERS, first, second)
    targets = (owners[:, None] * rows + jnp.arange(rows, dtype=jnp.int32)[None, :]).reshape(-1)
    columns = jnp.arange(targets.shape[0], dtype=jnp.int32)
    return (targets[:, None] == columns[None, :]).astype(jnp.bfloat16)


def vmem_call(kernel, out_shape, operands, products):
    whole = pl.BlockSpec(memory_space=pltpu.VMEM)
    return pl.pallas_call(
        kernel,
        out_shape=out_shape,
        in_specs=[whole] * len(operands),
        out_specs=(whole,) * len(out_shape),
        compiler_params=pltpu.CompilerParams(vmem_limit_bytes=20 << 20),
        cost_estimate=pl.CostEstimate(
            flops=2 * products,
            bytes_accessed=2 * sum(array.size for array in operands),
            transcendentals=0,
        ),
    )(*operands)


def projection_kernel(*refs):
    tokens, other_tokens, grads, other_grads, *quarters, left, right = refs[:9]
    nears, (told, part, other) = refs[9:11], refs[11:]
    width = nears[0].shape[1]
    count = left.shape[0]
    for near, start, order in zip(nears, (0, width), ((0, 1, 2), (0, 2, 1))):
        for index, quarter in enumerate(order):
            held = slice(index * count, (index + 1) * count)
            near[held, :] = quarters[quarter][:, start : start + width]
    nears[0][3 * count :, :] = left[...]
    nears[1][3 * count :, :] = right[:, :width]
    if right.shape[1] > width:
        for index, quarter in enumerate(quarters):
            told[index * count : (index + 1) * count, :] = quarter[:, 2 * width :]
        told[3 * count :, :] = right[:, width:]
    else:
        told[...] = jnp.zeros_like(told)
    half = nears[0].shape[0]
    for target, down, up in ((part, tokens, grads), (other, other_tokens, other_grads)):
        for source, near, start in ((down, nears[0], 0), (up, nears[1], half)):
            product = matmul(source[...], near[...], ((1,), (1,)))
            target[:, start : start + half] = product.astype(target.dtype)


def projected(inputs, quarters):
    row_count, width = inputs[0].shape
    count = 4 * quarters[0].shape[0]
    extra = max(quarters[0].shape[1] - 2 * width, 128)
    dtype = jnp.bfloat16 if lax.axis_size("tensor") == 1 else jnp.float32
    near = jax.ShapeDtypeStruct((count, width), jnp.bfloat16)
    result = jax.ShapeDtypeStruct((row_count, 2 * count), dtype)
    down_near, up_near, told, part, other = vmem_call(
        projection_kernel,
        (near, near, jax.ShapeDtypeStruct((count, extra), jnp.bfloat16), result, result),
        tuple(inputs) + tuple(quarters),
        4 * row_count * width * count,
    )
    other = shifted(tensor_total(other).astype(jnp.bfloat16), OWNERS, CORE)
    part = tensor_total(part).astype(jnp.bfloat16)
    results = []
    for start, (first, second) in ((0, (Y, X)), (count, (X, Y))):
        place = placement(count // 4 // radices(device_count(OWNERS))[Z], first, second)
        columns = slice(start, start + count)
        relative = lax.concatenate([part[:, columns], other[:, columns]], 1)
        results.append(matmul(relative, place).astype(jnp.bfloat16))
    return results, (down_near, up_near), told


def grad_kernel(*refs):
    quad, inputs, (sent, kept) = refs[:4], refs[4:8], refs[8:]
    half = quad[0].shape[1] // 2
    for target, columns in ((sent, slice(half, None)), (kept, slice(0, half))):
        total = None
        for part, block in zip(quad, inputs):
            term = matmul(part[:, columns], block[...], ((0,), (0,)))
            total = term if total is None else total + term
        target[...] = total.astype(target.dtype)


def quad_columns(relative, second):
    mine, along_second, along_core, across = jnp.split(relative, 4, axis=1)
    return (
        mine,
        shifted(along_core, OWNERS, CORE),
        shifted(along_second, OWNERS, second),
        shifted(across, OWNERS, second, CORE),
    )


def quad_grads_of(quad, quad_inputs):
    shape = (quad[0].shape[1] // 2, quad_inputs[0].shape[1])
    return vmem_call(
        grad_kernel,
        (jax.ShapeDtypeStruct(shape, jnp.bfloat16), jax.ShapeDtypeStruct(shape, jnp.float32)),
        quad + tuple(quad_inputs),
        4 * quad[0].size * shape[1],
    )


def matmul(left, right, contract=((1,), (0,))):
    return lax.dot_general(left, right, (contract, ((), ())), preferred_element_type=jnp.float32)


def selected(slot_ref, group, expert, slots, values=None):
    slot = slot_ref[group, expert]
    here = lax.broadcasted_iota(jnp.int32, (slots, slot.shape[1]), 0) == slot
    return jnp.where(here, 1.0 if values is None else values, 0.0).astype(jnp.bfloat16)


def weight_copies(sources, targets, arrived, expert):
    return [
        pltpu.make_async_copy(source.at[expert], target.at[expert], arrived.at[place, expert])
        for place, (source, target) in enumerate(zip(sources, targets))
    ]


def pick_rows(pick, quarter, target, held):
    target[held, :] = matmul(pick, quarter[...]).astype(jnp.bfloat16)


def spread_rows(slot_ref, scale_ref, results, targets):
    experts, groups, slots, _ = results.shape
    for group in range(groups):
        weights = jnp.concatenate(
            [
                selected(
                    slot_ref,
                    group,
                    expert,
                    slots,
                    None if scale_ref is None else scale_ref[group, expert],
                )
                for expert in range(experts)
            ],
            0,
        )
        values = jnp.concatenate([results[expert, group] for expert in range(experts)], 0)
        targets[group][...] = matmul(weights, values, ((0,), (0,))).astype(jnp.bfloat16)


def forward_kernel(*refs):
    slot_ref, scale_ref, *refs = refs
    rows, hidden, results, gate_ref, up_ref, down_ref, arrived = refs[-7:]
    experts, groups, slots, _ = results.shape
    quarters, hbm_weights, targets = refs[:groups], refs[groups : groups + 3], refs[groups + 3 : -7]
    width = hidden.shape[1]
    chunk = 256
    for expert in range(experts):
        for copy in weight_copies(hbm_weights, (gate_ref, up_ref, down_ref), arrived, expert):
            copy.start()

    @pl.loop(0, experts)
    def _(expert):
        copies = weight_copies(hbm_weights, (gate_ref, up_ref, down_ref), arrived, expert)
        for group in range(groups):
            held = slice(group * slots, (group + 1) * slots)
            pick_rows(selected(slot_ref, group, expert, slots), quarters[group], rows, held)
        copies[0].wait()
        copies[1].wait()
        for start in range(0, width, chunk):
            columns = slice(start, start + chunk)
            gate_act = matmul(rows[...], gate_ref[expert, :, columns])
            up_act = matmul(rows[...], up_ref[expert, :, columns])
            act = gate_act * jax.nn.sigmoid(gate_act) * up_act
            hidden[:, columns] = act.astype(jnp.bfloat16)
        copies[2].wait()
        result = matmul(hidden[...], down_ref[expert]).astype(jnp.bfloat16)
        for group in range(groups):
            results[expert, group] = result[group * slots : (group + 1) * slots, :]

    spread_rows(slot_ref, scale_ref, results, targets)


def backward_kernel(*refs):
    slot_ref, scale_ref, *refs = refs
    rows, grads, gate_grads, value_grads, results, gate_ref, up_ref, down_ref, arrived = refs[-9:]
    experts, groups, slots, _ = results.shape
    quarters, quarter_grads = refs[:groups], refs[groups : 2 * groups]
    hbm_weights, targets = refs[2 * groups : 2 * groups + 3], refs[2 * groups + 3 : -9]
    width = gate_grads.shape[1]
    chunk = 256
    for expert in range(experts):
        for copy in weight_copies(hbm_weights, (gate_ref, up_ref, down_ref), arrived, expert):
            copy.start()

    @pl.loop(0, experts)
    def _(expert):
        for group in range(groups):
            held = slice(group * slots, (group + 1) * slots)
            pick_rows(selected(slot_ref, group, expert, slots), quarters[group], rows, held)
            weighed = selected(slot_ref, group, expert, slots, scale_ref[group, expert])
            pick_rows(weighed, quarter_grads[group], grads, held)
        for copy in weight_copies(hbm_weights, (gate_ref, up_ref, down_ref), arrived, expert):
            copy.wait()
        for start in range(0, width, chunk):
            columns = slice(start, start + chunk)
            gate_act = matmul(rows[...], gate_ref[expert, :, columns])
            up_act = matmul(rows[...], up_ref[expert, :, columns])
            hidden_grad = matmul(grads[...], down_ref[expert, columns, :], ((1,), (1,)))
            sigmoid = jax.nn.sigmoid(gate_act)
            scaled = hidden_grad * sigmoid
            gate_grad = scaled * up_act * (1.0 + gate_act * (1.0 - sigmoid))
            gate_grads[:, columns] = gate_grad.astype(jnp.bfloat16)
            value_grads[:, columns] = (scaled * gate_act).astype(jnp.bfloat16)
        result = matmul(gate_grads[...], gate_ref[expert], ((1,), (1,)))
        result = result + matmul(value_grads[...], up_ref[expert], ((1,), (1,)))
        result = result.astype(jnp.bfloat16)
        for group in range(groups):
            results[expert, group] = result[group * slots : (group + 1) * slots, :]

    spread_rows(slot_ref, None, results, targets)


def expert_call(kernel, plan, quarters, weights, slot_count, grads=None):
    slots, scales = plan
    experts, latent_width, width = weights[0].shape
    groups, _, _, span = slots.shape
    picked = groups * slot_count
    narrow = pltpu.VMEM((picked, latent_width), jnp.bfloat16)
    wide = pltpu.VMEM((picked, width), jnp.bfloat16)
    products = 3
    scratch = [narrow, wide]
    operands = (slots, scales) + tuple(quarters)
    if grads is not None:
        products = 5
        scratch = [narrow, narrow, wide, wide]
        operands = operands + tuple(grads)
    operands = operands + tuple(weights)
    scratch = scratch + [
        pltpu.VMEM((experts, groups, slot_count, latent_width), jnp.bfloat16),
        *[pltpu.VMEM(weight.shape, jnp.bfloat16) for weight in weights],
        pltpu.SemaphoreType.DMA((3, experts)),
    ]
    whole = pl.BlockSpec(memory_space=pltpu.VMEM)
    return pl.pallas_call(
        kernel,
        out_shape=(jax.ShapeDtypeStruct((span, latent_width), jnp.bfloat16),) * groups,
        in_specs=[whole] * (len(operands) - 3) + [pl.BlockSpec(memory_space=pl.ANY)] * 3,
        out_specs=(whole,) * groups,
        scratch_shapes=scratch,
        compiler_params=pltpu.CompilerParams(vmem_limit_bytes=32 << 20),
        cost_estimate=pl.CostEstimate(
            flops=2 * products * experts * picked * latent_width * width,
            bytes_accessed=2 * sum(array.size for array in operands),
            transcendentals=experts * picked * width,
        ),
    )(*operands)


STAGES = ((0,), (1, 2), (3,))


def stage_sums(kernel, plans, near, far, weights, slot_count, stage, grads=None):
    plan = [
        lax.concatenate(
            [plans[side][part][index : index + 1] for side in (0, 1) for index in stage], 0
        )
        for part in (0, 1)
    ]
    return expert_call(
        kernel,
        plan,
        [side[index] for side in (near, far) for index in stage],
        weights,
        slot_count,
        None if grads is None else [side[index] for side in grads for index in stage],
    )


def by_quarter(stages):
    near, far = [], []
    for sums in stages:
        near.extend(sums[: len(sums) // 2])
        far.extend(sums[len(sums) // 2 :])
    return near, far


def expert_plans(told, local_experts, row_count):
    shards = lax.axis_size("expert")
    depth = radices(shards)[Z]
    told = told.astype(jnp.int32).reshape(shards, 2, -1, row_count)
    capacity = 3 * row_count * told.shape[2] // (2 * local_experts * shards)
    mine = lax.axis_index("expert") * local_experts + jnp.arange(local_experts, dtype=jnp.int32)
    chosen = told[:, 0][:, None] == mine[None, :, None, None]
    fixed = jnp.sum(jnp.where(chosen, told[:, 1][:, None], 0), axis=2)
    member = jnp.any(chosen, axis=2)
    earlier = jnp.arange(row_count)[:, None] < jnp.arange(row_count)[None, :]
    ranking = jnp.einsum(
        "set,tu->seu",
        member.astype(jnp.bfloat16),
        earlier.astype(jnp.bfloat16),
        preferred_element_type=jnp.float32,
    ).astype(jnp.int32)
    offset = (jnp.arange(shards, dtype=jnp.int32) % depth * capacity)[:, None, None]
    slots = jnp.where(member, ranking + offset, -1)
    scales = fixed.astype(jnp.float32) / 256.0

    def in_quarters(values):
        values = values.reshape(2, 4, depth, local_experts, row_count).transpose(0, 1, 3, 2, 4)
        return values.reshape(2, 4, local_experts, 1, depth * row_count)

    slots, scales = in_quarters(slots), in_quarters(scales)
    return [(slots[core], scales[core]) for core in (0, 1)], depth * capacity


def tied(*values):
    return lax.optimization_barrier(values)


def local(
    tokens, out_grad, routes, combine_fixed, down_proj, up_proj, expert_gate, expert_up, expert_down
):
    local_experts, latent_width, width = expert_gate.shape
    row_count = tokens.shape[0]
    rows = down_proj.shape[0]
    told = lax.concatenate([routes.T, combine_fixed.T], 0).astype(jnp.bfloat16)
    ride = lax.axis_size("dp") == 1
    sent = [down_proj, up_proj]
    if ride:
        sent.append(told.reshape(rows, -1))
    own, later_tokens, later_grads = tied(
        gather_depth(lax.concatenate(sent, 1), OWNERS), tokens, out_grad
    )
    along_y, along_x = shifted(own, OWNERS, Y), shifted(own, OWNERS, X)
    quarters = (
        own,
        along_y,
        along_x,
        shifted(along_y[:, : tokens.shape[1]], OWNERS, X),
        shifted(along_x[:, tokens.shape[1] :], OWNERS, Y),
    )
    other_tokens = shifted(later_tokens, OWNERS, CORE)
    other_grads = shifted(later_grads, OWNERS, CORE)
    down_place = placement(rows, Y, X)
    up_place = placement(rows, X, Y)
    (latent, mix_grad), (down_near, up_near), told_near = projected(
        (tokens, other_tokens, out_grad, other_grads), quarters
    )
    if not ride:
        told_near = lax.concatenate(
            list(gather_chips(gather_depth(told, EXPERT), EXPERT, Y, X)), 0
        )
    latent, told_near = tied(latent, told_near)
    latent_own = gather_depth(latent, EXPERT)
    latent_own, mix_grad = tied(latent_own, mix_grad)
    near = (latent_own, shifted(latent_own, EXPERT, Y), shifted(latent_own, EXPERT, X))
    mix_own = gather_depth(mix_grad, EXPERT)
    told_far = shifted(told_near, EXPERT, CORE)
    plans, slot_count = expert_plans(
        lax.concatenate([told_near, told_far], 0), local_experts, row_count
    )
    mix_own, near = tied(mix_own, near)
    near = gather_chips_by_turns(near, EXPERT, Y, X)
    far = tuple(shifted(part, EXPERT, CORE) for part in near[:3])
    near_grad = (mix_own, shifted(mix_own, EXPERT, Y), shifted(mix_own, EXPERT, X))
    near_grad = gather_chips_by_turns(near_grad, EXPERT, Y, X)

    weights = (expert_gate, expert_up, expert_down)
    shared = (weights, slot_count)
    first_sums = stage_sums(forward_kernel, plans, near, far, *shared, STAGES[0])
    last_near, first_sums = tied(near[3], first_sums)
    far = far + (shifted(last_near, EXPERT, CORE),)
    forward = [first_sums] + [
        stage_sums(forward_kernel, plans, near, far, *shared, stage) for stage in STAGES[1:]
    ]
    far_grad = tuple(shifted(part, EXPERT, CORE) for part in near_grad)
    last_sums, *along_grads = tied(forward[2], *near_grad[1:3])
    forward_near, forward_far = by_quarter(forward[:2] + [last_sums])
    across, along_y, along_x, own = core_totals(forward_near, forward_far)
    forward_sums = [part.astype(jnp.bfloat16) for part in (across, along_y, along_x)] + [own]
    near_grad = near_grad[:1] + tuple(along_grads) + near_grad[3:]
    backward = [
        stage_sums(backward_kernel, plans, near, far, *shared, stage, (near_grad, far_grad))
        for stage in STAGES
    ]
    backward[0], down_near, up_near = tied(backward[0], down_near, up_near)
    backward_near, backward_far = by_quarter(backward)
    down_far, up_far = [shifted(array, OWNERS, CORE) for array in (down_near, up_near)]

    mixed_sums = chip_totals(*forward_sums)
    backward_across, *backward_sums = core_totals(backward_near, backward_far)
    backward_across = across_by_turns(backward_across)
    mixed_sums, backward_across, backward_sums = tied(
        mixed_sums, backward_across, backward_sums
    )
    mixed_rows = tensor_total(depth_total(mixed_sums, EXPERT)).astype(jnp.bfloat16)
    mixed_relative = matmul(mixed_rows, up_place, ((1,), (1,))).astype(jnp.bfloat16)
    latent_sums = chip_totals_by_turns(*backward_across, *backward_sums)
    latent_sums, later_tokens, later_grads, *quad = tied(
        latent_sums, tokens, out_grad, *quad_columns(mixed_relative, Y)
    )
    next_grads, next_tokens = shifted(later_grads, OWNERS, Y), shifted(later_tokens, OWNERS, X)
    latent_grad, next_tokens, next_grads = tied(
        depth_total(latent_sums, EXPERT), next_tokens, next_grads
    )
    quad_tokens = (tokens, other_tokens, next_tokens, shifted(next_tokens, OWNERS, CORE))
    quad_grads = (out_grad, other_grads, next_grads, shifted(next_grads, OWNERS, CORE))
    latent_grad = tensor_total(latent_grad).astype(jnp.bfloat16)
    up_sent, up_kept = quad_grads_of(tuple(quad), quad_grads)
    up_sums = up_kept + shifted(up_sent, OWNERS, X).astype(jnp.float32)
    grad_relative = matmul(latent_grad, down_place, ((1,), (1,))).astype(jnp.bfloat16)
    quad = quad_columns(grad_relative, X)
    down_sent, down_kept = quad_grads_of(quad, quad_tokens)
    up_sums, mixed_relative, grad_relative, down_sent = tied(
        up_sums, mixed_relative, grad_relative, down_sent
    )
    up_grad = depth_total(up_sums, OWNERS)
    down_sums = down_kept + shifted(down_sent, OWNERS, Y).astype(jnp.float32)
    half = latent_width // 2
    layer_out = matmul(mixed_relative[:, :half], up_near)
    layer_out = (layer_out + matmul(mixed_relative[:, half:], up_far)).astype(jnp.bfloat16)
    token_grad = matmul(grad_relative[:, :half], down_near)
    token_grad = (token_grad + matmul(grad_relative[:, half:], down_far)).astype(jnp.bfloat16)
    down_grad = depth_total(down_sums, OWNERS)
    return (layer_out, token_grad, down_grad, up_grad)


def solution(mesh):
    in_specs = (
        P(("groups", "expert", "dp"), "tensor"),
        P(("groups", "expert", "dp"), "tensor"),
        P(("groups", "expert", "dp"), None),
        P(("groups", "expert", "dp"), None),
        P(("expert", "dp"), "tensor"),
        P(("expert", "dp"), "tensor"),
        P("expert", None, "tensor"),
        P("expert", None, "tensor"),
        P("expert", "tensor", None),
    )
    out_specs = (
        P(("groups", "expert", "dp"), "tensor"),
        P(("groups", "expert", "dp"), "tensor"),
        P(("groups", "expert", "dp"), "tensor"),
        P(("groups", "expert", "dp"), "tensor"),
    )
    return jax.shard_map(local, mesh=mesh, in_specs=in_specs, out_specs=out_specs, check_vma=False)
```

```python
import math

import jax
import jax.numpy as jnp
from jax import lax
from jax.experimental import pallas as pl
from jax.experimental.pallas import tpu as pltpu
from jax.sharding import PartitionSpec as P

OWNERS = ("expert", "dp")
EXPERT = ("expert",)
Z, Y, X, CORE = 0, 1, 2, 3


def tensor_total(partial_sum):
    return lax.psum(partial_sum, "tensor")


def radices(count):
    return (count // 8, 2, 2, 2)


def digit_of(axes, place):
    sizes = radices(math.prod(lax.axis_size(axis) for axis in axes))
    stride = math.prod(sizes[place + 1 :])
    return lax.rem(lax.axis_index(axes) // stride, sizes[place])


def shifted(block, axes, *places, step=1):
    count = math.prod(lax.axis_size(axis) for axis in axes)
    sizes = radices(count)
    pairs = []
    for here in range(count):
        there = here
        for place in places:
            stride = math.prod(sizes[place + 1 :])
            digit = here // stride % sizes[place]
            there += ((digit + step) % sizes[place] - digit) * stride
        pairs.append((here, there))
    return lax.ppermute(block, axes, pairs)


SIDES = ((0, 0), (1, 0), (0, 1), (1, 1))


def device_count(axes):
    return math.prod(lax.axis_size(axis) for axis in axes)


def relative_owners(axes, first, second):
    depth = radices(device_count(axes))[Z]
    owners = []
    for core_step in (0, 1):
        for first_step, second_step in SIDES:
            for z_step in range(depth):
                steps = {Z: depth - z_step, first: first_step, second: second_step, CORE: core_step}
                owner = 0
                for place, size in enumerate(radices(device_count(axes))):
                    digit = lax.rem(digit_of(axes, place) + steps[place], size)
                    owner = owner * size + digit
                owners.append(owner)
    return jnp.stack(owners)


def gather_depth(rows, axes):
    depth = radices(device_count(axes))[Z]
    return lax.concatenate(
        [rows] + [shifted(rows, axes, Z, step=step) for step in range(1, depth)], 0
    )


def gather_chips(own, axes, first, second):
    return (
        own,
        shifted(own, axes, first),
        shifted(own, axes, second),
        shifted(own, axes, first, second),
    )


def gather_chips_by_turns(alongs, axes, first, second):
    own, along_first, along_second = alongs
    half = own.shape[1] // 2
    left = shifted(along_first[:, :half], axes, second)
    right = shifted(along_second[:, half:], axes, first)
    return (own, along_first, along_second, lax.concatenate([left, right], 1))


def core_totals(near, far):
    return [
        near[index].astype(jnp.float32) + shifted(far[index], EXPERT, CORE).astype(jnp.float32)
        for index in (3, 1, 2, 0)
    ]


def depth_total(terms, axes):
    depth = radices(device_count(axes))[Z]
    pieces = jnp.split(terms, depth, axis=0)
    total = pieces[0]
    for step in range(1, depth):
        piece = shifted(pieces[step].astype(jnp.bfloat16), axes, Z, step=depth - step)
        total = total + piece.astype(jnp.float32)
    return total


def across_by_turns(across):
    across = across.astype(jnp.bfloat16)
    half = across.shape[1] // 2
    return shifted(across[:, :half], EXPERT, X), shifted(across[:, half:], EXPERT, Y)


def chip_totals_by_turns(left, right, along_y, along_x, own):
    half = left.shape[1]
    left, right = left.astype(jnp.float32), right.astype(jnp.float32)
    along_y = lax.concatenate([along_y[:, :half] + left, along_y[:, half:]], 1)
    along_x = lax.concatenate([along_x[:, :half], along_x[:, half:] + right], 1)
    own = own + shifted(along_y.astype(jnp.bfloat16), EXPERT, Y).astype(jnp.float32)
    return own + shifted(along_x.astype(jnp.bfloat16), EXPERT, X).astype(jnp.float32)


def placement(rows, first, second):
    owners = relative_owners(OWNERS, first, second)
    targets = (owners[:, None] * rows + jnp.arange(rows, dtype=jnp.int32)[None, :]).reshape(-1)
    columns = jnp.arange(targets.shape[0], dtype=jnp.int32)
    return (targets[:, None] == columns[None, :]).astype(jnp.bfloat16)


def vmem_call(kernel, out_shape, operands, products):
    whole = pl.BlockSpec(memory_space=pltpu.VMEM)
    return pl.pallas_call(
        kernel,
        out_shape=out_shape,
        in_specs=[whole] * len(operands),
        out_specs=(whole,) * len(out_shape),
        compiler_params=pltpu.CompilerParams(vmem_limit_bytes=20 << 20),
        cost_estimate=pl.CostEstimate(
            flops=2 * products,
            bytes_accessed=2 * sum(array.size for array in operands),
            transcendentals=0,
        ),
    )(*operands)


def projection_kernel(*refs):
    tokens, other_tokens, grads, other_grads, *quarters, left, right = refs[:9]
    nears, (told, part, other) = refs[9:11], refs[11:]
    width = nears[0].shape[1]
    count = left.shape[0]
    for near, start, order in zip(nears, (0, width), ((0, 1, 2), (0, 2, 1))):
        for index, quarter in enumerate(order):
            held = slice(index * count, (index + 1) * count)
            near[held, :] = quarters[quarter][:, start : start + width]
    nears[0][3 * count :, :] = left[...]
    nears[1][3 * count :, :] = right[:, :width]
    if right.shape[1] > width:
        for index, quarter in enumerate(quarters):
            told[index * count : (index + 1) * count, :] = quarter[:, 2 * width :]
        told[3 * count :, :] = right[:, width:]
    else:
        told[...] = jnp.zeros_like(told)
    half = nears[0].shape[0]
    for target, down, up in ((part, tokens, grads), (other, other_tokens, other_grads)):
        for source, near, start in ((down, nears[0], 0), (up, nears[1], half)):
            product = matmul(source[...], near[...], ((1,), (1,)))
            target[:, start : start + half] = product.astype(target.dtype)


def projected(inputs, quarters):
    row_count, width = inputs[0].shape
    count = 4 * quarters[0].shape[0]
    extra = max(quarters[0].shape[1] - 2 * width, 128)
    dtype = jnp.bfloat16 if lax.axis_size("tensor") == 1 else jnp.float32
    near = jax.ShapeDtypeStruct((count, width), jnp.bfloat16)
    result = jax.ShapeDtypeStruct((row_count, 2 * count), dtype)
    down_near, up_near, told, part, other = vmem_call(
        projection_kernel,
        (near, near, jax.ShapeDtypeStruct((count, extra), jnp.bfloat16), result, result),
        tuple(inputs) + tuple(quarters),
        4 * row_count * width * count,
    )
    other = shifted(tensor_total(other).astype(jnp.bfloat16), OWNERS, CORE)
    part = tensor_total(part).astype(jnp.bfloat16)
    results = []
    for start, (first, second) in ((0, (Y, X)), (count, (X, Y))):
        place = placement(count // 4 // radices(device_count(OWNERS))[Z], first, second)
        columns = slice(start, start + count)
        relative = lax.concatenate([part[:, columns], other[:, columns]], 1)
        results.append(matmul(relative, place).astype(jnp.bfloat16))
    return results, (down_near, up_near), told


def grad_kernel(*refs):
    quad, inputs, (sent, kept) = refs[:4], refs[4:8], refs[8:]
    half = quad[0].shape[1] // 2
    for target, columns in ((sent, slice(half, None)), (kept, slice(0, half))):
        total = None
        for part, block in zip(quad, inputs):
            term = matmul(part[:, columns], block[...], ((0,), (0,)))
            total = term if total is None else total + term
        target[...] = total.astype(target.dtype)


def quad_columns(relative, second):
    mine, along_second, along_core, across = jnp.split(relative, 4, axis=1)
    return (
        mine,
        shifted(along_core, OWNERS, CORE),
        shifted(along_second, OWNERS, second),
        shifted(across, OWNERS, second, CORE),
    )


def quad_grads_of(quad, quad_inputs):
    shape = (quad[0].shape[1] // 2, quad_inputs[0].shape[1])
    return vmem_call(
        grad_kernel,
        (jax.ShapeDtypeStruct(shape, jnp.bfloat16), jax.ShapeDtypeStruct(shape, jnp.float32)),
        quad + tuple(quad_inputs),
        4 * quad[0].size * shape[1],
    )


def matmul(left, right, contract=((1,), (0,))):
    return lax.dot_general(left, right, (contract, ((), ())), preferred_element_type=jnp.float32)


def selected(slot_ref, group, expert, slots, values=None):
    slot = slot_ref[group, expert]
    here = lax.broadcasted_iota(jnp.int32, (slots, slot.shape[1]), 0) == slot
    return jnp.where(here, 1.0 if values is None else values, 0.0).astype(jnp.bfloat16)


def weight_copies(sources, targets, arrived, expert):
    return [
        pltpu.make_async_copy(source.at[expert], target.at[expert], arrived.at[place, expert])
        for place, (source, target) in enumerate(zip(sources, targets))
    ]


def pick_rows(pick, quarter, target, held):
    target[held, :] = matmul(pick, quarter[...]).astype(jnp.bfloat16)


def spread_rows(slot_ref, scale_ref, results, targets):
    experts, groups, slots, _ = results.shape
    for group in range(groups):
        weights = jnp.concatenate(
            [
                selected(
                    slot_ref,
                    group,
                    expert,
                    slots,
                    None if scale_ref is None else scale_ref[group, expert],
                )
                for expert in range(experts)
            ],
            0,
        )
        values = jnp.concatenate([results[expert, group] for expert in range(experts)], 0)
        targets[group][...] = matmul(weights, values, ((0,), (0,))).astype(jnp.bfloat16)


def forward_kernel(*refs):
    slot_ref, scale_ref, *refs = refs
    rows, hidden, results, gate_ref, up_ref, down_ref, arrived = refs[-7:]
    experts, groups, slots, _ = results.shape
    quarters, hbm_weights, targets = refs[:groups], refs[groups : groups + 3], refs[groups + 3 : -7]
    width = hidden.shape[1]
    chunk = 256
    for expert in range(experts):
        for copy in weight_copies(hbm_weights, (gate_ref, up_ref, down_ref), arrived, expert):
            copy.start()

    @pl.loop(0, experts)
    def _(expert):
        copies = weight_copies(hbm_weights, (gate_ref, up_ref, down_ref), arrived, expert)
        for group in range(groups):
            held = slice(group * slots, (group + 1) * slots)
            pick_rows(selected(slot_ref, group, expert, slots), quarters[group], rows, held)
        copies[0].wait()
        copies[1].wait()
        for start in range(0, width, chunk):
            columns = slice(start, start + chunk)
            gate_act = matmul(rows[...], gate_ref[expert, :, columns])
            up_act = matmul(rows[...], up_ref[expert, :, columns])
            act = gate_act * jax.nn.sigmoid(gate_act) * up_act
            hidden[:, columns] = act.astype(jnp.bfloat16)
        copies[2].wait()
        result = matmul(hidden[...], down_ref[expert]).astype(jnp.bfloat16)
        for group in range(groups):
            results[expert, group] = result[group * slots : (group + 1) * slots, :]

    spread_rows(slot_ref, scale_ref, results, targets)


def backward_kernel(*refs):
    slot_ref, scale_ref, *refs = refs
    rows, grads, gate_grads, value_grads, results, gate_ref, up_ref, down_ref, arrived = refs[-9:]
    experts, groups, slots, _ = results.shape
    quarters, quarter_grads = refs[:groups], refs[groups : 2 * groups]
    hbm_weights, targets = refs[2 * groups : 2 * groups + 3], refs[2 * groups + 3 : -9]
    width = gate_grads.shape[1]
    chunk = 256
    for expert in range(experts):
        for copy in weight_copies(hbm_weights, (gate_ref, up_ref, down_ref), arrived, expert):
            copy.start()

    @pl.loop(0, experts)
    def _(expert):
        for group in range(groups):
            held = slice(group * slots, (group + 1) * slots)
            pick_rows(selected(slot_ref, group, expert, slots), quarters[group], rows, held)
            weighed = selected(slot_ref, group, expert, slots, scale_ref[group, expert])
            pick_rows(weighed, quarter_grads[group], grads, held)
        for copy in weight_copies(hbm_weights, (gate_ref, up_ref, down_ref), arrived, expert):
            copy.wait()
        for start in range(0, width, chunk):
            columns = slice(start, start + chunk)
            gate_act = matmul(rows[...], gate_ref[expert, :, columns])
            up_act = matmul(rows[...], up_ref[expert, :, columns])
            hidden_grad = matmul(grads[...], down_ref[expert, columns, :], ((1,), (1,)))
            sigmoid = jax.nn.sigmoid(gate_act)
            scaled = hidden_grad * sigmoid
            gate_grad = scaled * up_act * (1.0 + gate_act * (1.0 - sigmoid))
            gate_grads[:, columns] = gate_grad.astype(jnp.bfloat16)
            value_grads[:, columns] = (scaled * gate_act).astype(jnp.bfloat16)
        result = matmul(gate_grads[...], gate_ref[expert], ((1,), (1,)))
        result = result + matmul(value_grads[...], up_ref[expert], ((1,), (1,)))
        result = result.astype(jnp.bfloat16)
        for group in range(groups):
            results[expert, group] = result[group * slots : (group + 1) * slots, :]

    spread_rows(slot_ref, None, results, targets)


def expert_call(kernel, plan, quarters, weights, slot_count, grads=None):
    slots, scales = plan
    experts, latent_width, width = weights[0].shape
    groups, _, _, span = slots.shape
    picked = groups * slot_count
    narrow = pltpu.VMEM((picked, latent_width), jnp.bfloat16)
    wide = pltpu.VMEM((picked, width), jnp.bfloat16)
    products = 3
    scratch = [narrow, wide]
    operands = (slots, scales) + tuple(quarters)
    if grads is not None:
        products = 5
        scratch = [narrow, narrow, wide, wide]
        operands = operands + tuple(grads)
    operands = operands + tuple(weights)
    scratch = scratch + [
        pltpu.VMEM((experts, groups, slot_count, latent_width), jnp.bfloat16),
        *[pltpu.VMEM(weight.shape, jnp.bfloat16) for weight in weights],
        pltpu.SemaphoreType.DMA((3, experts)),
    ]
    whole = pl.BlockSpec(memory_space=pltpu.VMEM)
    return pl.pallas_call(
        kernel,
        out_shape=(jax.ShapeDtypeStruct((span, latent_width), jnp.bfloat16),) * groups,
        in_specs=[whole] * (len(operands) - 3) + [pl.BlockSpec(memory_space=pl.ANY)] * 3,
        out_specs=(whole,) * groups,
        scratch_shapes=scratch,
        compiler_params=pltpu.CompilerParams(vmem_limit_bytes=32 << 20),
        cost_estimate=pl.CostEstimate(
            flops=2 * products * experts * picked * latent_width * width,
            bytes_accessed=2 * sum(array.size for array in operands),
            transcendentals=experts * picked * width,
        ),
    )(*operands)


STAGES = ((0,), (1, 2), (3,))


def stage_sums(kernel, plans, near, far, weights, slot_count, stage, grads=None):
    plan = [
        lax.concatenate(
            [plans[side][part][index : index + 1] for side in (0, 1) for index in stage], 0
        )
        for part in (0, 1)
    ]
    return expert_call(
        kernel,
        plan,
        [side[index] for side in (near, far) for index in stage],
        weights,
        slot_count,
        None if grads is None else [side[index] for side in grads for index in stage],
    )


def by_quarter(stages):
    near, far = [], []
    for sums in stages:
        near.extend(sums[: len(sums) // 2])
        far.extend(sums[len(sums) // 2 :])
    return near, far


def expert_plans(told, local_experts, row_count):
    shards = lax.axis_size("expert")
    depth = radices(shards)[Z]
    told = told.astype(jnp.int32).reshape(shards, 2, -1, row_count)
    capacity = 3 * row_count * told.shape[2] // (2 * local_experts * shards)
    mine = lax.axis_index("expert") * local_experts + jnp.arange(local_experts, dtype=jnp.int32)
    chosen = told[:, 0][:, None] == mine[None, :, None, None]
    fixed = jnp.sum(jnp.where(chosen, told[:, 1][:, None], 0), axis=2)
    member = jnp.any(chosen, axis=2)
    earlier = jnp.arange(row_count)[:, None] < jnp.arange(row_count)[None, :]
    ranking = jnp.einsum(
        "set,tu->seu",
        member.astype(jnp.bfloat16),
        earlier.astype(jnp.bfloat16),
        preferred_element_type=jnp.float32,
    ).astype(jnp.int32)
    offset = (jnp.arange(shards, dtype=jnp.int32) % depth * capacity)[:, None, None]
    slots = jnp.where(member, ranking + offset, -1)
    scales = fixed.astype(jnp.float32) / 256.0

    def in_quarters(values):
        values = values.reshape(2, 4, depth, local_experts, row_count).transpose(0, 1, 3, 2, 4)
        return values.reshape(2, 4, local_experts, 1, depth * row_count)

    slots, scales = in_quarters(slots), in_quarters(scales)
    return [(slots[core], scales[core]) for core in (0, 1)], depth * capacity


def tied(*values):
    return lax.optimization_barrier(values)


def local(
    tokens, out_grad, routes, combine_fixed, down_proj, up_proj, expert_gate, expert_up, expert_down
):
    local_experts, latent_width, width = expert_gate.shape
    row_count = tokens.shape[0]
    rows = down_proj.shape[0]
    told = lax.concatenate([routes.T, combine_fixed.T], 0).astype(jnp.bfloat16)
    ride = lax.axis_size("dp") == 1
    sent = [down_proj, up_proj]
    if ride:
        sent.append(told.reshape(rows, -1))
    own, later_tokens, later_grads = tied(
        gather_depth(lax.concatenate(sent, 1), OWNERS), tokens, out_grad
    )
    along_y, along_x = shifted(own, OWNERS, Y), shifted(own, OWNERS, X)
    quarters = (
        own,
        along_y,
        along_x,
        shifted(along_y[:, : tokens.shape[1]], OWNERS, X),
        shifted(along_x[:, tokens.shape[1] :], OWNERS, Y),
    )
    other_tokens = shifted(later_tokens, OWNERS, CORE)
    other_grads = shifted(later_grads, OWNERS, CORE)
    down_place = placement(rows, Y, X)
    up_place = placement(rows, X, Y)
    (latent, mix_grad), (down_near, up_near), told_near = projected(
        (tokens, other_tokens, out_grad, other_grads), quarters
    )
    if not ride:
        told_near = lax.concatenate(
            list(gather_chips(gather_depth(told, EXPERT), EXPERT, Y, X)), 0
        )
    latent, later_tokens, later_grads, told_near = tied(latent, tokens, out_grad, told_near)
    latent_own = gather_depth(latent, EXPERT)
    next_tokens, next_grads = shifted(later_tokens, OWNERS, X), shifted(later_grads, OWNERS, Y)
    latent_own, mix_grad = tied(latent_own, mix_grad)
    near = (latent_own, shifted(latent_own, EXPERT, Y), shifted(latent_own, EXPERT, X))
    mix_own = gather_depth(mix_grad, EXPERT)
    told_far = shifted(told_near, EXPERT, CORE)
    plans, slot_count = expert_plans(
        lax.concatenate([told_near, told_far], 0), local_experts, row_count
    )
    mix_own, near, next_tokens, next_grads = tied(mix_own, near, next_tokens, next_grads)
    near = gather_chips_by_turns(near, EXPERT, Y, X)
    far = tuple(shifted(part, EXPERT, CORE) for part in near[:3])
    near_grad = (mix_own, shifted(mix_own, EXPERT, Y), shifted(mix_own, EXPERT, X))
    near_grad = gather_chips_by_turns(near_grad, EXPERT, Y, X)

    weights = (expert_gate, expert_up, expert_down)
    shared = (weights, slot_count)
    first_sums = stage_sums(forward_kernel, plans, near, far, *shared, STAGES[0])
    last_near, first_sums = tied(near[3], first_sums)
    far = far + (shifted(last_near, EXPERT, CORE),)
    forward = [first_sums] + [
        stage_sums(forward_kernel, plans, near, far, *shared, stage) for stage in STAGES[1:]
    ]
    forward_near, forward_far = by_quarter(forward)
    far_grad = tuple(shifted(part, EXPERT, CORE) for part in near_grad)
    forward_across, *forward_sums = core_totals(forward_near, forward_far)
    forward_across = across_by_turns(forward_across)
    forward_across, along_grads = tied(forward_across, near_grad[1:])
    near_grad = near_grad[:1] + tuple(along_grads)
    backward = [
        stage_sums(backward_kernel, plans, near, far, *shared, stage, (near_grad, far_grad))
        for stage in STAGES
    ]
    backward[0], next_tokens, next_grads, down_near, up_near = tied(
        backward[0], next_tokens, next_grads, down_near, up_near
    )
    backward_near, backward_far = by_quarter(backward)
    last_tokens, last_grads, down_far, up_far = [
        shifted(array, OWNERS, CORE) for array in (next_tokens, next_grads, down_near, up_near)
    ]
    quad_tokens = (tokens, other_tokens, next_tokens, last_tokens)
    quad_grads = (out_grad, other_grads, next_grads, last_grads)

    mixed_sums = chip_totals_by_turns(*forward_across, *forward_sums)
    backward_across, *backward_sums = core_totals(backward_near, backward_far)
    backward_across = across_by_turns(backward_across)
    mixed_sums, backward_across, backward_sums = tied(
        mixed_sums, backward_across, backward_sums
    )
    mixed_rows = tensor_total(depth_total(mixed_sums, EXPERT)).astype(jnp.bfloat16)
    mixed_relative = matmul(mixed_rows, up_place, ((1,), (1,))).astype(jnp.bfloat16)
    latent_sums = chip_totals_by_turns(*backward_across, *backward_sums)
    quad = quad_columns(mixed_relative, Y)
    latent_grad = tensor_total(depth_total(latent_sums, EXPERT)).astype(jnp.bfloat16)
    up_sent, up_kept = quad_grads_of(quad, quad_grads)
    up_sums = up_kept + shifted(up_sent, OWNERS, X).astype(jnp.float32)
    grad_relative = matmul(latent_grad, down_place, ((1,), (1,))).astype(jnp.bfloat16)
    quad = quad_columns(grad_relative, X)
    down_sent, down_kept = quad_grads_of(quad, quad_tokens)
    up_sums, mixed_relative, grad_relative, down_sent = tied(
        up_sums, mixed_relative, grad_relative, down_sent
    )
    up_grad = depth_total(up_sums, OWNERS)
    down_sums = down_kept + shifted(down_sent, OWNERS, Y).astype(jnp.float32)
    half = latent_width // 2
    layer_out = matmul(mixed_relative[:, :half], up_near)
    layer_out = (layer_out + matmul(mixed_relative[:, half:], up_far)).astype(jnp.bfloat16)
    token_grad = matmul(grad_relative[:, :half], down_near)
    token_grad = (token_grad + matmul(grad_relative[:, half:], down_far)).astype(jnp.bfloat16)
    down_grad = depth_total(down_sums, OWNERS)
    return (layer_out, token_grad, down_grad, up_grad)


def solution(mesh):
    in_specs = (
        P(("groups", "expert", "dp"), "tensor"),
        P(("groups", "expert", "dp"), "tensor"),
        P(("groups", "expert", "dp"), None),
        P(("groups", "expert", "dp"), None),
        P(("expert", "dp"), "tensor"),
        P(("expert", "dp"), "tensor"),
        P("expert", None, "tensor"),
        P("expert", None, "tensor"),
        P("expert", "tensor", None),
    )
    out_specs = (
        P(("groups", "expert", "dp"), "tensor"),
        P(("groups", "expert", "dp"), "tensor"),
        P(("groups", "expert", "dp"), "tensor"),
        P(("groups", "expert", "dp"), "tensor"),
    )
    return jax.shard_map(local, mesh=mesh, in_specs=in_specs, out_specs=out_specs, check_vma=False)
```

```python
import math

import jax
import jax.numpy as jnp
from jax import lax
from jax.experimental import pallas as pl
from jax.experimental.pallas import tpu as pltpu
from jax.sharding import PartitionSpec as P

OWNERS = ("expert", "dp")
EXPERT = ("expert",)
Z, Y, X, CORE = 0, 1, 2, 3


def tensor_total(partial_sum):
    return lax.psum(partial_sum, "tensor")


def radices(count):
    return (count // 8, 2, 2, 2)


def digit_of(axes, place):
    sizes = radices(math.prod(lax.axis_size(axis) for axis in axes))
    stride = math.prod(sizes[place + 1 :])
    return lax.rem(lax.axis_index(axes) // stride, sizes[place])


def shifted(block, axes, *places, step=1):
    count = math.prod(lax.axis_size(axis) for axis in axes)
    sizes = radices(count)
    pairs = []
    for here in range(count):
        there = here
        for place in places:
            stride = math.prod(sizes[place + 1 :])
            digit = here // stride % sizes[place]
            there += ((digit + step) % sizes[place] - digit) * stride
        pairs.append((here, there))
    return lax.ppermute(block, axes, pairs)


SIDES = ((0, 0), (1, 0), (0, 1), (1, 1))


def device_count(axes):
    return math.prod(lax.axis_size(axis) for axis in axes)


def relative_owners(axes, first, second):
    depth = radices(device_count(axes))[Z]
    owners = []
    for core_step in (0, 1):
        for first_step, second_step in SIDES:
            for z_step in range(depth):
                steps = {Z: depth - z_step, first: first_step, second: second_step, CORE: core_step}
                owner = 0
                for place, size in enumerate(radices(device_count(axes))):
                    digit = lax.rem(digit_of(axes, place) + steps[place], size)
                    owner = owner * size + digit
                owners.append(owner)
    return jnp.stack(owners)


def gather_depth(rows, axes):
    depth = radices(device_count(axes))[Z]
    return lax.concatenate(
        [rows] + [shifted(rows, axes, Z, step=step) for step in range(1, depth)], 0
    )


def gather_chips(own, axes, first, second):
    return (
        own,
        shifted(own, axes, first),
        shifted(own, axes, second),
        shifted(own, axes, first, second),
    )


def gather_chips_by_turns(alongs, axes, first, second):
    own, along_first, along_second = alongs
    half = own.shape[1] // 2
    left = shifted(along_first[:, :half], axes, second)
    right = shifted(along_second[:, half:], axes, first)
    return (own, along_first, along_second, lax.concatenate([left, right], 1))


def core_totals(near, far):
    return [
        near[index].astype(jnp.float32) + shifted(far[index], EXPERT, CORE).astype(jnp.float32)
        for index in (3, 1, 2, 0)
    ]


def depth_total(terms, axes):
    depth = radices(device_count(axes))[Z]
    pieces = jnp.split(terms, depth, axis=0)
    total = pieces[0]
    for step in range(1, depth):
        piece = shifted(pieces[step].astype(jnp.bfloat16), axes, Z, step=depth - step)
        total = total + piece.astype(jnp.float32)
    return total


def chip_totals(across, along_y, along_x, own):
    across = shifted(across.astype(jnp.bfloat16), EXPERT, X, Y)
    along_y = shifted(along_y.astype(jnp.bfloat16), EXPERT, Y)
    along_x = shifted(along_x.astype(jnp.bfloat16), EXPERT, X)
    total = own + across.astype(jnp.float32)
    return total + along_y.astype(jnp.float32) + along_x.astype(jnp.float32)


def across_by_turns(across):
    across = across.astype(jnp.bfloat16)
    half = across.shape[1] // 2
    return shifted(across[:, :half], EXPERT, X), shifted(across[:, half:], EXPERT, Y)


def chip_totals_by_turns(left, right, along_y, along_x, own):
    half = left.shape[1]
    left, right = left.astype(jnp.float32), right.astype(jnp.float32)
    along_y = lax.concatenate([along_y[:, :half] + left, along_y[:, half:]], 1)
    along_x = lax.concatenate([along_x[:, :half], along_x[:, half:] + right], 1)
    own = own + shifted(along_y.astype(jnp.bfloat16), EXPERT, Y).astype(jnp.float32)
    return own + shifted(along_x.astype(jnp.bfloat16), EXPERT, X).astype(jnp.float32)


def placement(rows, first, second):
    owners = relative_owners(OWNERS, first, second)
    targets = (owners[:, None] * rows + jnp.arange(rows, dtype=jnp.int32)[None, :]).reshape(-1)
    columns = jnp.arange(targets.shape[0], dtype=jnp.int32)
    return (targets[:, None] == columns[None, :]).astype(jnp.bfloat16)


def vmem_call(kernel, out_shape, operands, products):
    whole = pl.BlockSpec(memory_space=pltpu.VMEM)
    return pl.pallas_call(
        kernel,
        out_shape=out_shape,
        in_specs=[whole] * len(operands),
        out_specs=(whole,) * len(out_shape),
        compiler_params=pltpu.CompilerParams(vmem_limit_bytes=20 << 20),
        cost_estimate=pl.CostEstimate(
            flops=2 * products,
            bytes_accessed=2 * sum(array.size for array in operands),
            transcendentals=0,
        ),
    )(*operands)


def projection_kernel(*refs):
    tokens, other_tokens, grads, other_grads, *quarters, left, right = refs[:9]
    nears, (told, part, other) = refs[9:11], refs[11:]
    width = nears[0].shape[1]
    count = left.shape[0]
    for near, start, order in zip(nears, (0, width), ((0, 1, 2), (0, 2, 1))):
        for index, quarter in enumerate(order):
            held = slice(index * count, (index + 1) * count)
            near[held, :] = quarters[quarter][:, start : start + width]
    nears[0][3 * count :, :] = left[...]
    nears[1][3 * count :, :] = right[:, :width]
    if right.shape[1] > width:
        for index, quarter in enumerate(quarters):
            told[index * count : (index + 1) * count, :] = quarter[:, 2 * width :]
        told[3 * count :, :] = right[:, width:]
    else:
        told[...] = jnp.zeros_like(told)
    half = nears[0].shape[0]
    for target, down, up in ((part, tokens, grads), (other, other_tokens, other_grads)):
        for source, near, start in ((down, nears[0], 0), (up, nears[1], half)):
            product = matmul(source[...], near[...], ((1,), (1,)))
            target[:, start : start + half] = product.astype(target.dtype)


def projected(inputs, quarters):
    row_count, width = inputs[0].shape
    count = 4 * quarters[0].shape[0]
    extra = max(quarters[0].shape[1] - 2 * width, 128)
    dtype = jnp.bfloat16 if lax.axis_size("tensor") == 1 else jnp.float32
    near = jax.ShapeDtypeStruct((count, width), jnp.bfloat16)
    result = jax.ShapeDtypeStruct((row_count, 2 * count), dtype)
    down_near, up_near, told, part, other = vmem_call(
        projection_kernel,
        (near, near, jax.ShapeDtypeStruct((count, extra), jnp.bfloat16), result, result),
        tuple(inputs) + tuple(quarters),
        4 * row_count * width * count,
    )
    other = shifted(tensor_total(other).astype(jnp.bfloat16), OWNERS, CORE)
    part = tensor_total(part).astype(jnp.bfloat16)
    results = []
    for start, (first, second) in ((0, (Y, X)), (count, (X, Y))):
        place = placement(count // 4 // radices(device_count(OWNERS))[Z], first, second)
        columns = slice(start, start + count)
        relative = lax.concatenate([part[:, columns], other[:, columns]], 1)
        results.append(matmul(relative, place).astype(jnp.bfloat16))
    return results, (down_near, up_near), told


def grad_kernel(*refs):
    quad, inputs, (sent, kept) = refs[:4], refs[4:8], refs[8:]
    half = quad[0].shape[1] // 2
    for target, columns in ((sent, slice(half, None)), (kept, slice(0, half))):
        total = None
        for part, block in zip(quad, inputs):
            term = matmul(part[:, columns], block[...], ((0,), (0,)))
            total = term if total is None else total + term
        target[...] = total.astype(target.dtype)


def quad_columns(relative, second):
    mine, along_second, along_core, across = jnp.split(relative, 4, axis=1)
    return (
        mine,
        shifted(along_core, OWNERS, CORE),
        shifted(along_second, OWNERS, second),
        shifted(across, OWNERS, second, CORE),
    )


def quad_grads_of(quad, quad_inputs):
    shape = (quad[0].shape[1] // 2, quad_inputs[0].shape[1])
    return vmem_call(
        grad_kernel,
        (jax.ShapeDtypeStruct(shape, jnp.bfloat16), jax.ShapeDtypeStruct(shape, jnp.float32)),
        quad + tuple(quad_inputs),
        4 * quad[0].size * shape[1],
    )


def matmul(left, right, contract=((1,), (0,))):
    return lax.dot_general(left, right, (contract, ((), ())), preferred_element_type=jnp.float32)


def selected(slot_ref, group, expert, slots, values=None):
    slot = slot_ref[group, expert]
    here = lax.broadcasted_iota(jnp.int32, (slots, slot.shape[1]), 0) == slot
    return jnp.where(here, 1.0 if values is None else values, 0.0).astype(jnp.bfloat16)


def weight_copies(sources, targets, arrived, expert):
    return [
        pltpu.make_async_copy(source.at[expert], target.at[expert], arrived.at[place, expert])
        for place, (source, target) in enumerate(zip(sources, targets))
    ]


def pick_rows(pick, quarter, target, held):
    target[held, :] = matmul(pick, quarter[...]).astype(jnp.bfloat16)


def spread_rows(slot_ref, scale_ref, results, targets):
    experts, groups, slots, _ = results.shape
    for group in range(groups):
        weights = jnp.concatenate(
            [
                selected(
                    slot_ref,
                    group,
                    expert,
                    slots,
                    None if scale_ref is None else scale_ref[group, expert],
                )
                for expert in range(experts)
            ],
            0,
        )
        values = jnp.concatenate([results[expert, group] for expert in range(experts)], 0)
        targets[group][...] = matmul(weights, values, ((0,), (0,))).astype(jnp.bfloat16)


def forward_kernel(*refs):
    slot_ref, scale_ref, *refs = refs
    rows, hidden, results, gate_ref, up_ref, down_ref, arrived = refs[-7:]
    experts, groups, slots, _ = results.shape
    quarters, hbm_weights, targets = refs[:groups], refs[groups : groups + 3], refs[groups + 3 : -7]
    width = hidden.shape[1]
    chunk = 256
    for expert in range(experts):
        for copy in weight_copies(hbm_weights, (gate_ref, up_ref, down_ref), arrived, expert):
            copy.start()

    @pl.loop(0, experts)
    def _(expert):
        copies = weight_copies(hbm_weights, (gate_ref, up_ref, down_ref), arrived, expert)
        for group in range(groups):
            held = slice(group * slots, (group + 1) * slots)
            pick_rows(selected(slot_ref, group, expert, slots), quarters[group], rows, held)
        copies[0].wait()
        copies[1].wait()
        for start in range(0, width, chunk):
            columns = slice(start, start + chunk)
            gate_act = matmul(rows[...], gate_ref[expert, :, columns])
            up_act = matmul(rows[...], up_ref[expert, :, columns])
            act = gate_act * jax.nn.sigmoid(gate_act) * up_act
            hidden[:, columns] = act.astype(jnp.bfloat16)
        copies[2].wait()
        result = matmul(hidden[...], down_ref[expert]).astype(jnp.bfloat16)
        for group in range(groups):
            results[expert, group] = result[group * slots : (group + 1) * slots, :]

    spread_rows(slot_ref, scale_ref, results, targets)


def backward_kernel(*refs):
    slot_ref, scale_ref, *refs = refs
    rows, grads, gate_grads, value_grads, results, gate_ref, up_ref, down_ref, arrived = refs[-9:]
    experts, groups, slots, _ = results.shape
    quarters, quarter_grads = refs[:groups], refs[groups : 2 * groups]
    hbm_weights, targets = refs[2 * groups : 2 * groups + 3], refs[2 * groups + 3 : -9]
    width = gate_grads.shape[1]
    chunk = 256
    for expert in range(experts):
        for copy in weight_copies(hbm_weights, (gate_ref, up_ref, down_ref), arrived, expert):
            copy.start()

    @pl.loop(0, experts)
    def _(expert):
        for group in range(groups):
            held = slice(group * slots, (group + 1) * slots)
            pick_rows(selected(slot_ref, group, expert, slots), quarters[group], rows, held)
            weighed = selected(slot_ref, group, expert, slots, scale_ref[group, expert])
            pick_rows(weighed, quarter_grads[group], grads, held)
        for copy in weight_copies(hbm_weights, (gate_ref, up_ref, down_ref), arrived, expert):
            copy.wait()
        for start in range(0, width, chunk):
            columns = slice(start, start + chunk)
            gate_act = matmul(rows[...], gate_ref[expert, :, columns])
            up_act = matmul(rows[...], up_ref[expert, :, columns])
            hidden_grad = matmul(grads[...], down_ref[expert, columns, :], ((1,), (1,)))
            sigmoid = jax.nn.sigmoid(gate_act)
            scaled = hidden_grad * sigmoid
            gate_grad = scaled * up_act * (1.0 + gate_act * (1.0 - sigmoid))
            gate_grads[:, columns] = gate_grad.astype(jnp.bfloat16)
            value_grads[:, columns] = (scaled * gate_act).astype(jnp.bfloat16)
        result = matmul(gate_grads[...], gate_ref[expert], ((1,), (1,)))
        result = result + matmul(value_grads[...], up_ref[expert], ((1,), (1,)))
        result = result.astype(jnp.bfloat16)
        for group in range(groups):
            results[expert, group] = result[group * slots : (group + 1) * slots, :]

    spread_rows(slot_ref, None, results, targets)


def expert_call(kernel, plan, quarters, weights, slot_count, grads=None):
    slots, scales = plan
    experts, latent_width, width = weights[0].shape
    groups, _, _, span = slots.shape
    picked = groups * slot_count
    narrow = pltpu.VMEM((picked, latent_width), jnp.bfloat16)
    wide = pltpu.VMEM((picked, width), jnp.bfloat16)
    products = 3
    scratch = [narrow, wide]
    operands = (slots, scales) + tuple(quarters)
    if grads is not None:
        products = 5
        scratch = [narrow, narrow, wide, wide]
        operands = operands + tuple(grads)
    operands = operands + tuple(weights)
    scratch = scratch + [
        pltpu.VMEM((experts, groups, slot_count, latent_width), jnp.bfloat16),
        *[pltpu.VMEM(weight.shape, jnp.bfloat16) for weight in weights],
        pltpu.SemaphoreType.DMA((3, experts)),
    ]
    whole = pl.BlockSpec(memory_space=pltpu.VMEM)
    return pl.pallas_call(
        kernel,
        out_shape=(jax.ShapeDtypeStruct((span, latent_width), jnp.bfloat16),) * groups,
        in_specs=[whole] * (len(operands) - 3) + [pl.BlockSpec(memory_space=pl.ANY)] * 3,
        out_specs=(whole,) * groups,
        scratch_shapes=scratch,
        compiler_params=pltpu.CompilerParams(vmem_limit_bytes=32 << 20),
        cost_estimate=pl.CostEstimate(
            flops=2 * products * experts * picked * latent_width * width,
            bytes_accessed=2 * sum(array.size for array in operands),
            transcendentals=experts * picked * width,
        ),
    )(*operands)


STAGES = ((0,), (1, 2), (3,))


def stage_sums(kernel, plans, near, far, weights, slot_count, stage, grads=None):
    plan = [
        lax.concatenate(
            [plans[side][part][index : index + 1] for side in (0, 1) for index in stage], 0
        )
        for part in (0, 1)
    ]
    return expert_call(
        kernel,
        plan,
        [side[index] for side in (near, far) for index in stage],
        weights,
        slot_count,
        None if grads is None else [side[index] for side in grads for index in stage],
    )


def by_quarter(stages):
    near, far = [], []
    for sums in stages:
        near.extend(sums[: len(sums) // 2])
        far.extend(sums[len(sums) // 2 :])
    return near, far


def expert_plans(told, local_experts, row_count):
    shards = lax.axis_size("expert")
    depth = radices(shards)[Z]
    told = told.astype(jnp.int32).reshape(shards, 2, -1, row_count)
    capacity = 3 * row_count * told.shape[2] // (2 * local_experts * shards)
    mine = lax.axis_index("expert") * local_experts + jnp.arange(local_experts, dtype=jnp.int32)
    chosen = told[:, 0][:, None] == mine[None, :, None, None]
    fixed = jnp.sum(jnp.where(chosen, told[:, 1][:, None], 0), axis=2)
    member = jnp.any(chosen, axis=2)
    earlier = jnp.arange(row_count)[:, None] < jnp.arange(row_count)[None, :]
    ranking = jnp.einsum(
        "set,tu->seu",
        member.astype(jnp.bfloat16),
        earlier.astype(jnp.bfloat16),
        preferred_element_type=jnp.float32,
    ).astype(jnp.int32)
    offset = (jnp.arange(shards, dtype=jnp.int32) % depth * capacity)[:, None, None]
    slots = jnp.where(member, ranking + offset, -1)
    scales = fixed.astype(jnp.float32) / 256.0

    def in_quarters(values):
        values = values.reshape(2, 4, depth, local_experts, row_count).transpose(0, 1, 3, 2, 4)
        return values.reshape(2, 4, local_experts, 1, depth * row_count)

    slots, scales = in_quarters(slots), in_quarters(scales)
    return [(slots[core], scales[core]) for core in (0, 1)], depth * capacity


def tied(*values):
    return lax.optimization_barrier(values)


def local(
    tokens, out_grad, routes, combine_fixed, down_proj, up_proj, expert_gate, expert_up, expert_down
):
    local_experts, latent_width, width = expert_gate.shape
    row_count = tokens.shape[0]
    rows = down_proj.shape[0]
    told = lax.concatenate([routes.T, combine_fixed.T], 0).astype(jnp.bfloat16)
    ride = lax.axis_size("dp") == 1
    sent = [down_proj, up_proj]
    if ride:
        sent.append(told.reshape(rows, -1))
    own, later_tokens, later_grads = tied(
        gather_depth(lax.concatenate(sent, 1), OWNERS), tokens, out_grad
    )
    along_y, along_x = shifted(own, OWNERS, Y), shifted(own, OWNERS, X)
    quarters = (
        own,
        along_y,
        along_x,
        shifted(along_y[:, : tokens.shape[1]], OWNERS, X),
        shifted(along_x[:, tokens.shape[1] :], OWNERS, Y),
    )
    other_tokens = shifted(later_tokens, OWNERS, CORE)
    other_grads = shifted(later_grads, OWNERS, CORE)
    down_place = placement(rows, Y, X)
    up_place = placement(rows, X, Y)
    (latent, mix_grad), (down_near, up_near), told_near = projected(
        (tokens, other_tokens, out_grad, other_grads), quarters
    )
    if not ride:
        told_near = lax.concatenate(
            list(gather_chips(gather_depth(told, EXPERT), EXPERT, Y, X)), 0
        )
    latent, later_tokens, later_grads, told_near = tied(latent, tokens, out_grad, told_near)
    latent_own = gather_depth(latent, EXPERT)
    next_tokens, next_grads = shifted(later_tokens, OWNERS, X), shifted(later_grads, OWNERS, Y)
    latent_own, mix_grad = tied(latent_own, mix_grad)
    near = (latent_own, shifted(latent_own, EXPERT, Y), shifted(latent_own, EXPERT, X))
    mix_own = gather_depth(mix_grad, EXPERT)
    told_far = shifted(told_near, EXPERT, CORE)
    plans, slot_count = expert_plans(
        lax.concatenate([told_near, told_far], 0), local_experts, row_count
    )
    mix_own, near, next_tokens, next_grads = tied(mix_own, near, next_tokens, next_grads)
    near = gather_chips_by_turns(near, EXPERT, Y, X)
    far = tuple(shifted(part, EXPERT, CORE) for part in near[:3])
    near_grad = (mix_own, shifted(mix_own, EXPERT, Y), shifted(mix_own, EXPERT, X))

    weights = (expert_gate, expert_up, expert_down)
    shared = (weights, slot_count)
    first_sums = stage_sums(forward_kernel, plans, near, far, *shared, STAGES[0])
    last_near, first_sums = tied(near[3], first_sums)
    far = far + (shifted(last_near, EXPERT, CORE),)
    middle_sums, last_sums, near_grad = tied(
        stage_sums(forward_kernel, plans, near, far, *shared, STAGES[1]),
        stage_sums(forward_kernel, plans, near, far, *shared, STAGES[2]),
        near_grad,
    )
    near_grad = gather_chips_by_turns(near_grad, EXPERT, Y, X)
    forward = [first_sums, middle_sums, last_sums]
    forward_near, forward_far = by_quarter(forward)
    far_grad = tuple(shifted(part, EXPERT, CORE) for part in near_grad)
    across, along_y, along_x, own = core_totals(forward_near, forward_far)
    forward_sums = [part.astype(jnp.bfloat16) for part in (across, along_y, along_x)] + [own]
    mix_own, *forward_alongs = tied(near_grad[0], *forward_sums[1:])
    near_grad = (mix_own,) + tuple(near_grad[1:])
    backward = [
        stage_sums(
            backward_kernel, plans, near, far, *shared, STAGES[0], (near_grad, far_grad)
        )
    ]
    along_grads, forward_across = tied(near_grad[1:], forward_sums[0])
    forward_sums = [forward_across] + forward_alongs
    near_grad = near_grad[:1] + tuple(along_grads)
    backward += [
        stage_sums(backward_kernel, plans, near, far, *shared, stage, (near_grad, far_grad))
        for stage in STAGES[1:]
    ]
    backward[0], next_tokens, next_grads, down_near, up_near = tied(
        backward[0], next_tokens, next_grads, down_near, up_near
    )
    backward_near, backward_far = by_quarter(backward)
    last_tokens, last_grads, down_far, up_far = [
        shifted(array, OWNERS, CORE) for array in (next_tokens, next_grads, down_near, up_near)
    ]
    quad_tokens = (tokens, other_tokens, next_tokens, last_tokens)
    quad_grads = (out_grad, other_grads, next_grads, last_grads)

    mixed_sums = chip_totals(*forward_sums)
    backward_across, *backward_sums = core_totals(backward_near, backward_far)
    backward_across = across_by_turns(backward_across)
    mixed_sums, backward_across, backward_sums = tied(
        mixed_sums, backward_across, backward_sums
    )
    mixed_rows = tensor_total(depth_total(mixed_sums, EXPERT)).astype(jnp.bfloat16)
    mixed_relative = matmul(mixed_rows, up_place, ((1,), (1,))).astype(jnp.bfloat16)
    latent_sums = chip_totals_by_turns(*backward_across, *backward_sums)
    mixed_relative, latent_sums = tied(mixed_relative, latent_sums)
    quad = quad_columns(mixed_relative, Y)
    latent_grad = tensor_total(depth_total(latent_sums, EXPERT)).astype(jnp.bfloat16)
    up_sent, up_kept = quad_grads_of(quad, quad_grads)
    up_sums = up_kept + shifted(up_sent, OWNERS, X).astype(jnp.float32)
    grad_relative = matmul(latent_grad, down_place, ((1,), (1,))).astype(jnp.bfloat16)
    quad = quad_columns(grad_relative, X)
    down_sent, down_kept = quad_grads_of(quad, quad_tokens)
    up_sums, mixed_relative, grad_relative, down_sent = tied(
        up_sums, mixed_relative, grad_relative, down_sent
    )
    up_grad = depth_total(up_sums, OWNERS)
    down_sums = down_kept + shifted(down_sent, OWNERS, Y).astype(jnp.float32)
    half = latent_width // 2
    layer_out = matmul(mixed_relative[:, :half], up_near)
    layer_out = (layer_out + matmul(mixed_relative[:, half:], up_far)).astype(jnp.bfloat16)
    token_grad = matmul(grad_relative[:, :half], down_near)
    token_grad = (token_grad + matmul(grad_relative[:, half:], down_far)).astype(jnp.bfloat16)
    down_grad = depth_total(down_sums, OWNERS)
    return (layer_out, token_grad, down_grad, up_grad)


def solution(mesh):
    in_specs = (
        P(("groups", "expert", "dp"), "tensor"),
        P(("groups", "expert", "dp"), "tensor"),
        P(("groups", "expert", "dp"), None),
        P(("groups", "expert", "dp"), None),
        P(("expert", "dp"), "tensor"),
        P(("expert", "dp"), "tensor"),
        P("expert", None, "tensor"),
        P("expert", None, "tensor"),
        P("expert", "tensor", None),
    )
    out_specs = (
        P(("groups", "expert", "dp"), "tensor"),
        P(("groups", "expert", "dp"), "tensor"),
        P(("groups", "expert", "dp"), "tensor"),
        P(("groups", "expert", "dp"), "tensor"),
    )
    return jax.shard_map(local, mesh=mesh, in_specs=in_specs, out_specs=out_specs, check_vma=False)
```

```python
import math

import jax
import jax.numpy as jnp
from jax import lax
from jax.experimental import pallas as pl
from jax.experimental.pallas import tpu as pltpu
from jax.sharding import PartitionSpec as P

OWNERS = ("expert", "dp")
EXPERT = ("expert",)
Z, Y, X, CORE = 0, 1, 2, 3


def tensor_total(partial_sum):
    return lax.psum(partial_sum, "tensor")


def radices(count):
    return (count // 8, 2, 2, 2)


def digit_of(axes, place):
    sizes = radices(math.prod(lax.axis_size(axis) for axis in axes))
    stride = math.prod(sizes[place + 1 :])
    return lax.rem(lax.axis_index(axes) // stride, sizes[place])


def shifted(block, axes, *places, step=1):
    count = math.prod(lax.axis_size(axis) for axis in axes)
    sizes = radices(count)
    pairs = []
    for here in range(count):
        there = here
        for place in places:
            stride = math.prod(sizes[place + 1 :])
            digit = here // stride % sizes[place]
            there += ((digit + step) % sizes[place] - digit) * stride
        pairs.append((here, there))
    return lax.ppermute(block, axes, pairs)


SIDES = ((0, 0), (1, 0), (0, 1), (1, 1))


def device_count(axes):
    return math.prod(lax.axis_size(axis) for axis in axes)


def relative_owners(axes, first, second):
    depth = radices(device_count(axes))[Z]
    owners = []
    for core_step in (0, 1):
        for first_step, second_step in SIDES:
            for z_step in range(depth):
                steps = {Z: depth - z_step, first: first_step, second: second_step, CORE: core_step}
                owner = 0
                for place, size in enumerate(radices(device_count(axes))):
                    digit = lax.rem(digit_of(axes, place) + steps[place], size)
                    owner = owner * size + digit
                owners.append(owner)
    return jnp.stack(owners)


def gather_depth(rows, axes):
    depth = radices(device_count(axes))[Z]
    return lax.concatenate(
        [rows] + [shifted(rows, axes, Z, step=step) for step in range(1, depth)], 0
    )


def gather_chips(own, axes, first, second):
    return (
        own,
        shifted(own, axes, first),
        shifted(own, axes, second),
        shifted(own, axes, first, second),
    )


def gather_chips_by_turns(alongs, axes, first, second):
    own, along_first, along_second = alongs
    half = own.shape[1] // 2
    left = shifted(along_first[:, :half], axes, second)
    right = shifted(along_second[:, half:], axes, first)
    return (own, along_first, along_second, lax.concatenate([left, right], 1))


def core_totals(near, far):
    return [
        near[index].astype(jnp.float32) + shifted(far[index], EXPERT, CORE).astype(jnp.float32)
        for index in (3, 1, 2, 0)
    ]


def depth_total(terms, axes):
    depth = radices(device_count(axes))[Z]
    pieces = jnp.split(terms, depth, axis=0)
    total = pieces[0]
    for step in range(1, depth):
        piece = shifted(pieces[step].astype(jnp.bfloat16), axes, Z, step=depth - step)
        total = total + piece.astype(jnp.float32)
    return total


def chip_totals(across, along_y, along_x, own):
    across = shifted(across.astype(jnp.bfloat16), EXPERT, X, Y)
    along_y = shifted(along_y.astype(jnp.bfloat16), EXPERT, Y)
    along_x = shifted(along_x.astype(jnp.bfloat16), EXPERT, X)
    total = own + across.astype(jnp.float32)
    return total + along_y.astype(jnp.float32) + along_x.astype(jnp.float32)


def across_by_turns(across):
    across = across.astype(jnp.bfloat16)
    half = across.shape[1] // 2
    return shifted(across[:, :half], EXPERT, X), shifted(across[:, half:], EXPERT, Y)


def chip_totals_by_turns(left, right, along_y, along_x, own):
    half = left.shape[1]
    left, right = left.astype(jnp.float32), right.astype(jnp.float32)
    along_y = lax.concatenate([along_y[:, :half] + left, along_y[:, half:]], 1)
    along_x = lax.concatenate([along_x[:, :half], along_x[:, half:] + right], 1)
    own = own + shifted(along_y.astype(jnp.bfloat16), EXPERT, Y).astype(jnp.float32)
    return own + shifted(along_x.astype(jnp.bfloat16), EXPERT, X).astype(jnp.float32)


def placement(rows, first, second):
    owners = relative_owners(OWNERS, first, second)
    targets = (owners[:, None] * rows + jnp.arange(rows, dtype=jnp.int32)[None, :]).reshape(-1)
    columns = jnp.arange(targets.shape[0], dtype=jnp.int32)
    return (targets[:, None] == columns[None, :]).astype(jnp.bfloat16)


def vmem_call(kernel, out_shape, operands, products):
    whole = pl.BlockSpec(memory_space=pltpu.VMEM)
    return pl.pallas_call(
        kernel,
        out_shape=out_shape,
        in_specs=[whole] * len(operands),
        out_specs=(whole,) * len(out_shape),
        compiler_params=pltpu.CompilerParams(vmem_limit_bytes=20 << 20),
        cost_estimate=pl.CostEstimate(
            flops=2 * products,
            bytes_accessed=2 * sum(array.size for array in operands),
            transcendentals=0,
        ),
    )(*operands)


def projection_kernel(*refs):
    tokens, other_tokens, grads, other_grads, *quarters, left, right = refs[:9]
    nears, (told, part, other) = refs[9:11], refs[11:]
    width = nears[0].shape[1]
    count = left.shape[0]
    for near, start, order in zip(nears, (0, width), ((0, 1, 2), (0, 2, 1))):
        for index, quarter in enumerate(order):
            held = slice(index * count, (index + 1) * count)
            near[held, :] = quarters[quarter][:, start : start + width]
    nears[0][3 * count :, :] = left[...]
    nears[1][3 * count :, :] = right[:, :width]
    if right.shape[1] > width:
        for index, quarter in enumerate(quarters):
            told[index * count : (index + 1) * count, :] = quarter[:, 2 * width :]
        told[3 * count :, :] = right[:, width:]
    else:
        told[...] = jnp.zeros_like(told)
    half = nears[0].shape[0]
    for target, down, up in ((part, tokens, grads), (other, other_tokens, other_grads)):
        for source, near, start in ((down, nears[0], 0), (up, nears[1], half)):
            product = matmul(source[...], near[...], ((1,), (1,)))
            target[:, start : start + half] = product.astype(target.dtype)


def projected(inputs, quarters):
    row_count, width = inputs[0].shape
    count = 4 * quarters[0].shape[0]
    extra = max(quarters[0].shape[1] - 2 * width, 128)
    dtype = jnp.bfloat16 if lax.axis_size("tensor") == 1 else jnp.float32
    near = jax.ShapeDtypeStruct((count, width), jnp.bfloat16)
    result = jax.ShapeDtypeStruct((row_count, 2 * count), dtype)
    down_near, up_near, told, part, other = vmem_call(
        projection_kernel,
        (near, near, jax.ShapeDtypeStruct((count, extra), jnp.bfloat16), result, result),
        tuple(inputs) + tuple(quarters),
        4 * row_count * width * count,
    )
    other = shifted(tensor_total(other).astype(jnp.bfloat16), OWNERS, CORE)
    part = tensor_total(part).astype(jnp.bfloat16)
    results = []
    for start, (first, second) in ((0, (Y, X)), (count, (X, Y))):
        place = placement(count // 4 // radices(device_count(OWNERS))[Z], first, second)
        columns = slice(start, start + count)
        relative = lax.concatenate([part[:, columns], other[:, columns]], 1)
        results.append(matmul(relative, place).astype(jnp.bfloat16))
    return results, (down_near, up_near), told


def grad_kernel(*refs):
    quad, inputs, (sent, kept) = refs[:4], refs[4:8], refs[8:]
    half = quad[0].shape[1] // 2
    for target, columns in ((sent, slice(half, None)), (kept, slice(0, half))):
        total = None
        for part, block in zip(quad, inputs):
            term = matmul(part[:, columns], block[...], ((0,), (0,)))
            total = term if total is None else total + term
        target[...] = total.astype(target.dtype)


def quad_columns(relative, second):
    mine, along_second, along_core, across = jnp.split(relative, 4, axis=1)
    return (
        mine,
        shifted(along_core, OWNERS, CORE),
        shifted(along_second, OWNERS, second),
        shifted(across, OWNERS, second, CORE),
    )


def quad_grads_of(quad, quad_inputs):
    shape = (quad[0].shape[1] // 2, quad_inputs[0].shape[1])
    return vmem_call(
        grad_kernel,
        (jax.ShapeDtypeStruct(shape, jnp.bfloat16), jax.ShapeDtypeStruct(shape, jnp.float32)),
        quad + tuple(quad_inputs),
        4 * quad[0].size * shape[1],
    )


def matmul(left, right, contract=((1,), (0,))):
    return lax.dot_general(left, right, (contract, ((), ())), preferred_element_type=jnp.float32)


def selected(slot_ref, group, expert, slots, values=None):
    slot = slot_ref[group, expert]
    here = lax.broadcasted_iota(jnp.int32, (slots, slot.shape[1]), 0) == slot
    return jnp.where(here, 1.0 if values is None else values, 0.0).astype(jnp.bfloat16)


def weight_copies(sources, targets, arrived, expert):
    return [
        pltpu.make_async_copy(source.at[expert], target.at[expert], arrived.at[place, expert])
        for place, (source, target) in enumerate(zip(sources, targets))
    ]


def pick_rows(pick, quarter, target, held):
    target[held, :] = matmul(pick, quarter[...]).astype(jnp.bfloat16)


def spread_rows(slot_ref, scale_ref, results, targets):
    experts, groups, slots, _ = results.shape
    for group in range(groups):
        weights = jnp.concatenate(
            [
                selected(
                    slot_ref,
                    group,
                    expert,
                    slots,
                    None if scale_ref is None else scale_ref[group, expert],
                )
                for expert in range(experts)
            ],
            0,
        )
        values = jnp.concatenate([results[expert, group] for expert in range(experts)], 0)
        targets[group][...] = matmul(weights, values, ((0,), (0,))).astype(jnp.bfloat16)


def forward_kernel(*refs):
    slot_ref, scale_ref, *refs = refs
    rows, hidden, results, gate_ref, up_ref, down_ref, arrived = refs[-7:]
    experts, groups, slots, _ = results.shape
    quarters, hbm_weights, targets = refs[:groups], refs[groups : groups + 3], refs[groups + 3 : -7]
    width = hidden.shape[1]
    chunk = 256
    for expert in range(experts):
        for copy in weight_copies(hbm_weights, (gate_ref, up_ref, down_ref), arrived, expert):
            copy.start()

    @pl.loop(0, experts)
    def _(expert):
        copies = weight_copies(hbm_weights, (gate_ref, up_ref, down_ref), arrived, expert)
        for group in range(groups):
            held = slice(group * slots, (group + 1) * slots)
            pick_rows(selected(slot_ref, group, expert, slots), quarters[group], rows, held)
        copies[0].wait()
        copies[1].wait()
        for start in range(0, width, chunk):
            columns = slice(start, start + chunk)
            gate_act = matmul(rows[...], gate_ref[expert, :, columns])
            up_act = matmul(rows[...], up_ref[expert, :, columns])
            act = gate_act * jax.nn.sigmoid(gate_act) * up_act
            hidden[:, columns] = act.astype(jnp.bfloat16)
        copies[2].wait()
        result = matmul(hidden[...], down_ref[expert]).astype(jnp.bfloat16)
        for group in range(groups):
            results[expert, group] = result[group * slots : (group + 1) * slots, :]

    spread_rows(slot_ref, scale_ref, results, targets)


def backward_kernel(*refs):
    slot_ref, scale_ref, *refs = refs
    rows, grads, gate_grads, value_grads, results, gate_ref, up_ref, down_ref, arrived = refs[-9:]
    experts, groups, slots, _ = results.shape
    quarters, quarter_grads = refs[:groups], refs[groups : 2 * groups]
    hbm_weights, targets = refs[2 * groups : 2 * groups + 3], refs[2 * groups + 3 : -9]
    width = gate_grads.shape[1]
    chunk = 256
    for expert in range(experts):
        for copy in weight_copies(hbm_weights, (gate_ref, up_ref, down_ref), arrived, expert):
            copy.start()

    @pl.loop(0, experts)
    def _(expert):
        for group in range(groups):
            held = slice(group * slots, (group + 1) * slots)
            pick_rows(selected(slot_ref, group, expert, slots), quarters[group], rows, held)
            weighed = selected(slot_ref, group, expert, slots, scale_ref[group, expert])
            pick_rows(weighed, quarter_grads[group], grads, held)
        for copy in weight_copies(hbm_weights, (gate_ref, up_ref, down_ref), arrived, expert):
            copy.wait()
        for start in range(0, width, chunk):
            columns = slice(start, start + chunk)
            gate_act = matmul(rows[...], gate_ref[expert, :, columns])
            up_act = matmul(rows[...], up_ref[expert, :, columns])
            hidden_grad = matmul(grads[...], down_ref[expert, columns, :], ((1,), (1,)))
            sigmoid = jax.nn.sigmoid(gate_act)
            scaled = hidden_grad * sigmoid
            gate_grad = scaled * up_act * (1.0 + gate_act * (1.0 - sigmoid))
            gate_grads[:, columns] = gate_grad.astype(jnp.bfloat16)
            value_grads[:, columns] = (scaled * gate_act).astype(jnp.bfloat16)
        result = matmul(gate_grads[...], gate_ref[expert], ((1,), (1,)))
        result = result + matmul(value_grads[...], up_ref[expert], ((1,), (1,)))
        result = result.astype(jnp.bfloat16)
        for group in range(groups):
            results[expert, group] = result[group * slots : (group + 1) * slots, :]

    spread_rows(slot_ref, None, results, targets)


def expert_call(kernel, plan, quarters, weights, slot_count, grads=None):
    slots, scales = plan
    experts, latent_width, width = weights[0].shape
    groups, _, _, span = slots.shape
    picked = groups * slot_count
    narrow = pltpu.VMEM((picked, latent_width), jnp.bfloat16)
    wide = pltpu.VMEM((picked, width), jnp.bfloat16)
    products = 3
    scratch = [narrow, wide]
    operands = (slots, scales) + tuple(quarters)
    if grads is not None:
        products = 5
        scratch = [narrow, narrow, wide, wide]
        operands = operands + tuple(grads)
    operands = operands + tuple(weights)
    scratch = scratch + [
        pltpu.VMEM((experts, groups, slot_count, latent_width), jnp.bfloat16),
        *[pltpu.VMEM(weight.shape, jnp.bfloat16) for weight in weights],
        pltpu.SemaphoreType.DMA((3, experts)),
    ]
    whole = pl.BlockSpec(memory_space=pltpu.VMEM)
    return pl.pallas_call(
        kernel,
        out_shape=(jax.ShapeDtypeStruct((span, latent_width), jnp.bfloat16),) * groups,
        in_specs=[whole] * (len(operands) - 3) + [pl.BlockSpec(memory_space=pl.ANY)] * 3,
        out_specs=(whole,) * groups,
        scratch_shapes=scratch,
        compiler_params=pltpu.CompilerParams(vmem_limit_bytes=32 << 20),
        cost_estimate=pl.CostEstimate(
            flops=2 * products * experts * picked * latent_width * width // 3,
            bytes_accessed=2 * sum(array.size for array in operands) // 3,
            transcendentals=0,
        ),
    )(*operands)


STAGES = ((0,), (1, 2), (3,))


def stage_sums(kernel, plans, near, far, weights, slot_count, stage, grads=None):
    plan = [
        lax.concatenate(
            [plans[side][part][index : index + 1] for side in (0, 1) for index in stage], 0
        )
        for part in (0, 1)
    ]
    return expert_call(
        kernel,
        plan,
        [side[index] for side in (near, far) for index in stage],
        weights,
        slot_count,
        None if grads is None else [side[index] for side in grads for index in stage],
    )


def by_quarter(stages):
    near, far = [], []
    for sums in stages:
        near.extend(sums[: len(sums) // 2])
        far.extend(sums[len(sums) // 2 :])
    return near, far


def expert_plans(told, local_experts, row_count):
    shards = lax.axis_size("expert")
    depth = radices(shards)[Z]
    told = told.astype(jnp.int32).reshape(shards, 2, -1, row_count)
    capacity = 3 * row_count * told.shape[2] // (2 * local_experts * shards)
    mine = lax.axis_index("expert") * local_experts + jnp.arange(local_experts, dtype=jnp.int32)
    chosen = told[:, 0][:, None] == mine[None, :, None, None]
    fixed = jnp.sum(jnp.where(chosen, told[:, 1][:, None], 0), axis=2)
    member = jnp.any(chosen, axis=2)
    earlier = jnp.arange(row_count)[:, None] < jnp.arange(row_count)[None, :]
    ranking = jnp.einsum(
        "set,tu->seu",
        member.astype(jnp.bfloat16),
        earlier.astype(jnp.bfloat16),
        preferred_element_type=jnp.float32,
    ).astype(jnp.int32)
    offset = (jnp.arange(shards, dtype=jnp.int32) % depth * capacity)[:, None, None]
    slots = jnp.where(member, ranking + offset, -1)
    scales = fixed.astype(jnp.float32) / 256.0

    def in_quarters(values):
        values = values.reshape(2, 4, depth, local_experts, row_count).transpose(0, 1, 3, 2, 4)
        return values.reshape(2, 4, local_experts, 1, depth * row_count)

    slots, scales = in_quarters(slots), in_quarters(scales)
    return [(slots[core], scales[core]) for core in (0, 1)], depth * capacity


def tied(*values):
    return lax.optimization_barrier(values)


def local(
    tokens, out_grad, routes, combine_fixed, down_proj, up_proj, expert_gate, expert_up, expert_down
):
    local_experts, latent_width, width = expert_gate.shape
    row_count = tokens.shape[0]
    rows = down_proj.shape[0]
    told = lax.concatenate([routes.T, combine_fixed.T], 0).astype(jnp.bfloat16)
    ride = lax.axis_size("dp") == 1
    sent = [down_proj, up_proj]
    if ride:
        sent.append(told.reshape(rows, -1))
    own, later_tokens, later_grads = tied(
        gather_depth(lax.concatenate(sent, 1), OWNERS), tokens, out_grad
    )
    along_y, along_x = shifted(own, OWNERS, Y), shifted(own, OWNERS, X)
    quarters = (
        own,
        along_y,
        along_x,
        shifted(along_y[:, : tokens.shape[1]], OWNERS, X),
        shifted(along_x[:, tokens.shape[1] :], OWNERS, Y),
    )
    other_tokens = shifted(later_tokens, OWNERS, CORE)
    other_grads = shifted(later_grads, OWNERS, CORE)
    down_place = placement(rows, Y, X)
    up_place = placement(rows, X, Y)
    (latent, mix_grad), (down_near, up_near), told_near = projected(
        (tokens, other_tokens, out_grad, other_grads), quarters
    )
    if not ride:
        told_near = lax.concatenate(
            list(gather_chips(gather_depth(told, EXPERT), EXPERT, Y, X)), 0
        )
    latent, later_tokens, later_grads, told_near = tied(latent, tokens, out_grad, told_near)
    latent_own = gather_depth(latent, EXPERT)
    next_tokens, next_grads = shifted(later_tokens, OWNERS, X), shifted(later_grads, OWNERS, Y)
    latent_own, mix_grad = tied(latent_own, mix_grad)
    near = (latent_own, shifted(latent_own, EXPERT, Y), shifted(latent_own, EXPERT, X))
    mix_own = gather_depth(mix_grad, EXPERT)
    told_far = shifted(told_near, EXPERT, CORE)
    plans, slot_count = expert_plans(
        lax.concatenate([told_near, told_far], 0), local_experts, row_count
    )
    mix_own, near, next_tokens, next_grads = tied(mix_own, near, next_tokens, next_grads)
    near = gather_chips_by_turns(near, EXPERT, Y, X)
    far = tuple(shifted(part, EXPERT, CORE) for part in near[:3])
    near_grad = (mix_own, shifted(mix_own, EXPERT, Y), shifted(mix_own, EXPERT, X))

    weights = (expert_gate, expert_up, expert_down)
    shared = (weights, slot_count)
    first_sums = stage_sums(forward_kernel, plans, near, far, *shared, STAGES[0])
    last_near, first_sums = tied(near[3], first_sums)
    far = far + (shifted(last_near, EXPERT, CORE),)
    middle_sums, last_sums, near_grad = tied(
        stage_sums(forward_kernel, plans, near, far, *shared, STAGES[1]),
        stage_sums(forward_kernel, plans, near, far, *shared, STAGES[2]),
        near_grad,
    )
    near_grad = gather_chips_by_turns(near_grad, EXPERT, Y, X)
    forward = [first_sums, middle_sums, last_sums]
    forward_near, forward_far = by_quarter(forward)
    far_grad = tuple(shifted(part, EXPERT, CORE) for part in near_grad)
    across, along_y, along_x, own = core_totals(forward_near, forward_far)
    forward_sums = [part.astype(jnp.bfloat16) for part in (across, along_y, along_x)] + [own]
    mix_own, *forward_alongs = tied(near_grad[0], *forward_sums[1:])
    near_grad = (mix_own,) + tuple(near_grad[1:])
    backward = [
        stage_sums(
            backward_kernel, plans, near, far, *shared, STAGES[0], (near_grad, far_grad)
        )
    ]
    along_grads, forward_across = tied(near_grad[1:], forward_sums[0])
    forward_sums = [forward_across] + forward_alongs
    near_grad = near_grad[:1] + tuple(along_grads)
    backward += [
        stage_sums(backward_kernel, plans, near, far, *shared, stage, (near_grad, far_grad))
        for stage in STAGES[1:]
    ]
    backward[0], next_tokens, next_grads, down_near, up_near = tied(
        backward[0], next_tokens, next_grads, down_near, up_near
    )
    backward_near, backward_far = by_quarter(backward)
    last_tokens, last_grads, down_far, up_far = [
        shifted(array, OWNERS, CORE) for array in (next_tokens, next_grads, down_near, up_near)
    ]
    quad_tokens = (tokens, other_tokens, next_tokens, last_tokens)
    quad_grads = (out_grad, other_grads, next_grads, last_grads)

    mixed_sums = chip_totals(*forward_sums)
    backward_across, *backward_sums = core_totals(backward_near, backward_far)
    backward_across = across_by_turns(backward_across)
    mixed_sums, backward_across, backward_sums = tied(
        mixed_sums, backward_across, backward_sums
    )
    mixed_rows = tensor_total(depth_total(mixed_sums, EXPERT)).astype(jnp.bfloat16)
    mixed_relative = matmul(mixed_rows, up_place, ((1,), (1,))).astype(jnp.bfloat16)
    latent_sums = chip_totals_by_turns(*backward_across, *backward_sums)
    mixed_relative, latent_sums = tied(mixed_relative, latent_sums)
    quad = quad_columns(mixed_relative, Y)
    latent_grad = tensor_total(depth_total(latent_sums, EXPERT)).astype(jnp.bfloat16)
    up_sent, up_kept = quad_grads_of(quad, quad_grads)
    up_sums = up_kept + shifted(up_sent, OWNERS, X).astype(jnp.float32)
    grad_relative = matmul(latent_grad, down_place, ((1,), (1,))).astype(jnp.bfloat16)
    quad = quad_columns(grad_relative, X)
    down_sent, down_kept = quad_grads_of(quad, quad_tokens)
    up_sums, mixed_relative, grad_relative, down_sent = tied(
        up_sums, mixed_relative, grad_relative, down_sent
    )
    up_grad = depth_total(up_sums, OWNERS)
    down_sums = down_kept + shifted(down_sent, OWNERS, Y).astype(jnp.float32)
    half = latent_width // 2
    layer_out = matmul(mixed_relative[:, :half], up_near)
    layer_out = (layer_out + matmul(mixed_relative[:, half:], up_far)).astype(jnp.bfloat16)
    token_grad = matmul(grad_relative[:, :half], down_near)
    token_grad = (token_grad + matmul(grad_relative[:, half:], down_far)).astype(jnp.bfloat16)
    down_grad = depth_total(down_sums, OWNERS)
    return (layer_out, token_grad, down_grad, up_grad)


def solution(mesh):
    in_specs = (
        P(("groups", "expert", "dp"), "tensor"),
        P(("groups", "expert", "dp"), "tensor"),
        P(("groups", "expert", "dp"), None),
        P(("groups", "expert", "dp"), None),
        P(("expert", "dp"), "tensor"),
        P(("expert", "dp"), "tensor"),
        P("expert", None, "tensor"),
        P("expert", None, "tensor"),
        P("expert", "tensor", None),
    )
    out_specs = (
        P(("groups", "expert", "dp"), "tensor"),
        P(("groups", "expert", "dp"), "tensor"),
        P(("groups", "expert", "dp"), "tensor"),
        P(("groups", "expert", "dp"), "tensor"),
    )
    return jax.shard_map(local, mesh=mesh, in_specs=in_specs, out_specs=out_specs, check_vma=False)
```

```python
import math

import jax
import jax.numpy as jnp
from jax import lax
from jax.experimental import pallas as pl
from jax.experimental.pallas import tpu as pltpu
from jax.sharding import PartitionSpec as P

OWNERS = ("expert", "dp")
EXPERT = ("expert",)
Z, Y, X, CORE = 0, 1, 2, 3


def tensor_total(partial_sum):
    return lax.psum(partial_sum, "tensor")


def radices(count):
    return (count // 8, 2, 2, 2)


def digit_of(axes, place):
    sizes = radices(math.prod(lax.axis_size(axis) for axis in axes))
    stride = math.prod(sizes[place + 1 :])
    return lax.rem(lax.axis_index(axes) // stride, sizes[place])


def shifted(block, axes, *places, step=1):
    count = math.prod(lax.axis_size(axis) for axis in axes)
    sizes = radices(count)
    pairs = []
    for here in range(count):
        there = here
        for place in places:
            stride = math.prod(sizes[place + 1 :])
            digit = here // stride % sizes[place]
            there += ((digit + step) % sizes[place] - digit) * stride
        pairs.append((here, there))
    return lax.ppermute(block, axes, pairs)


SIDES = ((0, 0), (1, 0), (0, 1), (1, 1))


def device_count(axes):
    return math.prod(lax.axis_size(axis) for axis in axes)


def relative_owners(axes, first, second):
    depth = radices(device_count(axes))[Z]
    owners = []
    for core_step in (0, 1):
        for first_step, second_step in SIDES:
            for z_step in range(depth):
                steps = {Z: depth - z_step, first: first_step, second: second_step, CORE: core_step}
                owner = 0
                for place, size in enumerate(radices(device_count(axes))):
                    digit = lax.rem(digit_of(axes, place) + steps[place], size)
                    owner = owner * size + digit
                owners.append(owner)
    return jnp.stack(owners)


def gather_depth(rows, axes):
    depth = radices(device_count(axes))[Z]
    return lax.concatenate(
        [rows] + [shifted(rows, axes, Z, step=step) for step in range(1, depth)], 0
    )


def gather_chips(own, axes, first, second):
    return (
        own,
        shifted(own, axes, first),
        shifted(own, axes, second),
        shifted(own, axes, first, second),
    )


def gather_chips_by_turns(alongs, axes, first, second):
    own, along_first, along_second = alongs
    half = own.shape[1] // 2
    left = shifted(along_first[:, :half], axes, second)
    right = shifted(along_second[:, half:], axes, first)
    return (own, along_first, along_second, lax.concatenate([left, right], 1))


def core_totals(near, far):
    return [
        near[index].astype(jnp.float32) + shifted(far[index], EXPERT, CORE).astype(jnp.float32)
        for index in (3, 1, 2, 0)
    ]


def depth_total(terms, axes):
    depth = radices(device_count(axes))[Z]
    pieces = jnp.split(terms, depth, axis=0)
    total = pieces[0]
    for step in range(1, depth):
        piece = shifted(pieces[step].astype(jnp.bfloat16), axes, Z, step=depth - step)
        total = total + piece.astype(jnp.float32)
    return total


def chip_totals(across, along_y, along_x, own):
    across = shifted(across.astype(jnp.bfloat16), EXPERT, X, Y)
    along_y = shifted(along_y.astype(jnp.bfloat16), EXPERT, Y)
    along_x = shifted(along_x.astype(jnp.bfloat16), EXPERT, X)
    total = own + across.astype(jnp.float32)
    return total + along_y.astype(jnp.float32) + along_x.astype(jnp.float32)


def across_by_turns(across):
    across = across.astype(jnp.bfloat16)
    half = across.shape[1] // 2
    return shifted(across[:, :half], EXPERT, X), shifted(across[:, half:], EXPERT, Y)


def chip_totals_by_turns(left, right, along_y, along_x, own):
    half = left.shape[1]
    left, right = left.astype(jnp.float32), right.astype(jnp.float32)
    along_y = lax.concatenate([along_y[:, :half] + left, along_y[:, half:]], 1)
    along_x = lax.concatenate([along_x[:, :half], along_x[:, half:] + right], 1)
    own = own + shifted(along_y.astype(jnp.bfloat16), EXPERT, Y).astype(jnp.float32)
    return own + shifted(along_x.astype(jnp.bfloat16), EXPERT, X).astype(jnp.float32)


def placement(rows, first, second):
    owners = relative_owners(OWNERS, first, second)
    targets = (owners[:, None] * rows + jnp.arange(rows, dtype=jnp.int32)[None, :]).reshape(-1)
    columns = jnp.arange(targets.shape[0], dtype=jnp.int32)
    return (targets[:, None] == columns[None, :]).astype(jnp.bfloat16)


def vmem_call(kernel, out_shape, operands, products):
    whole = pl.BlockSpec(memory_space=pltpu.VMEM)
    return pl.pallas_call(
        kernel,
        out_shape=out_shape,
        in_specs=[whole] * len(operands),
        out_specs=(whole,) * len(out_shape),
        compiler_params=pltpu.CompilerParams(vmem_limit_bytes=20 << 20),
        cost_estimate=pl.CostEstimate(
            flops=2 * products,
            bytes_accessed=2 * sum(array.size for array in operands),
            transcendentals=0,
        ),
    )(*operands)


def projection_kernel(*refs):
    tokens, other_tokens, grads, other_grads, *quarters, left, right = refs[:9]
    nears, (told, part, other) = refs[9:11], refs[11:]
    width = nears[0].shape[1]
    count = left.shape[0]
    for near, start, order in zip(nears, (0, width), ((0, 1, 2), (0, 2, 1))):
        for index, quarter in enumerate(order):
            held = slice(index * count, (index + 1) * count)
            near[held, :] = quarters[quarter][:, start : start + width]
    nears[0][3 * count :, :] = left[...]
    nears[1][3 * count :, :] = right[:, :width]
    if right.shape[1] > width:
        for index, quarter in enumerate(quarters):
            told[index * count : (index + 1) * count, :] = quarter[:, 2 * width :]
        told[3 * count :, :] = right[:, width:]
    else:
        told[...] = jnp.zeros_like(told)
    half = nears[0].shape[0]
    for target, down, up in ((part, tokens, grads), (other, other_tokens, other_grads)):
        for source, near, start in ((down, nears[0], 0), (up, nears[1], half)):
            product = matmul(source[...], near[...], ((1,), (1,)))
            target[:, start : start + half] = product.astype(target.dtype)


def projected(inputs, quarters):
    row_count, width = inputs[0].shape
    count = 4 * quarters[0].shape[0]
    extra = max(quarters[0].shape[1] - 2 * width, 128)
    dtype = jnp.bfloat16 if lax.axis_size("tensor") == 1 else jnp.float32
    near = jax.ShapeDtypeStruct((count, width), jnp.bfloat16)
    result = jax.ShapeDtypeStruct((row_count, 2 * count), dtype)
    down_near, up_near, told, part, other = vmem_call(
        projection_kernel,
        (near, near, jax.ShapeDtypeStruct((count, extra), jnp.bfloat16), result, result),
        tuple(inputs) + tuple(quarters),
        4 * row_count * width * count,
    )
    other = shifted(tensor_total(other).astype(jnp.bfloat16), OWNERS, CORE)
    part = tensor_total(part).astype(jnp.bfloat16)
    results = []
    for start, (first, second) in ((0, (Y, X)), (count, (X, Y))):
        place = placement(count // 4 // radices(device_count(OWNERS))[Z], first, second)
        columns = slice(start, start + count)
        relative = lax.concatenate([part[:, columns], other[:, columns]], 1)
        results.append(matmul(relative, place).astype(jnp.bfloat16))
    return results, (down_near, up_near), told


def grad_kernel(*refs):
    quad, inputs, (sent, kept) = refs[:4], refs[4:8], refs[8:]
    half = quad[0].shape[1] // 2
    for target, columns in ((sent, slice(half, None)), (kept, slice(0, half))):
        total = None
        for part, block in zip(quad, inputs):
            term = matmul(part[:, columns], block[...], ((0,), (0,)))
            total = term if total is None else total + term
        target[...] = total.astype(target.dtype)


def quad_columns(relative, second):
    mine, along_second, along_core, across = jnp.split(relative, 4, axis=1)
    return (
        mine,
        shifted(along_core, OWNERS, CORE),
        shifted(along_second, OWNERS, second),
        shifted(across, OWNERS, second, CORE),
    )


def quad_grads_of(quad, quad_inputs):
    shape = (quad[0].shape[1] // 2, quad_inputs[0].shape[1])
    return vmem_call(
        grad_kernel,
        (jax.ShapeDtypeStruct(shape, jnp.bfloat16), jax.ShapeDtypeStruct(shape, jnp.float32)),
        quad + tuple(quad_inputs),
        4 * quad[0].size * shape[1],
    )


def matmul(left, right, contract=((1,), (0,))):
    return lax.dot_general(left, right, (contract, ((), ())), preferred_element_type=jnp.float32)


def selected(slot_ref, group, expert, slots, values=None):
    slot = slot_ref[group, expert]
    here = lax.broadcasted_iota(jnp.int32, (slots, slot.shape[1]), 0) == slot
    return jnp.where(here, 1.0 if values is None else values, 0.0).astype(jnp.bfloat16)


def weight_copies(sources, targets, arrived, expert):
    return [
        pltpu.make_async_copy(source.at[expert], target.at[expert], arrived.at[place, expert])
        for place, (source, target) in enumerate(zip(sources, targets))
    ]


def pick_rows(pick, quarter, target, held):
    target[held, :] = matmul(pick, quarter[...]).astype(jnp.bfloat16)


def spread_rows(slot_ref, scale_ref, results, targets):
    experts, groups, slots, _ = results.shape
    for group in range(groups):
        weights = jnp.concatenate(
            [
                selected(
                    slot_ref,
                    group,
                    expert,
                    slots,
                    None if scale_ref is None else scale_ref[group, expert],
                )
                for expert in range(experts)
            ],
            0,
        )
        values = jnp.concatenate([results[expert, group] for expert in range(experts)], 0)
        targets[group][...] = matmul(weights, values, ((0,), (0,))).astype(jnp.bfloat16)


def forward_kernel(*refs):
    slot_ref, scale_ref, *refs = refs
    rows, hidden, results, gate_ref, up_ref, down_ref, arrived = refs[-7:]
    experts, groups, slots, _ = results.shape
    quarters, hbm_weights, targets = refs[:groups], refs[groups : groups + 3], refs[groups + 3 : -7]
    width = hidden.shape[1]
    chunk = 256
    for expert in range(experts):
        for copy in weight_copies(hbm_weights, (gate_ref, up_ref, down_ref), arrived, expert):
            copy.start()

    @pl.loop(0, experts)
    def _(expert):
        copies = weight_copies(hbm_weights, (gate_ref, up_ref, down_ref), arrived, expert)
        for group in range(groups):
            held = slice(group * slots, (group + 1) * slots)
            pick_rows(selected(slot_ref, group, expert, slots), quarters[group], rows, held)
        copies[0].wait()
        copies[1].wait()
        for start in range(0, width, chunk):
            columns = slice(start, start + chunk)
            gate_act = matmul(rows[...], gate_ref[expert, :, columns])
            up_act = matmul(rows[...], up_ref[expert, :, columns])
            act = gate_act * jax.nn.sigmoid(gate_act) * up_act
            hidden[:, columns] = act.astype(jnp.bfloat16)
        copies[2].wait()
        result = matmul(hidden[...], down_ref[expert]).astype(jnp.bfloat16)
        for group in range(groups):
            results[expert, group] = result[group * slots : (group + 1) * slots, :]

    spread_rows(slot_ref, scale_ref, results, targets)


def backward_kernel(*refs):
    slot_ref, scale_ref, *refs = refs
    rows, grads, gate_grads, value_grads, results, gate_ref, up_ref, down_ref, arrived = refs[-9:]
    experts, groups, slots, _ = results.shape
    quarters, quarter_grads = refs[:groups], refs[groups : 2 * groups]
    hbm_weights, targets = refs[2 * groups : 2 * groups + 3], refs[2 * groups + 3 : -9]
    width = gate_grads.shape[1]
    chunk = 256
    for expert in range(experts):
        for copy in weight_copies(hbm_weights, (gate_ref, up_ref, down_ref), arrived, expert):
            copy.start()

    @pl.loop(0, experts)
    def _(expert):
        for group in range(groups):
            held = slice(group * slots, (group + 1) * slots)
            pick_rows(selected(slot_ref, group, expert, slots), quarters[group], rows, held)
            weighed = selected(slot_ref, group, expert, slots, scale_ref[group, expert])
            pick_rows(weighed, quarter_grads[group], grads, held)
        for copy in weight_copies(hbm_weights, (gate_ref, up_ref, down_ref), arrived, expert):
            copy.wait()
        for start in range(0, width, chunk):
            columns = slice(start, start + chunk)
            gate_act = matmul(rows[...], gate_ref[expert, :, columns])
            up_act = matmul(rows[...], up_ref[expert, :, columns])
            hidden_grad = matmul(grads[...], down_ref[expert, columns, :], ((1,), (1,)))
            sigmoid = jax.nn.sigmoid(gate_act)
            scaled = hidden_grad * sigmoid
            gate_grad = scaled * up_act * (1.0 + gate_act * (1.0 - sigmoid))
            gate_grads[:, columns] = gate_grad.astype(jnp.bfloat16)
            value_grads[:, columns] = (scaled * gate_act).astype(jnp.bfloat16)
        result = matmul(gate_grads[...], gate_ref[expert], ((1,), (1,)))
        result = result + matmul(value_grads[...], up_ref[expert], ((1,), (1,)))
        result = result.astype(jnp.bfloat16)
        for group in range(groups):
            results[expert, group] = result[group * slots : (group + 1) * slots, :]

    spread_rows(slot_ref, None, results, targets)


def expert_call(kernel, plan, quarters, weights, slot_count, grads=None):
    slots, scales = plan
    experts, latent_width, width = weights[0].shape
    groups, _, _, span = slots.shape
    picked = groups * slot_count
    narrow = pltpu.VMEM((picked, latent_width), jnp.bfloat16)
    wide = pltpu.VMEM((picked, width), jnp.bfloat16)
    products = 3
    scratch = [narrow, wide]
    operands = (slots, scales) + tuple(quarters)
    if grads is not None:
        products = 5
        scratch = [narrow, narrow, wide, wide]
        operands = operands + tuple(grads)
    operands = operands + tuple(weights)
    scratch = scratch + [
        pltpu.VMEM((experts, groups, slot_count, latent_width), jnp.bfloat16),
        *[pltpu.VMEM(weight.shape, jnp.bfloat16) for weight in weights],
        pltpu.SemaphoreType.DMA((3, experts)),
    ]
    whole = pl.BlockSpec(memory_space=pltpu.VMEM)
    return pl.pallas_call(
        kernel,
        out_shape=(jax.ShapeDtypeStruct((span, latent_width), jnp.bfloat16),) * groups,
        in_specs=[whole] * (len(operands) - 3) + [pl.BlockSpec(memory_space=pl.ANY)] * 3,
        out_specs=(whole,) * groups,
        scratch_shapes=scratch,
        compiler_params=pltpu.CompilerParams(vmem_limit_bytes=32 << 20),
        cost_estimate=pl.CostEstimate(
            flops=2 * products * experts * picked * latent_width * width // 3,
            bytes_accessed=2 * sum(array.size for array in operands) // 3,
            transcendentals=0,
        ),
    )(*operands)


STAGES = ((0,), (1, 2), (3,))


def stage_sums(kernel, plans, near, far, weights, slot_count, stage, grads=None):
    plan = [
        lax.concatenate(
            [plans[side][part][index : index + 1] for side in (0, 1) for index in stage], 0
        )
        for part in (0, 1)
    ]
    return expert_call(
        kernel,
        plan,
        [side[index] for side in (near, far) for index in stage],
        weights,
        slot_count,
        None if grads is None else [side[index] for side in grads for index in stage],
    )


def by_quarter(stages):
    near, far = [], []
    for sums in stages:
        near.extend(sums[: len(sums) // 2])
        far.extend(sums[len(sums) // 2 :])
    return near, far


def expert_plans(told, local_experts, row_count):
    shards = lax.axis_size("expert")
    depth = radices(shards)[Z]
    told = told.astype(jnp.int32).reshape(shards, 2, -1, row_count)
    capacity = 3 * row_count * told.shape[2] // (2 * local_experts * shards)
    mine = lax.axis_index("expert") * local_experts + jnp.arange(local_experts, dtype=jnp.int32)
    chosen = told[:, 0][:, None] == mine[None, :, None, None]
    fixed = jnp.sum(jnp.where(chosen, told[:, 1][:, None], 0), axis=2)
    member = jnp.any(chosen, axis=2)
    earlier = jnp.arange(row_count)[:, None] < jnp.arange(row_count)[None, :]
    ranking = jnp.einsum(
        "set,tu->seu",
        member.astype(jnp.bfloat16),
        earlier.astype(jnp.bfloat16),
        preferred_element_type=jnp.float32,
    ).astype(jnp.int32)
    offset = (jnp.arange(shards, dtype=jnp.int32) % depth * capacity)[:, None, None]
    slots = jnp.where(member, ranking + offset, -1)
    scales = fixed.astype(jnp.float32) / 256.0

    def in_quarters(values):
        values = values.reshape(2, 4, depth, local_experts, row_count).transpose(0, 1, 3, 2, 4)
        return values.reshape(2, 4, local_experts, 1, depth * row_count)

    slots, scales = in_quarters(slots), in_quarters(scales)
    return [(slots[core], scales[core]) for core in (0, 1)], depth * capacity


def tied(*values):
    return lax.optimization_barrier(values)


def local(
    tokens, out_grad, routes, combine_fixed, down_proj, up_proj, expert_gate, expert_up, expert_down
):
    local_experts, latent_width, width = expert_gate.shape
    row_count = tokens.shape[0]
    rows = down_proj.shape[0]
    told = lax.concatenate([routes.T, combine_fixed.T], 0).astype(jnp.bfloat16)
    ride = lax.axis_size("dp") == 1
    sent = [down_proj, up_proj]
    if ride:
        sent.append(told.reshape(rows, -1))
    own, later_tokens, later_grads = tied(
        gather_depth(lax.concatenate(sent, 1), OWNERS), tokens, out_grad
    )
    along_y, along_x = shifted(own, OWNERS, Y), shifted(own, OWNERS, X)
    quarters = (
        own,
        along_y,
        along_x,
        shifted(along_y[:, : tokens.shape[1]], OWNERS, X),
        shifted(along_x[:, tokens.shape[1] :], OWNERS, Y),
    )
    other_tokens = shifted(later_tokens, OWNERS, CORE)
    other_grads = shifted(later_grads, OWNERS, CORE)
    down_place = placement(rows, Y, X)
    up_place = placement(rows, X, Y)
    (latent, mix_grad), (down_near, up_near), told_near = projected(
        (tokens, other_tokens, out_grad, other_grads), quarters
    )
    if not ride:
        told_near = lax.concatenate(
            list(gather_chips(gather_depth(told, EXPERT), EXPERT, Y, X)), 0
        )
    latent, later_tokens, later_grads, told_near = tied(latent, tokens, out_grad, told_near)
    latent_own = gather_depth(latent, EXPERT)
    next_tokens, next_grads = shifted(later_tokens, OWNERS, X), shifted(later_grads, OWNERS, Y)
    latent_own, mix_grad = tied(latent_own, mix_grad)
    near = (latent_own, shifted(latent_own, EXPERT, Y), shifted(latent_own, EXPERT, X))
    mix_own = gather_depth(mix_grad, EXPERT)
    told_far = shifted(told_near, EXPERT, CORE)
    plans, slot_count = expert_plans(
        lax.concatenate([told_near, told_far], 0), local_experts, row_count
    )
    mix_own, near, next_tokens, next_grads = tied(mix_own, near, next_tokens, next_grads)
    near = gather_chips_by_turns(near, EXPERT, Y, X)
    far = tuple(shifted(part, EXPERT, CORE) for part in near[:3])
    near_grad = (mix_own, shifted(mix_own, EXPERT, Y), shifted(mix_own, EXPERT, X))

    weights = (expert_gate, expert_up, expert_down)
    shared = (weights, slot_count)
    first_sums = stage_sums(forward_kernel, plans, near, far, *shared, STAGES[0])
    last_near, first_sums = tied(near[3], first_sums)
    far = far + (shifted(last_near, EXPERT, CORE),)
    middle_sums, last_sums, near_grad = tied(
        stage_sums(forward_kernel, plans, near, far, *shared, STAGES[1]),
        stage_sums(forward_kernel, plans, near, far, *shared, STAGES[2]),
        near_grad,
    )
    near_grad = gather_chips_by_turns(near_grad, EXPERT, Y, X)
    forward = [first_sums, middle_sums, last_sums]
    forward_near, forward_far = by_quarter(forward)
    far_grad = tuple(shifted(part, EXPERT, CORE) for part in near_grad)
    across, along_y, along_x, own = core_totals(forward_near, forward_far)
    forward_sums = [part.astype(jnp.bfloat16) for part in (across, along_y, along_x)] + [own]
    mix_own, *forward_alongs = tied(near_grad[0], *forward_sums[1:])
    near_grad = (mix_own,) + tuple(near_grad[1:])
    backward = [
        stage_sums(
            backward_kernel, plans, near, far, *shared, STAGES[0], (near_grad, far_grad)
        )
    ]
    along_grads, forward_across = tied(near_grad[1:], forward_sums[0])
    forward_sums = [forward_across] + forward_alongs
    near_grad = near_grad[:1] + tuple(along_grads)
    across_sums, along_grads = tied(
        stage_sums(backward_kernel, plans, near, far, *shared, STAGES[2], (near_grad, far_grad)),
        near_grad[1:3],
    )
    near_grad = near_grad[:1] + tuple(along_grads) + near_grad[3:]
    backward.append(
        stage_sums(backward_kernel, plans, near, far, *shared, STAGES[1], (near_grad, far_grad))
    )
    backward.append(across_sums)
    backward[0], next_tokens, next_grads, down_near, up_near = tied(
        backward[0], next_tokens, next_grads, down_near, up_near
    )
    backward_near, backward_far = by_quarter(backward)
    last_tokens, last_grads, down_far, up_far = [
        shifted(array, OWNERS, CORE) for array in (next_tokens, next_grads, down_near, up_near)
    ]
    quad_tokens = (tokens, other_tokens, next_tokens, last_tokens)
    quad_grads = (out_grad, other_grads, next_grads, last_grads)

    mixed_sums = chip_totals(*forward_sums)
    backward_across, *backward_sums = core_totals(backward_near, backward_far)
    backward_across = across_by_turns(backward_across)
    mixed_sums, backward_across, backward_sums = tied(
        mixed_sums, backward_across, backward_sums
    )
    mixed_rows = tensor_total(depth_total(mixed_sums, EXPERT)).astype(jnp.bfloat16)
    mixed_relative = matmul(mixed_rows, up_place, ((1,), (1,))).astype(jnp.bfloat16)
    latent_sums = chip_totals_by_turns(*backward_across, *backward_sums)
    mixed_relative, latent_sums = tied(mixed_relative, latent_sums)
    quad = quad_columns(mixed_relative, Y)
    latent_grad = tensor_total(depth_total(latent_sums, EXPERT)).astype(jnp.bfloat16)
    up_sent, up_kept = quad_grads_of(quad, quad_grads)
    up_sums = up_kept + shifted(up_sent, OWNERS, X).astype(jnp.float32)
    grad_relative = matmul(latent_grad, down_place, ((1,), (1,))).astype(jnp.bfloat16)
    quad = quad_columns(grad_relative, X)
    down_sent, down_kept = quad_grads_of(quad, quad_tokens)
    up_sums, mixed_relative, grad_relative, down_sent = tied(
        up_sums, mixed_relative, grad_relative, down_sent
    )
    up_grad = depth_total(up_sums, OWNERS)
    down_sums = down_kept + shifted(down_sent, OWNERS, Y).astype(jnp.float32)
    half = latent_width // 2
    layer_out = matmul(mixed_relative[:, :half], up_near)
    layer_out = (layer_out + matmul(mixed_relative[:, half:], up_far)).astype(jnp.bfloat16)
    token_grad = matmul(grad_relative[:, :half], down_near)
    token_grad = (token_grad + matmul(grad_relative[:, half:], down_far)).astype(jnp.bfloat16)
    down_grad = depth_total(down_sums, OWNERS)
    return (layer_out, token_grad, down_grad, up_grad)


def solution(mesh):
    in_specs = (
        P(("groups", "expert", "dp"), "tensor"),
        P(("groups", "expert", "dp"), "tensor"),
        P(("groups", "expert", "dp"), None),
        P(("groups", "expert", "dp"), None),
        P(("expert", "dp"), "tensor"),
        P(("expert", "dp"), "tensor"),
        P("expert", None, "tensor"),
        P("expert", None, "tensor"),
        P("expert", "tensor", None),
    )
    out_specs = (
        P(("groups", "expert", "dp"), "tensor"),
        P(("groups", "expert", "dp"), "tensor"),
        P(("groups", "expert", "dp"), "tensor"),
        P(("groups", "expert", "dp"), "tensor"),
    )
    return jax.shard_map(local, mesh=mesh, in_specs=in_specs, out_specs=out_specs, check_vma=False)
```
